512 devices in a mesh: tile: 64 (over x_lo, z, core), mode: 8 (over x_hi, y).
Axes of the slice: x: 4 (x_hi: 2, x_lo: 2; x = x_hi * 2 + x_lo), y: 4, z: 16, core: 2. Of those that a mesh axis runs over, the one named last changes fastest.
Arguments:
- object_tiles: float32 [2, 288, 32768], P(None, None, 'tile'), may hold values from -6 to 6
- probe_modes: float32 [8, 2, 256, 256], P('mode'), may hold values from -6 to 6
- measured: bfloat16 [64, 3, 256, 256], P('tile'), may hold values from 0 to 8
- row_offset: int32 [64, 3], P('tile'), may hold values from 0 to 32
- col_offset: int32 [64, 3], P('tile'), may hold values from 0 to 511
- live_counts: int32 [64], P('tile'), may hold values from 1 to 3, 128 in all
- visit_order: int32 [64, 3], P('tile'), may hold values from 0 to 2, each once within a row
Outputs:
- object_out: float32 [2, 288, 32768], P(None, None, 'tile')
- probe_out: float32 [8, 2, 256, 256], P('mode')
The draws below stay inside these ranges and needn't reach their ends.
Inputs may be any that keep to these rules, and one draw needn't show every extreme that they name: `live_counts`: they sum to 128, and some tile owns 3 positions. `visit_order`: each tile's row is a permutation of its 3 slots. `col_offset`: a patch may reach up to 255 columns into the next tile.
All inputs are finite; a program needn't handle non-finite values. No bound on the sum of `live_counts` on one device may be relied on, other than what follows from the above.
Results may differ from the reference program's by a relative error of at most 0.0003.
Values sent between devices are 32-bit elements; how exact they have to be, the bound alone decides.
No kernel may reach another device: no remote copies, remote signals or barrier semaphores. Data moves between devices by JAX's collectives and lax.ppermute only.
A program may use at most 64 MiB of HBM per device.

```python
import math
import jax
import jax.numpy as jnp
import numpy as np
from jax import lax

PATCH = 256
TILE_H = 288
TILE_W = 512
SLOTS = 3
TILES = 64
MODES = 8


def set_ends(drawn, own_key, least, largest):
    longest = drawn.shape.index(max(drawn.shape))
    spots = []
    for shift in (0, 1):
        where = [jax.random.randint(jax.random.fold_in(own_key, axis), (), 0, length) for axis, length in enumerate(drawn.shape)]
        where[longest] = (where[longest] + shift) % drawn.shape[longest]
        spots.append(tuple(where))
    return drawn.at[spots[0]].set(least).at[spots[1]].set(largest)


def block_levels(key, dims, pieces, smallest, high):
    def one(position, blocks):
        steps = jax.random.uniform(jax.random.fold_in(jax.random.fold_in(key, 6), position), (blocks,), jnp.float32, smallest / len(pieces), high / len(pieces))
        return jnp.repeat(jnp.exp(steps), dims[position] // blocks).reshape((-1,) + (1,) * (len(dims) - position - 1))

    gain = one(*pieces[0])
    for cut in pieces[1:]:
        gain = gain * one(*cut)
    return gain


def length_profile(number_of, total, bound, lean):
    portions = [(1 << 20) // math.isqrt(rank ** lean) + 1 for rank in range(2, number_of + 1)]
    rest, holding = total - bound - (number_of - 1), [1] * (number_of - 1)
    while rest > 0:
        candidates = [i for i in range(number_of - 1) if holding[i] < bound]
        pool, left = sum([portions[i] for i in candidates]), rest
        for i in candidates:
            more = min(bound - holding[i], max(1, left * portions[i] // pool), rest)
            holding[i] = holding[i] + more
            rest = rest - more
    return np.array([bound] + holding)


def ragged_sizes(key, amount, total, limit, slope):
    if amount == 2:
        one = jax.random.randint(key, (), max(1, total - limit), min(limit, total - 1) + 1)
        return jnp.stack([one, total - one])
    sizes = jnp.asarray(length_profile(amount, total, limit, slope), jnp.int32)
    couples = (amount - 1) // 2
    donor, receiver = sizes[1:1 + 2 * couples:2], sizes[2:2 + 2 * couples:2]
    margin = jnp.minimum(donor - 1, limit - receiver)
    passed = jax.random.randint(jax.random.fold_in(key, 1), (couples,), 0, 1 << 20) % (margin + 1)
    sizes = sizes.at[1:1 + 2 * couples:2].set(donor - passed).at[2:2 + 2 * couples:2].set(receiver + passed)
    return sizes[jax.random.permutation(jax.random.fold_in(key, 2), amount)]


def centred(key, extent, deviation, reach, split=(), kind=jnp.bfloat16):
    entries = deviation * jax.random.normal(key, extent, jnp.float32)
    if split:
        entries = entries * block_levels(key, extent, split, -0.22, 0.18)
    return jnp.clip(entries, -reach, reach).astype(kind)


def setup_inputs(seed: int = 0) -> dict:
    arg_keys = jax.random.split(jax.random.key(seed), 8)
    return {
        "object_tiles": centred(arg_keys[0], (2, TILE_H, TILES * TILE_W), 0.7, 6.0, ((2, 64),), jnp.float32),
        "probe_modes": centred(arg_keys[1], (MODES, 2, PATCH, PATCH), 0.5, 6.0, ((0, 8),), jnp.float32),
        "measured": jnp.clip(8.0 * jax.random.uniform(arg_keys[2], (TILES, SLOTS, PATCH, PATCH), jnp.float32) ** block_levels(arg_keys[2], (TILES, SLOTS, PATCH, PATCH), ((0, 64),), -0.2, 0.2), 0.0, 8.0).astype(jnp.bfloat16),
        "row_offset": set_ends(jax.random.randint(arg_keys[3], (TILES, SLOTS), 0, TILE_H - PATCH + 1), jax.random.fold_in(arg_keys[3], 1), 0, TILE_H - PATCH).astype(jnp.int32),
        "col_offset": set_ends(jax.random.randint(arg_keys[4], (TILES, SLOTS), 0, TILE_W), jax.random.fold_in(arg_keys[4], 1), 0, TILE_W - 1).astype(jnp.int32),
        "live_counts": ragged_sizes(arg_keys[5], TILES, 2 * TILES, SLOTS, 2).astype(jnp.int32),
        "visit_order": jax.vmap(lambda own: jax.random.permutation(own, SLOTS))(jax.random.split(arg_keys[6], TILES)).reshape((TILES, SLOTS)).astype(jnp.int32),
    }


SOFT_FLOOR = 0.5
OBJECT_RATE = 1.0
OBJECT_DAMP = 0.5
PROBE_RATE = 1.0
PROBE_DAMP = 1.0

def mode_terms(probe_now, view, measured_now, live_flag):
    exit_real = probe_now[:, 0] * view[0] - probe_now[:, 1] * view[1]
    exit_imag = probe_now[:, 0] * view[1] + probe_now[:, 1] * view[0]
    far_field = jnp.fft.fft2(lax.complex(exit_real, exit_imag), norm='ortho')
    far_real = jnp.real(far_field)
    far_imag = jnp.imag(far_field)
    total_power = lax.optimization_barrier(jnp.sum(far_real * far_real + far_imag * far_imag, axis=0))
    ratio_map = jnp.sqrt((measured_now + SOFT_FLOOR) / (total_power + SOFT_FLOOR)) - 1.0
    back_field = jnp.fft.ifft2(lax.complex(far_real * ratio_map, far_imag * ratio_map), norm='ortho')
    chi_real = jnp.real(back_field) * live_flag
    chi_imag = jnp.imag(back_field) * live_flag
    grad_real = lax.optimization_barrier(jnp.sum(probe_now[:, 0] * chi_real + probe_now[:, 1] * chi_imag, axis=0))
    grad_imag = lax.optimization_barrier(jnp.sum(probe_now[:, 0] * chi_imag - probe_now[:, 1] * chi_real, axis=0))
    illumination = lax.optimization_barrier(jnp.sum(probe_now[:, 0] * probe_now[:, 0] + probe_now[:, 1] * probe_now[:, 1], axis=0))
    update = OBJECT_RATE * jnp.stack([grad_real, grad_imag]) / (illumination + OBJECT_DAMP)
    numer_real = view[0] * chi_real + view[1] * chi_imag
    numer_imag = view[0] * chi_imag - view[1] * chi_real
    numer_term = jnp.stack([numer_real, numer_imag], axis=1)
    denom_term = (view[0] * view[0] + view[1] * view[1]) * live_flag
    return (update, numer_term, denom_term)

def reference(object_tiles, probe_modes, measured, row_offset, col_offset, live_counts, visit_order):
    total_width = TILES * TILE_W
    padded = jnp.pad(object_tiles, ((0, 0), (0, 0), (0, PATCH)))
    probe_now = probe_modes
    zero_index = jnp.zeros((), jnp.int32)
    for step_index in range(SLOTS):

        def visit(carry, tile_index, padded=padded, probe_now=probe_now, step_index=step_index):
            canvas, numer, denom = carry
            slot_index = visit_order[tile_index, step_index]
            live_flag = (slot_index < live_counts[tile_index]).astype(jnp.float32)
            row_start = row_offset[tile_index, slot_index].astype(jnp.int32)
            col_start = (col_offset[tile_index, slot_index] + tile_index * TILE_W).astype(jnp.int32)
            view = lax.dynamic_slice(padded, (zero_index, row_start, col_start), (2, PATCH, PATCH))
            measured_now = measured[tile_index, slot_index].astype(jnp.float32)
            update, numer_term, denom_term = mode_terms(probe_now, view, measured_now, live_flag)
            before = lax.dynamic_slice(canvas, (zero_index, row_start, col_start), (2, PATCH, PATCH))
            canvas = lax.dynamic_update_slice(canvas, before + update, (zero_index, row_start, col_start))
            return ((canvas, numer + numer_term, denom + denom_term), None)
        start = (jnp.zeros(padded.shape, jnp.float32), jnp.zeros(probe_now.shape, jnp.float32), jnp.zeros((PATCH, PATCH), jnp.float32))
        (canvas, numer, denom), _ = lax.scan(visit, start, jnp.arange(TILES, dtype=jnp.int32))
        padded = jnp.concatenate([padded[:, :, :total_width] + canvas[:, :, :total_width], jnp.zeros((2, TILE_H, PATCH), jnp.float32)], axis=2)
        probe_now = probe_now + PROBE_RATE * numer / (denom + PROBE_DAMP)
    return (padded[:, :, :total_width], probe_now)
```

```python
import math

import jax
import jax.numpy as jnp
import numpy as np
from jax import lax
from jax.experimental import pallas as pl
from jax.experimental.pallas import tpu as pltpu
from jax.sharding import Mesh
from jax.sharding import PartitionSpec as P

SOFT_FLOOR = 0.5
OBJECT_RATE = 1.0
OBJECT_DAMP = 0.5
PROBE_RATE = 1.0
PROBE_DAMP = 1.0

SIDE = 256
HEIGHT = 288
WIDTH = 512
WIDE = WIDTH + SIDE
MODES = 8
SLAB = SIDE // MODES
STEPS = 3
TILES = 64
RINGS = 16
ROW_SPAN = SIDE + 8
COL_SPAN = SIDE + 128

TILE_AXES = ("xlo", "z", "core")
MODE_AXES = ("xhi", "y")

ROW, COL, SLOT, LIVE, MODE, CORE, XLO, RING, HAS_NEXT = range(9)

F32 = jnp.float32
BF16 = jnp.bfloat16


def fourier_tables():
    index = np.arange(SIDE)
    angles = (index[:, None] * index[None, :] % SIDE) * (2.0 * math.pi / SIDE)
    both = np.stack([np.cos(angles), np.sin(angles)]) / math.sqrt(SIDE)
    high = both.astype(jnp.bfloat16)
    low = (both - high.astype(np.float64)).astype(jnp.bfloat16)
    return np.stack([high, low], axis=1)


def halves(value):
    high = value.astype(BF16)
    return high, (value - high.astype(F32)).astype(BF16)


def dot(left, right):
    return jnp.dot(left, right, preferred_element_type=F32)


def transform(real, imag, tables, direction):
    high, low = halves(jnp.concatenate([real, imag], axis=0))

    def rows_by(which):
        return (
            dot(high, tables[which, 0]) + dot(low, tables[which, 0]) + dot(high, tables[which, 1])
        )

    by_cos, by_sin = rows_by(0), rows_by(1)
    half_real = by_cos[:SIDE] + direction * by_sin[SIDE:]
    half_imag = by_cos[SIDE:] - direction * by_sin[:SIDE]
    high, low = halves(jnp.concatenate([half_real, half_imag], axis=1))

    def columns_by(which):
        return (
            dot(tables[which, 0], high) + dot(tables[which, 0], low) + dot(tables[which, 1], high)
        )

    by_cos, by_sin = columns_by(0), columns_by(1)
    return (
        by_cos[:, :SIDE] + direction * by_sin[:, SIDE:],
        by_cos[:, SIDE:] - direction * by_sin[:, :SIDE],
    )


def window(scal):
    row, col = scal[ROW], scal[COL]
    row_block = jnp.minimum(row // 8, 3)
    col_block = jnp.minimum(col // 128, 3)
    rows = pl.ds(pl.multiple_of(row_block * 8, 8), ROW_SPAN)
    cols = pl.ds(pl.multiple_of(col_block * 128, 128), COL_SPAN)
    return rows, cols, row - row_block * 8, col - col_block * 128


def forward(scal, extended, view, probe, tables, far, power):
    rows, cols, row_rest, col_rest = window(scal)
    for part in range(2):
        block = extended[part, rows, cols]
        block = pltpu.roll(block, lax.rem(COL_SPAN - col_rest, COL_SPAN), 1)[:, :SIDE]
        block = pltpu.roll(block, lax.rem(ROW_SPAN - row_rest, ROW_SPAN), 0)[:SIDE]
        view[part] = block
    view_real, view_imag = view[0], view[1]
    probe_real, probe_imag = probe[0], probe[1]
    far_real, far_imag = transform(
        probe_real * view_real - probe_imag * view_imag,
        probe_real * view_imag + probe_imag * view_real,
        tables,
        1.0,
    )
    far[0] = far_real
    far[1] = far_imag
    power[...] = far_real * far_real + far_imag * far_imag


def first_kernel(scal, own, beside, probe_in, tables, extended, view, probe, shard, far, power):
    extended[:, :, :WIDTH] = own[...]
    extended[:, :, WIDTH:] = beside[...]
    probe[...] = probe_in[0]
    row = pl.multiple_of(scal[CORE] * 128 + scal[XLO] * 64 + scal[RING] // 2 * 8, 8)

    @pl.when(lax.rem(scal[RING], 2) == 0)
    def _():
        shard[...] = probe_in[0, :, pl.ds(row, 8), :128]

    @pl.when(lax.rem(scal[RING], 2) == 1)
    def _():
        shard[...] = probe_in[0, :, pl.ds(row, 8), 128:]

    forward(scal, extended, view, probe, tables, far, power)


def untile_probe(scal, pieces, store):
    for which, piece in enumerate(pieces):
        core = scal[CORE] if which < 2 else 1 - scal[CORE]
        xlo = scal[XLO] if which % 2 == 0 else 1 - scal[XLO]
        first = core * 128 + xlo * 64
        for ring in range(RINGS):
            row = pl.multiple_of(first + ring // 2 * 8, 8)
            store(row, ring % 2 * 128, piece[ring])


def next_kernel(
    scal,
    part_object,
    from_left,
    from_right,
    piece0,
    piece1,
    piece2,
    piece3,
    tables,
    extended,
    view,
    probe,
    far,
    power,
):
    extended[:, :, :SIDE] = part_object[:, :, :SIDE] + from_left[...]
    extended[:, :, SIDE:WIDTH] = part_object[:, :, SIDE:WIDTH]
    extended[:, :, WIDTH:] = part_object[:, :, WIDTH:] + from_right[...]

    def store(row, col, value):
        probe[:, pl.ds(row, 8), col : col + 128] = value

    untile_probe(scal, (piece0, piece1, piece2, piece3), store)
    forward(scal, extended, view, probe, tables, far, power)


def last_kernel(
    scal, part_object, from_left, piece0, piece1, piece2, piece3, object_out, probe_out
):
    object_out[:, :, :SIDE] = part_object[:, :, :SIDE] + from_left[...]
    object_out[:, :, SIDE:] = part_object[:, :, SIDE:WIDTH]

    def store(row, col, value):
        probe_out[0, :, pl.ds(row, 8), col : col + 128] = value

    untile_probe(scal, (piece0, piece1, piece2, piece3), store)


def ratio_kernel(scal, powers, measured, copies):
    total = powers[0]
    for mode in range(1, MODES):
        total = total + powers[mode]
    rows = pl.ds(pl.multiple_of(scal[MODE] * SLAB, SLAB), SLAB)
    counts = measured[0, scal[SLOT], rows, :].astype(F32)
    ratio = jnp.sqrt((counts + SOFT_FLOOR) / (total + SOFT_FLOOR)) - 1.0
    ratio = ratio * scal[LIVE].astype(F32)
    for mode in range(MODES):
        copies[mode] = ratio


def backward_kernel(scal, far, ratio_in, view, probe, tables, grads, keep, send):
    ratio = ratio_in[...]
    chi_real, chi_imag = transform(far[0] * ratio, far[1] * ratio, tables, -1.0)
    probe_real, probe_imag = probe[0], probe[1]
    view_real, view_imag = view[0], view[1]
    grad_real = probe_real * chi_real + probe_imag * chi_imag
    grad_imag = probe_real * chi_imag - probe_imag * chi_real
    light = probe_real * probe_real + probe_imag * probe_imag
    for mode in range(MODES):
        rows = slice(mode * SLAB, mode * SLAB + SLAB)
        grads[mode, 0] = grad_real[rows]
        grads[mode, 1] = grad_imag[rows]
        grads[mode, 2] = light[rows]
    sums = (
        view_real * chi_real + view_imag * chi_imag,
        view_real * chi_imag - view_imag * chi_real,
        (view_real * view_real + view_imag * view_imag) * scal[LIVE].astype(F32),
    )

    def put(target, core):
        for xlo in range(2):
            for ring in range(RINGS):
                row = core * 128 + xlo * 64 + ring // 2 * 8
                col = ring % 2 * 128
                for which in range(3):
                    target[xlo, ring, which] = sums[which][row : row + 8, col : col + 128]

    @pl.when(scal[CORE] == 0)
    def _():
        put(keep, 0)
        put(send, 1)

    @pl.when(scal[CORE] == 1)
    def _():
        put(keep, 1)
        put(send, 0)


def halve_kernel(scal, mine, theirs, keep, send):
    xlo = scal[XLO]
    keep[...] = mine[xlo] + theirs[xlo]
    send[...] = mine[1 - xlo] + theirs[1 - xlo]


def step_kernel(grads, copies):
    total = grads[0]
    for mode in range(1, MODES):
        total = total + grads[mode]
    step = OBJECT_RATE * total[:2] / (total[2:] + OBJECT_DAMP)
    for mode in range(MODES):
        copies[mode] = step


def place_kernel(scal, steps, extended, mine, theirs, part_object, to_left, to_right, sums):
    sums[...] = mine[...] + theirs[...]
    rows, cols, row_rest, col_rest = window(scal)
    part_object[...] = jnp.zeros_like(part_object)
    for part in range(2):
        block = jnp.concatenate(
            [steps[mode, part] for mode in range(MODES)] + [jnp.zeros((8, SIDE), F32)], axis=0
        )
        block = pltpu.roll(block, row_rest, 0)
        block = jnp.concatenate([block, jnp.zeros((ROW_SPAN, 128), F32)], axis=1)
        block = pltpu.roll(block, col_rest, 1)
        part_object[part, rows, cols] = block
    to_left[...] = part_object[:, :, :SIDE]
    to_right[...] = part_object[:, :, WIDTH:]
    part_object[:, :, :WIDTH] = part_object[:, :, :WIDTH] + extended[:, :, :WIDTH]
    part_object[:, :, WIDTH:] = part_object[:, :, WIDTH:] * scal[HAS_NEXT].astype(
        F32
    ) + extended[:, :, WIDTH:]


def probe_kernel(sums, shard_in, shard, copies):
    total = sums[0]
    for ring in range(1, RINGS):
        total = total + sums[ring]
    new = shard_in[...] + PROBE_RATE * total[:2] / (total[2:] + PROBE_DAMP)
    shard[...] = new
    for ring in range(RINGS):
        copies[ring] = new


def call(kernel, outs, *args, scalars=True):
    vmem = pl.BlockSpec(memory_space=pltpu.VMEM)
    in_specs = [vmem] * len(args)
    if scalars:
        in_specs[0] = pl.BlockSpec(memory_space=pltpu.SMEM)
    return pl.pallas_call(
        kernel,
        out_shape=[jax.ShapeDtypeStruct(shape, F32) for shape in outs],
        in_specs=in_specs,
        out_specs=[vmem] * len(outs),
        compiler_params=pltpu.CompilerParams(vmem_limit_bytes=32 * 1024 * 1024),
        name=kernel.__name__,
    )(*args)


def shift_tile(value, steps):
    first, last = max(0, -steps), min(TILES, TILES - steps)
    return lax.ppermute(value, TILE_AXES, [(i, i + steps) for i in range(first, last)])


def other(value, axis):
    return lax.ppermute(value, axis, [(0, 1), (1, 0)])


def exchange(value, axes):
    return lax.all_to_all(value, axes, 0, 0, tiled=True)


def per_device(
    object_tiles, probe_modes, measured, row_offset, col_offset, live_counts, visit_order
):
    beside = shift_tile(object_tiles[:, :, :SIDE], -1)
    tables = jnp.asarray(fourier_tables())
    slots = visit_order[0]
    tile = lax.axis_index(TILE_AXES)
    places = [
        lax.axis_index(MODE_AXES),
        lax.axis_index("core"),
        lax.axis_index("xlo"),
        lax.axis_index("z"),
        (tile < TILES - 1).astype(jnp.int32),
    ]
    chosen = slots[:, None] == jnp.arange(STEPS, dtype=jnp.int32)[None, :]
    per_step = [
        jnp.sum(jnp.where(chosen, row_offset, 0), axis=1),
        jnp.sum(jnp.where(chosen, col_offset, 0), axis=1),
        slots,
        (slots < live_counts[0]).astype(jnp.int32),
    ]
    scalars = jnp.stack(
        per_step + [jnp.broadcast_to(place, (STEPS,)) for place in places], axis=1
    )
    plane = (SIDE, SIDE)
    pair = (2, SIDE, SIDE)
    extended_shape = (2, HEIGHT, WIDE)
    edge = (2, HEIGHT, SIDE)
    for step in range(STEPS):
        scal = scalars[step]
        if step == 0:
            extended, view, probe, shard, far, power = call(
                first_kernel,
                [extended_shape, pair, pair, (2, 8, 128), pair, plane],
                scal,
                object_tiles,
                beside,
                probe_modes,
                tables,
            )
        else:
            extended, view, probe, far, power = call(
                next_kernel,
                [extended_shape, pair, pair, pair, plane],
                scal,
                part_object,
                from_left,
                from_right,
                *pieces,
                tables,
            )
        powers = exchange(power.reshape(MODES, SLAB, SIDE), MODE_AXES)
        (copies,) = call(ratio_kernel, [(MODES, SLAB, SIDE)], scal, powers, measured)
        ratio = exchange(copies, MODE_AXES).reshape(SIDE, SIDE)
        grads, keep, send = call(
            backward_kernel,
            [(MODES, 3, SLAB, SIDE)] + [(2, RINGS, 3, 8, 128)] * 2,
            scal,
            far,
            ratio,
            view,
            probe,
            tables,
        )
        received = other(send, "core")
        grads = exchange(grads, MODE_AXES)
        keep, send = call(halve_kernel, [(RINGS, 3, 8, 128)] * 2, scal, keep, received)
        received = other(send, "xlo")
        (copies,) = call(step_kernel, [(MODES, 2, SLAB, SIDE)], grads, scalars=False)
        steps = exchange(copies, MODE_AXES)
        part_object, to_left, to_right, sums = call(
            place_kernel,
            [extended_shape, edge, edge, (RINGS, 3, 8, 128)],
            scal,
            steps,
            extended,
            keep,
            received,
        )
        from_left = shift_tile(to_right, 1)
        if step < STEPS - 1:
            from_right = shift_tile(to_left, -1)
        sums = exchange(sums, "z")
        shard, copies = call(
            probe_kernel, [(2, 8, 128), (RINGS, 2, 8, 128)], sums, shard, scalars=False
        )
        piece = exchange(copies, "z")
        beyond = other(piece, "xlo")
        pieces = (piece, beyond, other(piece, "core"), other(beyond, "core"))
    return call(
        last_kernel,
        [(2, HEIGHT, WIDTH), (1, 2, SIDE, SIDE)],
        scal,
        part_object,
        from_left,
        *pieces,
    )


def solution(mesh):
    grid = Mesh(mesh.devices.reshape(2, 16, 2, 2, 4), TILE_AXES + MODE_AXES)
    return jax.shard_map(
        per_device,
        mesh=grid,
        in_specs=(
            P(None, None, TILE_AXES),
            P(MODE_AXES, None, None, None),
            P(TILE_AXES, None, None, None),
            P(TILE_AXES, None),
            P(TILE_AXES, None),
            P(TILE_AXES),
            P(TILE_AXES, None),
        ),
        out_specs=(P(None, None, TILE_AXES), P(MODE_AXES, None, None, None)),
        check_vma=False,
    )
```

```python
import math

import jax
import jax.numpy as jnp
import numpy as np
from jax import lax
from jax.experimental import pallas as pl
from jax.experimental.pallas import tpu as pltpu
from jax.sharding import Mesh
from jax.sharding import PartitionSpec as P

SOFT_FLOOR = 0.5
OBJECT_RATE = 1.0
OBJECT_DAMP = 0.5
PROBE_RATE = 1.0
PROBE_DAMP = 1.0

SIDE = 256
HEIGHT = 288
WIDTH = 512
WIDE = WIDTH + SIDE
MODES = 8
SLAB = SIDE // MODES
STEPS = 3
TILES = 64
RINGS = 16
ROW_SPAN = SIDE + 8
COL_SPAN = SIDE + 128
VMEM_LIMIT = 16 * 1024 * 1024

TILE_AXES = ("xlo", "z", "core")
MODE_AXES = ("xhi", "y")

ROW, COL, SLOT, LIVE, MODE, CORE, XLO, RING, HAS_NEXT = range(9)

F32 = jnp.float32
BF16 = jnp.bfloat16


def fourier_tables():
    index = np.arange(SIDE)
    angles = (index[:, None] * index[None, :] % SIDE) * (2.0 * math.pi / SIDE)
    both = np.stack([np.cos(angles), np.sin(angles)]) / math.sqrt(SIDE)
    high = both.astype(jnp.bfloat16)
    low = (both - high.astype(np.float64)).astype(jnp.bfloat16)
    return np.stack([high, low], axis=1)


def halves(value):
    high = value.astype(BF16)
    return high, (value - high.astype(F32)).astype(BF16)


def dot(left, right):
    return jnp.dot(left, right, preferred_element_type=F32)


def transform(real, imag, tables, direction):
    high, low = halves(jnp.concatenate([real, imag], axis=0))

    def rows_by(which):
        return (
            dot(high, tables[which, 0]) + dot(low, tables[which, 0]) + dot(high, tables[which, 1])
        )

    by_cos, by_sin = rows_by(0), rows_by(1)
    half_real = by_cos[:SIDE] + direction * by_sin[SIDE:]
    half_imag = by_cos[SIDE:] - direction * by_sin[:SIDE]
    high, low = halves(jnp.concatenate([half_real, half_imag], axis=1))

    def columns_by(which):
        return (
            dot(tables[which, 0], high) + dot(tables[which, 0], low) + dot(tables[which, 1], high)
        )

    by_cos, by_sin = columns_by(0), columns_by(1)
    return (
        by_cos[:, :SIDE] + direction * by_sin[:, SIDE:],
        by_cos[:, SIDE:] - direction * by_sin[:, :SIDE],
    )


def window(scal):
    row, col = scal[ROW], scal[COL]
    row_block = jnp.minimum(row // 8, 3)
    col_block = jnp.minimum(col // 128, 3)
    rows = pl.ds(pl.multiple_of(row_block * 8, 8), ROW_SPAN)
    cols = pl.ds(pl.multiple_of(col_block * 128, 128), COL_SPAN)
    return rows, cols, row - row_block * 8, col - col_block * 128


def take_patch(scal, extended, view):
    rows, cols, row_rest, col_rest = window(scal)
    for part in range(2):
        block = extended[part, rows, cols]
        block = pltpu.roll(block, lax.rem(COL_SPAN - col_rest, COL_SPAN), 1)[:, :SIDE]
        block = pltpu.roll(block, lax.rem(ROW_SPAN - row_rest, ROW_SPAN), 0)[:SIDE]
        view[part] = block


def forward(view, probe, tables, far, power):
    view_real, view_imag = view[0], view[1]
    probe_real, probe_imag = probe[0], probe[1]
    far_real, far_imag = transform(
        probe_real * view_real - probe_imag * view_imag,
        probe_real * view_imag + probe_imag * view_real,
        tables,
        1.0,
    )
    far[0] = far_real
    far[1] = far_imag
    power[...] = far_real * far_real + far_imag * far_imag


def first_kernel(scal, own, beside, probe_in, tables, extended, view, probe, shard, far, power):
    extended[:, :, :WIDTH] = own[...]
    extended[:, :, WIDTH:] = beside[...]
    probe[...] = probe_in[0]
    row = pl.multiple_of(scal[CORE] * 128 + scal[XLO] * 64 + scal[RING] // 2 * 8, 8)

    @pl.when(lax.rem(scal[RING], 2) == 0)
    def _():
        shard[...] = probe_in[0, :, pl.ds(row, 8), :128]

    @pl.when(lax.rem(scal[RING], 2) == 1)
    def _():
        shard[...] = probe_in[0, :, pl.ds(row, 8), 128:]

    take_patch(scal, extended, view)
    forward(view, probe, tables, far, power)


def untile_probe(scal, pieces, store):
    for which, piece in enumerate(pieces):
        core = scal[CORE] if which < 2 else 1 - scal[CORE]
        xlo = scal[XLO] if which % 2 == 0 else 1 - scal[XLO]
        first = core * 128 + xlo * 64
        for ring in range(RINGS):
            row = pl.multiple_of(first + ring // 2 * 8, 8)
            store(row, ring % 2 * 128, piece[ring])


def view_kernel(scal, part_object, from_left, from_right, extended, view):
    extended[:, :, :SIDE] = part_object[:, :, :SIDE] + from_left[...]
    extended[:, :, SIDE:WIDTH] = part_object[:, :, SIDE:WIDTH]
    extended[:, :, WIDTH:] = part_object[:, :, WIDTH:] + from_right[...]
    take_patch(scal, extended, view)


def next_kernel(scal, view, piece0, piece1, piece2, piece3, tables, probe, far, power):
    def store(row, col, value):
        probe[:, pl.ds(row, 8), col : col + 128] = value

    untile_probe(scal, (piece0, piece1, piece2, piece3), store)
    forward(view, probe, tables, far, power)


def last_kernel(
    scal, part_object, from_left, piece0, piece1, piece2, piece3, object_out, probe_out
):
    object_out[:, :, :SIDE] = part_object[:, :, :SIDE] + from_left[...]
    object_out[:, :, SIDE:] = part_object[:, :, SIDE:WIDTH]

    def store(row, col, value):
        probe_out[0, :, pl.ds(row, 8), col : col + 128] = value

    untile_probe(scal, (piece0, piece1, piece2, piece3), store)


def ratio_kernel(scal, powers, measured, copies):
    total = powers[0]
    for mode in range(1, MODES):
        total = total + powers[mode]
    rows = pl.ds(pl.multiple_of(scal[MODE] * SLAB, SLAB), SLAB)
    counts = measured[0, scal[SLOT], rows, :].astype(F32)
    ratio = jnp.sqrt((counts + SOFT_FLOOR) / (total + SOFT_FLOOR)) - 1.0
    ratio = ratio * scal[LIVE].astype(F32)
    for mode in range(MODES):
        copies[mode] = ratio


def backward_kernel(scal, far, ratio_in, view, tables, chi, keep, send):
    ratio = ratio_in[...]
    chi_real, chi_imag = transform(far[0] * ratio, far[1] * ratio, tables, -1.0)
    chi[0] = chi_real
    chi[1] = chi_imag
    view_real, view_imag = view[0], view[1]
    sums = (
        view_real * chi_real + view_imag * chi_imag,
        view_real * chi_imag - view_imag * chi_real,
        (view_real * view_real + view_imag * view_imag) * scal[LIVE].astype(F32),
    )

    def put(target, core):
        for xlo in range(2):
            for ring in range(RINGS):
                row = core * 128 + xlo * 64 + ring // 2 * 8
                col = ring % 2 * 128
                for which in range(3):
                    target[xlo, ring, which] = sums[which][row : row + 8, col : col + 128]

    @pl.when(scal[CORE] == 0)
    def _():
        put(keep, 0)
        put(send, 1)

    @pl.when(scal[CORE] == 1)
    def _():
        put(keep, 1)
        put(send, 0)


def gradient_kernel(after, chi, probe, grads):
    del after
    for mode in range(MODES):
        rows = slice(mode * SLAB, mode * SLAB + SLAB)
        chi_real, chi_imag = chi[0, rows], chi[1, rows]
        probe_real, probe_imag = probe[0, rows], probe[1, rows]
        grads[mode, 0] = probe_real * chi_real + probe_imag * chi_imag
        grads[mode, 1] = probe_real * chi_imag - probe_imag * chi_real
        grads[mode, 2] = probe_real * probe_real + probe_imag * probe_imag


def halve_kernel(scal, mine, theirs, keep, send):
    xlo = scal[XLO]
    keep[...] = mine[xlo] + theirs[xlo]
    send[...] = mine[1 - xlo] + theirs[1 - xlo]


def step_kernel(after, grads, step):
    del after
    total = grads[0]
    for mode in range(1, MODES):
        total = total + grads[mode]
    step[...] = OBJECT_RATE * total[:2] / (total[2:] + OBJECT_DAMP)


def place_kernel(scal, after, mine, theirs, extended, part_object, to_left, to_right):
    del after
    first = scal[MODE] < MODES // 2
    rows, cols, row_rest, col_rest = window(scal)
    part_object[...] = jnp.zeros_like(part_object)
    for part in range(2):
        own = jnp.concatenate([mine[mode, part] for mode in range(MODES // 2)], axis=0)
        far = jnp.concatenate([theirs[mode, part] for mode in range(MODES // 2)], axis=0)
        block = jnp.concatenate(
            [
                jnp.where(first, own, far),
                jnp.where(first, far, own),
                jnp.zeros((ROW_SPAN - SIDE, SIDE), F32),
            ],
            axis=0,
        )
        block = pltpu.roll(block, row_rest, 0)
        block = jnp.concatenate([block, jnp.zeros((ROW_SPAN, 128), F32)], axis=1)
        block = pltpu.roll(block, col_rest, 1)
        part_object[part, rows, cols] = block
    to_left[...] = part_object[:, :, :SIDE]
    to_right[...] = part_object[:, :, WIDTH:]
    part_object[:, :, :WIDTH] = part_object[:, :, :WIDTH] + extended[:, :, :WIDTH]
    part_object[:, :, WIDTH:] = part_object[:, :, WIDTH:] * scal[HAS_NEXT].astype(
        F32
    ) + extended[:, :, WIDTH:]


def probe_kernel(sums, shard_in, shard, copies):
    total = sums[0]
    for ring in range(1, RINGS):
        total = total + sums[ring]
    new = shard_in[...] + PROBE_RATE * total[:2] / (total[2:] + PROBE_DAMP)
    shard[...] = new
    for ring in range(RINGS):
        copies[ring] = new


def call(kernel, outs, *args, scalars=True, after=False):
    vmem = pl.BlockSpec(memory_space=pltpu.VMEM)
    in_specs = [vmem] * len(args)
    if scalars:
        in_specs[0] = pl.BlockSpec(memory_space=pltpu.SMEM)
    if after:
        in_specs[int(scalars)] = pl.BlockSpec(memory_space=pl.ANY)
    return pl.pallas_call(
        kernel,
        out_shape=[jax.ShapeDtypeStruct(shape, F32) for shape in outs],
        in_specs=in_specs,
        out_specs=[vmem] * len(outs),
        compiler_params=pltpu.CompilerParams(vmem_limit_bytes=VMEM_LIMIT),
        name=kernel.__name__,
    )(*args)


def shift_tile(value, steps):
    first, last = max(0, -steps), min(TILES, TILES - steps)
    return lax.ppermute(value, TILE_AXES, [(i, i + steps) for i in range(first, last)])


def other(value, axis):
    return lax.ppermute(value, axis, [(0, 1), (1, 0)])


def exchange(value, axes):
    return lax.all_to_all(value, axes, 0, 0, tiled=True)


def per_device(
    object_tiles, probe_modes, measured, row_offset, col_offset, live_counts, visit_order
):
    beside = shift_tile(object_tiles[:, :, :SIDE], -1)
    tables = jnp.asarray(fourier_tables())
    slots = visit_order[0]
    tile = lax.axis_index(TILE_AXES)
    places = [
        lax.axis_index(MODE_AXES),
        lax.axis_index("core"),
        lax.axis_index("xlo"),
        lax.axis_index("z"),
        (tile < TILES - 1).astype(jnp.int32),
    ]
    chosen = slots[:, None] == jnp.arange(STEPS, dtype=jnp.int32)[None, :]
    per_step = [
        jnp.sum(jnp.where(chosen, row_offset, 0), axis=1),
        jnp.sum(jnp.where(chosen, col_offset, 0), axis=1),
        slots,
        (slots < live_counts[0]).astype(jnp.int32),
    ]
    scalars = jnp.stack(
        per_step + [jnp.broadcast_to(place, (STEPS,)) for place in places], axis=1
    )
    plane = (SIDE, SIDE)
    pair = (2, SIDE, SIDE)
    extended_shape = (2, HEIGHT, WIDE)
    edge = (2, HEIGHT, SIDE)
    for step in range(STEPS):
        scal = scalars[step]
        if step == 0:
            extended, view, probe, shard, far, power = call(
                first_kernel,
                [extended_shape, pair, pair, (2, 8, 128), pair, plane],
                scal,
                object_tiles,
                beside,
                probe_modes,
                tables,
            )
        else:
            extended, view = call(
                view_kernel, [extended_shape, pair], scal, part_object, from_left, from_right
            )
            probe, far, power = call(
                next_kernel, [pair, pair, plane], scal, view, *pieces, tables
            )
        powers = exchange(power.reshape(MODES, SLAB, SIDE), MODE_AXES)
        (copies,) = call(ratio_kernel, [(MODES, SLAB, SIDE)], scal, powers, measured)
        ratio = exchange(copies, MODE_AXES).reshape(SIDE, SIDE)
        chi, keep, send = call(
            backward_kernel,
            [pair] + [(2, RINGS, 3, 8, 128)] * 2,
            scal,
            far,
            ratio,
            view,
            tables,
        )
        received = other(send, "core")
        keep, send = call(halve_kernel, [(RINGS, 3, 8, 128)] * 2, scal, keep, received)
        received = other(send, "xlo")
        (grads,) = call(
            gradient_kernel, [(MODES, 3, SLAB, SIDE)], keep, chi, probe, scalars=False, after=True
        )
        grads = exchange(grads, MODE_AXES)
        sums = keep + received
        (object_step,) = call(
            step_kernel, [(2, SLAB, SIDE)], sums, grads, scalars=False, after=True
        )
        sums = exchange(sums, "z")
        shard, shards = call(
            probe_kernel, [(2, 8, 128), (RINGS, 2, 8, 128)], sums, shard, scalars=False
        )
        near_steps = lax.all_gather(object_step, "y")
        far_steps = other(near_steps, "xhi")
        part_object, to_left, to_right = call(
            place_kernel,
            [extended_shape, edge, edge],
            scal,
            shards,
            near_steps,
            far_steps,
            extended,
            after=True,
        )
        from_left = shift_tile(to_right, 1)
        if step < STEPS - 1:
            from_right = shift_tile(to_left, -1)
        piece = exchange(shards, "z")
        beyond = other(piece, "xlo")
        pieces = (piece, beyond, other(piece, "core"), other(beyond, "core"))
    return call(
        last_kernel,
        [(2, HEIGHT, WIDTH), (1, 2, SIDE, SIDE)],
        scal,
        part_object,
        from_left,
        *pieces,
    )


def solution(mesh):
    grid = Mesh(mesh.devices.reshape(2, 16, 2, 2, 4), TILE_AXES + MODE_AXES)
    return jax.shard_map(
        per_device,
        mesh=grid,
        in_specs=(
            P(None, None, TILE_AXES),
            P(MODE_AXES, None, None, None),
            P(TILE_AXES, None, None, None),
            P(TILE_AXES, None),
            P(TILE_AXES, None),
            P(TILE_AXES),
            P(TILE_AXES, None),
        ),
        out_specs=(P(None, None, TILE_AXES), P(MODE_AXES, None, None, None)),
        check_vma=False,
    )
```

```python
import math

import jax
import jax.numpy as jnp
import numpy as np
from jax import lax
from jax.experimental import pallas as pl
from jax.experimental.pallas import tpu as pltpu
from jax.sharding import Mesh
from jax.sharding import PartitionSpec as P

SOFT_FLOOR = 0.5
OBJECT_RATE = 1.0
OBJECT_DAMP = 0.5
PROBE_RATE = 1.0
PROBE_DAMP = 1.0

SIDE = 256
HEIGHT = 288
WIDTH = 512
WIDE = WIDTH + SIDE
MODES = 8
SLAB = SIDE // MODES
BAND = 2 * SLAB
STEPS = 3
TILES = 64
RINGS = 16
LANES = 128
COL_SPAN = SIDE + LANES
OUT_ROWS = 40
VMEM_LIMIT = 16 * 1024 * 1024

TILE_AXES = ("xlo", "z", "core")
MODE_AXES = ("xhi", "y")

ROW, COL, SLOT, LIVE, MODE, CORE, XLO, RING, HAS_NEXT = range(9)

F32 = jnp.float32
BF16 = jnp.bfloat16


def fourier_tables():
    index = np.arange(SIDE)
    angles = (index[:, None] * index[None, :] % SIDE) * (2.0 * math.pi / SIDE)
    both = np.stack([np.cos(angles), np.sin(angles)]) / math.sqrt(SIDE)
    high = both.astype(jnp.bfloat16)
    low = (both - high.astype(np.float64)).astype(jnp.bfloat16)
    return np.stack([high, low], axis=1)


def halves(value):
    high = value.astype(BF16)
    return high, (value - high.astype(F32)).astype(BF16)


def dot(left, right):
    return jnp.dot(left, right, preferred_element_type=F32)


def rows_transform(real, imag, tables, direction):
    high, low = halves(jnp.concatenate([real, imag], axis=0))

    def by(which):
        return (
            dot(high, tables[which, 0]) + dot(low, tables[which, 0]) + dot(high, tables[which, 1])
        )

    by_cos, by_sin = by(0), by(1)
    return (
        by_cos[:SIDE] + direction * by_sin[SIDE:],
        by_cos[SIDE:] - direction * by_sin[:SIDE],
    )


def columns_transform(real, imag, tables, direction):
    high, low = halves(jnp.concatenate([real, imag], axis=1))

    def by(which):
        return (
            dot(tables[which, 0], high) + dot(tables[which, 0], low) + dot(tables[which, 1], high)
        )

    by_cos, by_sin = by(0), by(1)
    return (
        by_cos[:, :SIDE] + direction * by_sin[:, SIDE:],
        by_cos[:, SIDE:] - direction * by_sin[:, :SIDE],
    )


def swap_blocks(parts):
    lanes = lax.broadcasted_iota(jnp.int32, (parts[0].shape[0], LANES), 1)
    grid = [[part[:, :LANES], part[:, LANES:]] for part in parts]
    grid = [[grid[(m & 3) | (h << 2)][m >> 2] for h in range(2)] for m in range(MODES)]
    for bit in (2, 1):
        shift = bit * SLAB
        low = (lanes & shift) == 0
        new = [None] * MODES
        for m in range(MODES):
            if m & bit:
                continue
            a, b = grid[m], grid[m | bit]
            new[m] = [jnp.where(low, a[h], pltpu.roll(b[h], shift, 1)) for h in range(2)]
            new[m | bit] = [
                jnp.where(low, pltpu.roll(a[h], LANES - shift, 1), b[h]) for h in range(2)
            ]
        grid = new
    return [jnp.concatenate(pair, axis=1) for pair in grid]


def stacked(pieces):
    return jnp.concatenate(list(pieces), axis=0)


def column_window(scal):
    col = scal[COL]
    block = jnp.minimum(col // LANES, WIDTH // LANES - 1)
    return pl.ds(pl.multiple_of(block * LANES, LANES), COL_SPAN), col - block * LANES


def take_patch(scal, band, view):
    cols, rest = column_window(scal)
    for part in range(2):
        block = band[part, :, cols]
        block = pltpu.roll(block, lax.rem(COL_SPAN - rest, COL_SPAN), 1)[:, :SIDE]
        view[part] = pltpu.roll(block, lax.rem(BAND - scal[ROW], BAND), 0)[:SLAB]


def forward(view, probe, tables, spectra):
    view_real = stacked([view[0]] * MODES)
    view_imag = stacked([view[1]] * MODES)
    probe_real = stacked(probe[mode, 0] for mode in range(MODES))
    probe_imag = stacked(probe[mode, 1] for mode in range(MODES))
    both = rows_transform(
        probe_real * view_real - probe_imag * view_imag,
        probe_real * view_imag + probe_imag * view_real,
        tables,
        1.0,
    )
    for part in range(2):
        blocks = [both[part][mode * SLAB : (mode + 1) * SLAB] for mode in range(MODES)]
        for place, block in enumerate(swap_blocks(blocks)):
            spectra[place, part] = block


def split_kernel(probe_in, pieces):
    for place in range(MODES):
        pieces[place] = probe_in[0, :, place * SLAB : (place + 1) * SLAB, :]


def first_kernel(scal, own, beside, probe, tables, band, view, shard, spectra):
    band[:, :, :WIDTH] = own[...]
    band[:, :, WIDTH:] = beside[...]
    take_patch(scal, band, view)
    mode = scal[RING] // 2
    rows = pl.ds(pl.multiple_of(scal[CORE] * 16 + scal[XLO] * 8, 8), 8)

    @pl.when(lax.rem(scal[RING], 2) == 0)
    def _():
        shard[...] = probe[mode, :, rows, :LANES]

    @pl.when(lax.rem(scal[RING], 2) == 1)
    def _():
        shard[...] = probe[mode, :, rows, LANES:]

    forward(view, probe, tables, spectra)


def piece_row(scal, which):
    core = scal[CORE] if which < 2 else 1 - scal[CORE]
    xlo = scal[XLO] if which % 2 == 0 else 1 - scal[XLO]
    return core * 16 + xlo * 8


def next_kernel(scal, view, piece0, piece1, piece2, piece3, tables, probe, spectra):
    for which, piece in enumerate((piece0, piece1, piece2, piece3)):
        rows = pl.ds(pl.multiple_of(piece_row(scal, which), 8), 8)
        for mode in range(MODES):
            probe[mode, :, rows, :LANES] = piece[2 * mode]
            probe[mode, :, rows, LANES:] = piece[2 * mode + 1]
    forward(view, probe, tables, spectra)


def counts_kernel(scal, measured, counts):
    block = measured[0, scal[SLOT]].astype(F32)
    block = pltpu.roll(block, lax.rem(SIDE - scal[MODE] * SLAB, SIDE), 1)[:, :LANES]
    lanes = lax.broadcasted_iota(jnp.int32, block.shape, 1)
    block = jnp.where(lanes < SLAB, block, 0.0)
    block = block + pltpu.roll(block, SLAB, 1)
    counts[...] = block + pltpu.roll(block, 2 * SLAB, 1)


def ratio_kernel(scal, spectra, counts, tables, out):
    real = stacked(spectra[place, 0] for place in range(MODES))
    imag = stacked(spectra[place, 1] for place in range(MODES))
    far_real, far_imag = columns_transform(real, imag, tables, 1.0)
    power = far_real * far_real + far_imag * far_imag
    total = power[:, :LANES] + power[:, LANES:]
    total = total + pltpu.roll(total, 2 * SLAB, 1)
    total = total + pltpu.roll(total, SLAB, 1)
    ratio = jnp.sqrt((counts[...] + SOFT_FLOOR) / (total + SOFT_FLOOR)) - 1.0
    ratio = ratio * scal[LIVE].astype(F32)
    ratio = jnp.concatenate([ratio, ratio], axis=1)
    both = columns_transform(far_real * ratio, far_imag * ratio, tables, -1.0)
    for part in range(2):
        for place in range(MODES):
            out[place, part] = both[part][place * SLAB : (place + 1) * SLAB]


def backward_kernel(scal, spectra, view, tables, chi, keep, send):
    real = stacked(swap_blocks([spectra[place, 0] for place in range(MODES)]))
    imag = stacked(swap_blocks([spectra[place, 1] for place in range(MODES)]))
    chi_real, chi_imag = rows_transform(real, imag, tables, -1.0)
    view_real, view_imag = view[0], view[1]
    sums = []
    for mode in range(MODES):
        real = chi_real[mode * SLAB : (mode + 1) * SLAB]
        imag = chi_imag[mode * SLAB : (mode + 1) * SLAB]
        chi[mode, 0] = real
        chi[mode, 1] = imag
        sums.append(view_real * real + view_imag * imag)
        sums.append(view_real * imag - view_imag * real)
    sums.append((view_real * view_real + view_imag * view_imag) * scal[LIVE].astype(F32))

    @pl.when(scal[CORE] == 0)
    def _():
        for index, value in enumerate(sums):
            keep[index] = value[:16]
            send[index] = value[16:]

    @pl.when(scal[CORE] == 1)
    def _():
        for index, value in enumerate(sums):
            keep[index] = value[16:]
            send[index] = value[:16]


def halve_kernel(scal, mine, theirs, keep, send):
    ours = pl.ds(pl.multiple_of(scal[XLO] * 8, 8), 8)
    others = pl.ds(pl.multiple_of((1 - scal[XLO]) * 8, 8), 8)
    keep[...] = mine[:, ours] + theirs[:, ours]
    send[...] = mine[:, others] + theirs[:, others]


def pack_kernel(mine, theirs, packed):
    for half in range(2):
        lanes = slice(half * LANES, (half + 1) * LANES)
        total = mine[:, :, lanes] + theirs[:, :, lanes]
        for mode in range(MODES):
            packed[2 * mode + half, 0] = total[2 * mode]
            packed[2 * mode + half, 1] = total[2 * mode + 1]
            packed[2 * mode + half, 2] = total[2 * MODES]


def step_kernel(chi, probe, step):
    real = imag = light = 0.0
    for mode in range(MODES):
        probe_real, probe_imag = probe[mode, 0], probe[mode, 1]
        real = real + (probe_real * chi[mode, 0] + probe_imag * chi[mode, 1])
        imag = imag + (probe_real * chi[mode, 1] - probe_imag * chi[mode, 0])
        light = light + (probe_real * probe_real + probe_imag * probe_imag)
    step[0] = OBJECT_RATE * real / (light + OBJECT_DAMP)
    step[1] = OBJECT_RATE * imag / (light + OBJECT_DAMP)


def place_kernel(scal, above, step, below, band, part_band, to_left, to_right):
    cols, rest = column_window(scal)
    height = 3 * SLAB
    part_band[...] = jnp.zeros_like(part_band)
    for part in range(2):
        block = stacked([above[part], step[part], below[part]])
        block = pltpu.roll(block, lax.rem(2 * SLAB + scal[ROW], height), 0)[:BAND]
        block = jnp.concatenate([block, jnp.zeros((BAND, LANES), F32)], axis=1)
        part_band[part, :, cols] = pltpu.roll(block, rest, 1)
    to_left[...] = part_band[:, :, :SIDE]
    to_right[...] = part_band[:, :, WIDTH:]
    part_band[:, :, :WIDTH] = part_band[:, :, :WIDTH] + band[:, :, :WIDTH]
    part_band[:, :, WIDTH:] = (
        part_band[:, :, WIDTH:] * scal[HAS_NEXT].astype(F32) + band[:, :, WIDTH:]
    )


def view_kernel(scal, part_band, from_left, from_right, band, view):
    band[:, :, :SIDE] = part_band[:, :, :SIDE] + from_left[...]
    band[:, :, SIDE:WIDTH] = part_band[:, :, SIDE:WIDTH]
    band[:, :, WIDTH:] = part_band[:, :, WIDTH:] + from_right[...]
    take_patch(scal, band, view)


def probe_kernel(sums, shard_in, shard, copies):
    total = sums[0]
    for ring in range(1, RINGS):
        total = total + sums[ring]
    new = shard_in[...] + PROBE_RATE * total[:2] / (total[2:] + PROBE_DAMP)
    shard[...] = new
    for ring in range(RINGS):
        copies[ring] = new


def out_rows_kernel(scal, part_band, from_left, rows_out):
    rows = pl.ds(pl.multiple_of(scal[MODE] // 2 * 8, 8), OUT_ROWS)
    rows_out[:, :, :SIDE] = part_band[:, rows, :SIDE] + from_left[:, rows, :]
    rows_out[:, :, SIDE:] = part_band[:, rows, SIDE:WIDTH]


def object_kernel(scal, near, far, object_out):
    def write(first, last):
        for place in range(MODES):
            source = first if place < MODES // 2 else last
            row = place * 9 // 2 * 8
            object_out[:, row : row + OUT_ROWS, :] = source[place % (MODES // 2)]

    @pl.when(scal[MODE] < MODES // 2)
    def _():
        write(near, far)

    @pl.when(scal[MODE] >= MODES // 2)
    def _():
        write(far, near)


def probe_out_kernel(scal, piece0, piece1, piece2, piece3, probe_out):
    for which, piece in enumerate((piece0, piece1, piece2, piece3)):
        first = piece_row(scal, which)
        for place in range(MODES):
            rows = pl.ds(pl.multiple_of(first + place * SLAB, 8), 8)
            probe_out[0, :, rows, :LANES] = piece[2 * place]
            probe_out[0, :, rows, LANES:] = piece[2 * place + 1]


def call(kernel, outs, *args, scalars=True, after=()):
    vmem = pl.BlockSpec(memory_space=pltpu.VMEM)
    in_specs = [vmem] * len(args) + [pl.BlockSpec(memory_space=pl.ANY)] * len(after)
    if scalars:
        in_specs[0] = pl.BlockSpec(memory_space=pltpu.SMEM)

    def body(*refs):
        kernel(*refs[: len(args)], *refs[len(args) + len(after) :])

    return pl.pallas_call(
        body,
        out_shape=[jax.ShapeDtypeStruct(shape, F32) for shape in outs],
        in_specs=in_specs,
        out_specs=[vmem] * len(outs),
        compiler_params=pltpu.CompilerParams(vmem_limit_bytes=VMEM_LIMIT),
        name=kernel.__name__,
    )(*args, *after)


def shift(value, axes, count, steps):
    first, last = max(0, -steps), min(count, count - steps)
    return lax.ppermute(value, axes, [(i, i + steps) for i in range(first, last)])


def other(value, axis):
    return lax.ppermute(value, axis, [(0, 1), (1, 0)])


def exchange(value, axes):
    return lax.all_to_all(value, axes, 0, 0, tiled=True)


def four_pieces(piece):
    beyond = other(piece, "xlo")
    return piece, beyond, other(piece, "core"), other(beyond, "core")


def per_device(
    object_tiles, probe_modes, measured, row_offset, col_offset, live_counts, visit_order
):
    tables = jnp.asarray(fourier_tables())
    slots = visit_order[0]
    tile = lax.axis_index(TILE_AXES)
    mode = lax.axis_index(MODE_AXES)
    own = lax.dynamic_slice_in_dim(object_tiles, mode * SLAB, BAND, axis=1)
    beside = shift(own[:, :, :SIDE], TILE_AXES, TILES, -1)
    places = [
        mode,
        lax.axis_index("core"),
        lax.axis_index("xlo"),
        lax.axis_index("z"),
        (tile < TILES - 1).astype(jnp.int32),
    ]
    chosen = slots[:, None] == jnp.arange(STEPS, dtype=jnp.int32)[None, :]
    per_step = [
        jnp.sum(jnp.where(chosen, row_offset, 0), axis=1),
        jnp.sum(jnp.where(chosen, col_offset, 0), axis=1),
        slots,
        (slots < live_counts[0]).astype(jnp.int32),
    ]
    scalars = jnp.stack(
        per_step + [jnp.broadcast_to(place, (STEPS,)) for place in places], axis=1
    )
    slabs = (MODES, 2, SLAB, SIDE)
    slab_pair = (2, SLAB, SIDE)
    band_shape = (2, BAND, WIDE)
    edge = (2, BAND, SIDE)
    (pieces,) = call(split_kernel, [slabs], probe_modes, scalars=False)
    probe = exchange(pieces, MODE_AXES)
    (counts,) = call(counts_kernel, [(SIDE, LANES)], scalars[0], measured)
    for step in range(STEPS):
        scal = scalars[step]
        final = step == STEPS - 1
        if step == 0:
            band, view, shard, spectra = call(
                first_kernel,
                [band_shape, slab_pair, (2, 8, LANES), slabs],
                scal,
                own,
                beside,
                probe,
                tables,
                after=(counts,),
            )
        else:
            band, view = call(
                view_kernel, [band_shape, slab_pair], scal, part_band, from_left, from_right
            )
            probe, spectra = call(
                next_kernel, [slabs, slabs], scal, view, *pieces, tables, after=(counts,)
            )
        spectra = exchange(spectra, MODE_AXES)
        (spectra,) = call(ratio_kernel, [slabs], scal, spectra, counts, tables)
        spectra = exchange(spectra, MODE_AXES)
        chi, keep, send = call(
            backward_kernel,
            [slabs] + [(2 * MODES + 1, 16, SIDE)] * 2,
            scal,
            spectra,
            view,
            tables,
        )
        received = other(send, "core")
        keep, send = call(halve_kernel, [(2 * MODES + 1, 8, SIDE)] * 2, scal, keep, received)
        received = other(send, "xlo")
        (object_step,) = call(
            step_kernel, [slab_pair], chi, probe, scalars=False, after=(keep,)
        )
        above = shift(object_step, MODE_AXES, MODES, 1)
        below = shift(object_step, MODE_AXES, MODES, -1)
        (packed,) = call(
            pack_kernel,
            [(RINGS, 3, 8, LANES)],
            keep,
            received,
            scalars=False,
            after=(above, below) if final else (object_step,),
        )
        sums = exchange(packed, "z")
        if not final:
            (counts,) = call(
                counts_kernel, [(SIDE, LANES)], scalars[step + 1], measured, after=(packed,)
            )
        placing = [scal, above, object_step, below, band]
        if final:
            part_band, _, to_right = call(
                place_kernel, [band_shape, edge, edge], *placing, after=(packed,)
            )
            from_left = shift(to_right, TILE_AXES, TILES, 1)
        shard, shards = call(
            probe_kernel,
            [(2, 8, LANES), (RINGS, 2, 8, LANES)],
            sums,
            shard,
            scalars=False,
            after=(from_left,) if final else (above, below, counts),
        )
        piece = exchange(shards, "z")
        if final:
            (rows_out,) = call(
                out_rows_kernel,
                [(2, OUT_ROWS, WIDTH)],
                scal,
                part_band,
                from_left,
                after=(shards,),
            )
            near = lax.all_gather(rows_out, "y")
            piece, near = lax.optimization_barrier((piece, near))
        else:
            part_band, to_left, to_right = call(
                place_kernel, [band_shape, edge, edge], *placing, after=(shards,)
            )
            from_left = shift(to_right, TILE_AXES, TILES, 1)
            from_right = shift(to_left, TILE_AXES, TILES, -1)
            piece, from_left, from_right = lax.optimization_barrier(
                (piece, from_left, from_right)
            )
            pieces = four_pieces(piece)
    far = other(near, "xhi")
    (object_out,) = call(object_kernel, [(2, HEIGHT, WIDTH)], scal, near, far)
    piece = exchange(piece.reshape(MODES, 4, 8, LANES), MODE_AXES)
    pieces = four_pieces(piece.reshape(RINGS, 2, 8, LANES))
    (probe_out,) = call(probe_out_kernel, [(1, 2, SIDE, SIDE)], scal, *pieces)
    return object_out, probe_out


def solution(mesh):
    grid = Mesh(mesh.devices.reshape(2, 16, 2, 2, 4), TILE_AXES + MODE_AXES)
    return jax.shard_map(
        per_device,
        mesh=grid,
        in_specs=(
            P(None, None, TILE_AXES),
            P(MODE_AXES, None, None, None),
            P(TILE_AXES, None, None, None),
            P(TILE_AXES, None),
            P(TILE_AXES, None),
            P(TILE_AXES),
            P(TILE_AXES, None),
        ),
        out_specs=(P(None, None, TILE_AXES), P(MODE_AXES, None, None, None)),
        check_vma=False,
    )
```

```python
import math

import jax
import jax.numpy as jnp
import numpy as np
from jax import lax
from jax.experimental import pallas as pl
from jax.experimental.pallas import tpu as pltpu
from jax.sharding import Mesh
from jax.sharding import PartitionSpec as P

SOFT_FLOOR = 0.5
OBJECT_RATE = 1.0
OBJECT_DAMP = 0.5
PROBE_RATE = 1.0
PROBE_DAMP = 1.0

SIDE = 256
HEIGHT = 288
WIDTH = 512
WIDE = WIDTH + SIDE
MODES = 8
SLAB = SIDE // MODES
BAND = 2 * SLAB
STEPS = 3
TILES = 64
RINGS = 16
LANES = 128
COL_SPAN = SIDE + LANES
OUT_ROWS = 40
VMEM_LIMIT = 16 * 1024 * 1024

TILE_AXES = ("xlo", "z", "core")
MODE_AXES = ("xhi", "y")

ROW, COL, SLOT, LIVE, MODE, CORE, XLO, RING, HAS_NEXT = range(9)

F32 = jnp.float32
BF16 = jnp.bfloat16


def fourier_tables():
    index = np.arange(SIDE)
    angles = (index[:, None] * index[None, :] % SIDE) * (2.0 * math.pi / SIDE)
    both = np.stack([np.cos(angles), np.sin(angles)]) / math.sqrt(SIDE)
    high = both.astype(jnp.bfloat16)
    low = (both - high.astype(np.float64)).astype(jnp.bfloat16)
    return np.stack([high, low], axis=1)


def halves(value):
    high = value.astype(BF16)
    return high, (value - high.astype(F32)).astype(BF16)


def dot(left, right):
    return jnp.dot(left, right, preferred_element_type=F32)


def rows_transform(real, imag, tables, direction):
    high, low = halves(jnp.concatenate([real, imag], axis=0))

    def by(which):
        return (
            dot(high, tables[which, 0]) + dot(low, tables[which, 0]) + dot(high, tables[which, 1])
        )

    by_cos, by_sin = by(0), by(1)
    return (
        by_cos[:SIDE] + direction * by_sin[SIDE:],
        by_cos[SIDE:] - direction * by_sin[:SIDE],
    )


def columns_transform(real, imag, tables, direction):
    high, low = halves(jnp.concatenate([real, imag], axis=1))

    def by(which):
        return (
            dot(tables[which, 0], high) + dot(tables[which, 0], low) + dot(tables[which, 1], high)
        )

    by_cos, by_sin = by(0), by(1)
    return (
        by_cos[:, :SIDE] + direction * by_sin[:, SIDE:],
        by_cos[:, SIDE:] - direction * by_sin[:, :SIDE],
    )


def swap_blocks(parts):
    lanes = lax.broadcasted_iota(jnp.int32, (parts[0].shape[0], LANES), 1)
    grid = [[part[:, :LANES], part[:, LANES:]] for part in parts]
    grid = [[grid[(m & 3) | (h << 2)][m >> 2] for h in range(2)] for m in range(MODES)]
    for bit in (2, 1):
        shift = bit * SLAB
        low = (lanes & shift) == 0
        new = [None] * MODES
        for m in range(MODES):
            if m & bit:
                continue
            a, b = grid[m], grid[m | bit]
            new[m] = [jnp.where(low, a[h], pltpu.roll(b[h], shift, 1)) for h in range(2)]
            new[m | bit] = [
                jnp.where(low, pltpu.roll(a[h], LANES - shift, 1), b[h]) for h in range(2)
            ]
        grid = new
    return [jnp.concatenate(pair, axis=1) for pair in grid]


def stacked(pieces):
    return jnp.concatenate(list(pieces), axis=0)


def column_window(scal):
    col = scal[COL]
    block = jnp.minimum(col // LANES, WIDTH // LANES - 1)
    return pl.ds(pl.multiple_of(block * LANES, LANES), COL_SPAN), col - block * LANES


def take_patch(scal, band, view):
    cols, rest = column_window(scal)
    for part in range(2):
        block = band[part, :, cols]
        block = pltpu.roll(block, lax.rem(COL_SPAN - rest, COL_SPAN), 1)[:, :SIDE]
        view[part] = pltpu.roll(block, lax.rem(BAND - scal[ROW], BAND), 0)[:SLAB]


def forward(view, probe, tables, spectra):
    view_real = stacked([view[0]] * MODES)
    view_imag = stacked([view[1]] * MODES)
    probe_real = stacked(probe[mode, 0] for mode in range(MODES))
    probe_imag = stacked(probe[mode, 1] for mode in range(MODES))
    both = rows_transform(
        probe_real * view_real - probe_imag * view_imag,
        probe_real * view_imag + probe_imag * view_real,
        tables,
        1.0,
    )
    for part in range(2):
        blocks = [both[part][mode * SLAB : (mode + 1) * SLAB] for mode in range(MODES)]
        for place, block in enumerate(swap_blocks(blocks)):
            spectra[place, part] = block


def first_kernel(scal, own, beside, probe, tables, band, view, shard, spectra):
    band[:, :, :WIDTH] = own[...]
    band[:, :, WIDTH:] = beside[...]
    take_patch(scal, band, view)
    mode = scal[RING] // 2
    rows = pl.ds(pl.multiple_of(scal[CORE] * 16 + scal[XLO] * 8, 8), 8)

    @pl.when(lax.rem(scal[RING], 2) == 0)
    def _():
        shard[...] = probe[mode, :, rows, :LANES]

    @pl.when(lax.rem(scal[RING], 2) == 1)
    def _():
        shard[...] = probe[mode, :, rows, LANES:]

    forward(view, probe, tables, spectra)


def next_kernel(view, pieces, tables, probe, spectra):
    for xlo in range(2):
        for core in range(2):
            row = core * 16 + xlo * 8
            for mode in range(MODES):
                probe[mode, :, row : row + 8, :LANES] = pieces[xlo, core, 2 * mode]
                probe[mode, :, row : row + 8, LANES:] = pieces[xlo, core, 2 * mode + 1]
    forward(view, probe, tables, spectra)


def counts_kernel(scal, measured, counts):
    block = measured[0, scal[SLOT]].astype(F32)
    block = pltpu.roll(block, lax.rem(SIDE - scal[MODE] * SLAB, SIDE), 1)[:, :LANES]
    lanes = lax.broadcasted_iota(jnp.int32, block.shape, 1)
    block = jnp.where(lanes < SLAB, block, 0.0)
    block = block + pltpu.roll(block, SLAB, 1)
    counts[...] = block + pltpu.roll(block, 2 * SLAB, 1)


def ratio_kernel(scal, spectra, counts, tables, out):
    real = stacked(spectra[place, 0] for place in range(MODES))
    imag = stacked(spectra[place, 1] for place in range(MODES))
    far_real, far_imag = columns_transform(real, imag, tables, 1.0)
    power = far_real * far_real + far_imag * far_imag
    total = power[:, :LANES] + power[:, LANES:]
    total = total + pltpu.roll(total, 2 * SLAB, 1)
    total = total + pltpu.roll(total, SLAB, 1)
    ratio = jnp.sqrt((counts[...] + SOFT_FLOOR) / (total + SOFT_FLOOR)) - 1.0
    ratio = ratio * scal[LIVE].astype(F32)
    ratio = jnp.concatenate([ratio, ratio], axis=1)
    both = columns_transform(far_real * ratio, far_imag * ratio, tables, -1.0)
    for part in range(2):
        for place in range(MODES):
            out[place, part] = both[part][place * SLAB : (place + 1) * SLAB]


def backward_kernel(scal, spectra, view, tables, chi, keep, send):
    real = stacked(swap_blocks([spectra[place, 0] for place in range(MODES)]))
    imag = stacked(swap_blocks([spectra[place, 1] for place in range(MODES)]))
    chi_real, chi_imag = rows_transform(real, imag, tables, -1.0)
    view_real, view_imag = view[0], view[1]
    sums = []
    for mode in range(MODES):
        real = chi_real[mode * SLAB : (mode + 1) * SLAB]
        imag = chi_imag[mode * SLAB : (mode + 1) * SLAB]
        chi[mode, 0] = real
        chi[mode, 1] = imag
        sums.append(view_real * real + view_imag * imag)
        sums.append(view_real * imag - view_imag * real)
    sums.append((view_real * view_real + view_imag * view_imag) * scal[LIVE].astype(F32))

    @pl.when(scal[CORE] == 0)
    def _():
        for index, value in enumerate(sums):
            keep[index] = value[:16]
            send[index] = value[16:]

    @pl.when(scal[CORE] == 1)
    def _():
        for index, value in enumerate(sums):
            keep[index] = value[16:]
            send[index] = value[:16]


def halve_kernel(scal, mine, theirs, keep, send):
    ours = pl.ds(pl.multiple_of(scal[XLO] * 8, 8), 8)
    others = pl.ds(pl.multiple_of((1 - scal[XLO]) * 8, 8), 8)
    keep[...] = mine[:, ours] + theirs[:, ours]
    send[...] = mine[:, others] + theirs[:, others]


def pack_kernel(mine, theirs, packed):
    for half in range(2):
        lanes = slice(half * LANES, (half + 1) * LANES)
        total = mine[:, :, lanes] + theirs[:, :, lanes]
        for mode in range(MODES):
            packed[2 * mode + half, 0] = total[2 * mode]
            packed[2 * mode + half, 1] = total[2 * mode + 1]
            packed[2 * mode + half, 2] = total[2 * MODES]


def step_kernel(chi, probe, step):
    real = imag = light = 0.0
    for mode in range(MODES):
        probe_real, probe_imag = probe[mode, 0], probe[mode, 1]
        real = real + (probe_real * chi[mode, 0] + probe_imag * chi[mode, 1])
        imag = imag + (probe_real * chi[mode, 1] - probe_imag * chi[mode, 0])
        light = light + (probe_real * probe_real + probe_imag * probe_imag)
    step[0] = OBJECT_RATE * real / (light + OBJECT_DAMP)
    step[1] = OBJECT_RATE * imag / (light + OBJECT_DAMP)


def place_kernel(scal, above, step, below, band, part_band, to_left, to_right):
    cols, rest = column_window(scal)
    height = 3 * SLAB
    part_band[...] = jnp.zeros_like(part_band)
    for part in range(2):
        block = stacked([above[part], step[part], below[part]])
        block = pltpu.roll(block, lax.rem(2 * SLAB + scal[ROW], height), 0)[:BAND]
        block = jnp.concatenate([block, jnp.zeros((BAND, LANES), F32)], axis=1)
        part_band[part, :, cols] = pltpu.roll(block, rest, 1)
    to_left[...] = part_band[:, :, :SIDE]
    to_right[...] = part_band[:, :, WIDTH:]
    part_band[:, :, :WIDTH] = part_band[:, :, :WIDTH] + band[:, :, :WIDTH]
    part_band[:, :, WIDTH:] = (
        part_band[:, :, WIDTH:] * scal[HAS_NEXT].astype(F32) + band[:, :, WIDTH:]
    )


def view_kernel(scal, part_band, from_left, from_right, band, view):
    band[:, :, :SIDE] = part_band[:, :, :SIDE] + from_left[...]
    band[:, :, SIDE:WIDTH] = part_band[:, :, SIDE:WIDTH]
    band[:, :, WIDTH:] = part_band[:, :, WIDTH:] + from_right[...]
    take_patch(scal, band, view)


def probe_kernel(sums, shard_in, shard, copies):
    total = sums[0]
    for ring in range(1, RINGS):
        total = total + sums[ring]
    new = shard_in[...] + PROBE_RATE * total[:2] / (total[2:] + PROBE_DAMP)
    shard[...] = new
    for ring in range(RINGS):
        copies[ring] = new


def out_rows_kernel(scal, part_band, from_left, rows_out):
    rows = pl.ds(pl.multiple_of(scal[MODE] // 2 * 8, 8), OUT_ROWS)
    rows_out[:, :, :SIDE] = part_band[:, rows, :SIDE] + from_left[:, rows, :]
    rows_out[:, :, SIDE:] = part_band[:, rows, SIDE:WIDTH]


def pair_kernel(mine, theirs, pair):
    pair[0] = mine[...]
    pair[1] = theirs[...]


def object_kernel(scal, own, plus, minus, across, object_out):
    xhi, y = scal[MODE] // 4, lax.rem(scal[MODE], 4)
    for source, steps in ((own, 0), (plus, 3), (minus, 1), (across, 2)):
        for beyond in range(2):
            half = xhi if beyond == 0 else 1 - xhi
            place = half * 4 + lax.rem(y + steps, 4)
            rows = pl.ds(pl.multiple_of(place * 9 // 2 * 8, 8), OUT_ROWS)
            object_out[:, rows, :] = source[beyond]


def probe_out_kernel(pieces, probe_out):
    for xlo in range(2):
        for core in range(2):
            for place in range(MODES):
                row = place * SLAB + core * 16 + xlo * 8
                probe_out[0, :, row : row + 8, :LANES] = pieces[xlo, core, 2 * place]
                probe_out[0, :, row : row + 8, LANES:] = pieces[xlo, core, 2 * place + 1]


def own_kernel(place, whole, own, left, sems):
    rows = pl.ds(pl.multiple_of(place[0] * SLAB, SLAB), BAND)
    first = pltpu.make_async_copy(whole.at[:, rows, :], own, sems.at[0])
    second = pltpu.make_async_copy(whole.at[:, rows, pl.ds(0, SIDE)], left, sems.at[1])
    first.start()
    second.start()
    first.wait()
    second.wait()


def take_own(mode, object_tiles, after):
    vmem = pl.BlockSpec(memory_space=pltpu.VMEM)
    anywhere = pl.BlockSpec(memory_space=pl.ANY)

    def body(place, whole, _, own, left, sems):
        own_kernel(place, whole, own, left, sems)

    return pl.pallas_call(
        body,
        out_shape=[
            jax.ShapeDtypeStruct((2, BAND, WIDTH), F32),
            jax.ShapeDtypeStruct((2, BAND, SIDE), F32),
        ],
        in_specs=[pl.BlockSpec(memory_space=pltpu.SMEM), anywhere, anywhere],
        out_specs=[vmem, vmem],
        scratch_shapes=[pltpu.SemaphoreType.DMA((2,))],
        compiler_params=pltpu.CompilerParams(vmem_limit_bytes=VMEM_LIMIT),
        name="own_kernel",
    )(mode.astype(jnp.int32).reshape(1), object_tiles, after)


def call(kernel, outs, *args, scalars=True, after=()):
    vmem = pl.BlockSpec(memory_space=pltpu.VMEM)
    in_specs = [vmem] * len(args) + [pl.BlockSpec(memory_space=pl.ANY)] * len(after)
    if scalars:
        in_specs[0] = pl.BlockSpec(memory_space=pltpu.SMEM)

    def body(*refs):
        kernel(*refs[: len(args)], *refs[len(args) + len(after) :])

    return pl.pallas_call(
        body,
        out_shape=[jax.ShapeDtypeStruct(shape, F32) for shape in outs],
        in_specs=in_specs,
        out_specs=[vmem] * len(outs),
        compiler_params=pltpu.CompilerParams(vmem_limit_bytes=VMEM_LIMIT),
        name=kernel.__name__,
    )(*args, *after)


def shift(value, axes, count, steps):
    first, last = max(0, -steps), min(count, count - steps)
    return lax.ppermute(value, axes, [(i, i + steps) for i in range(first, last)])


def other(value, axis):
    return lax.ppermute(value, axis, [(0, 1), (1, 0)])


def exchange(value, axes):
    return lax.all_to_all(value, axes, 0, 0, tiled=True)


def gather_pieces(piece):
    return lax.all_gather(piece, ("xlo", "core")).reshape(2, 2, RINGS, 2, 8, LANES)


def around(value, steps):
    return lax.ppermute(value, "y", [(i, (i + steps) % 4) for i in range(4)])


def per_device(
    object_tiles, probe_modes, measured, row_offset, col_offset, live_counts, visit_order
):
    tables = jnp.asarray(fourier_tables())
    slots = visit_order[0]
    tile = lax.axis_index(TILE_AXES)
    mode = lax.axis_index(MODE_AXES)
    pieces = probe_modes.reshape(2, MODES, SLAB, SIDE).transpose(1, 0, 2, 3)
    probe = exchange(pieces, MODE_AXES)
    own, left = take_own(mode, object_tiles, pieces)
    beside = shift(left, TILE_AXES, TILES, -1)
    places = [
        mode,
        lax.axis_index("core"),
        lax.axis_index("xlo"),
        lax.axis_index("z"),
        (tile < TILES - 1).astype(jnp.int32),
    ]
    chosen = slots[:, None] == jnp.arange(STEPS, dtype=jnp.int32)[None, :]
    per_step = [
        jnp.sum(jnp.where(chosen, row_offset, 0), axis=1),
        jnp.sum(jnp.where(chosen, col_offset, 0), axis=1),
        slots,
        (slots < live_counts[0]).astype(jnp.int32),
    ]
    scalars = jnp.stack(
        per_step + [jnp.broadcast_to(place, (STEPS,)) for place in places], axis=1
    )
    slabs = (MODES, 2, SLAB, SIDE)
    slab_pair = (2, SLAB, SIDE)
    band_shape = (2, BAND, WIDE)
    edge = (2, BAND, SIDE)
    (counts,) = call(counts_kernel, [(SIDE, LANES)], scalars[0], measured)
    for step in range(STEPS):
        scal = scalars[step]
        final = step == STEPS - 1
        if step == 0:
            band, view, shard, spectra = call(
                first_kernel,
                [band_shape, slab_pair, (2, 8, LANES), slabs],
                scal,
                own,
                beside,
                probe,
                tables,
                after=(counts,),
            )
        else:
            band, view = call(
                view_kernel, [band_shape, slab_pair], scal, part_band, from_left, from_right
            )
            probe, spectra = call(
                next_kernel,
                [slabs, slabs],
                view,
                pieces,
                tables,
                scalars=False,
                after=(counts,),
            )
        spectra = exchange(spectra, MODE_AXES)
        (spectra,) = call(ratio_kernel, [slabs], scal, spectra, counts, tables)
        spectra = exchange(spectra, MODE_AXES)
        chi, keep, send = call(
            backward_kernel,
            [slabs] + [(2 * MODES + 1, 16, SIDE)] * 2,
            scal,
            spectra,
            view,
            tables,
        )
        received = other(send, "core")
        keep, send = call(halve_kernel, [(2 * MODES + 1, 8, SIDE)] * 2, scal, keep, received)
        received = other(send, "xlo")
        (object_step,) = call(
            step_kernel, [slab_pair], chi, probe, scalars=False, after=(keep,)
        )
        above = shift(object_step, MODE_AXES, MODES, 1)
        below = shift(object_step, MODE_AXES, MODES, -1)
        (packed,) = call(
            pack_kernel,
            [(RINGS, 3, 8, LANES)],
            keep,
            received,
            scalars=False,
            after=(above, below) if final else (object_step,),
        )
        sums = exchange(packed, "z")
        if not final:
            (counts,) = call(
                counts_kernel, [(SIDE, LANES)], scalars[step + 1], measured, after=(packed,)
            )
        placing = [scal, above, object_step, below, band]
        if final:
            part_band, _, to_right = call(
                place_kernel, [band_shape, edge, edge], *placing, after=(packed,)
            )
            from_left = shift(to_right, TILE_AXES, TILES, 1)
            (rows_out,) = call(
                out_rows_kernel, [(2, OUT_ROWS, WIDTH)], scal, part_band, from_left
            )
            far_rows = other(rows_out, "xhi")
        shard, shards = call(
            probe_kernel,
            [(2, 8, LANES), (RINGS, 2, 8, LANES)],
            sums,
            shard,
            scalars=False,
            after=(far_rows,) if final else (above, below, counts),
        )
        piece = exchange(shards, "z")
        if final:
            (pair,) = call(
                pair_kernel,
                [(2, 2, OUT_ROWS, WIDTH)],
                rows_out,
                far_rows,
                scalars=False,
                after=(shards,),
            )
            plus, minus = around(pair, 1), around(pair, -1)
            piece, plus, minus = lax.optimization_barrier((piece, plus, minus))
        else:
            part_band, to_left, to_right = call(
                place_kernel, [band_shape, edge, edge], *placing, after=(shards,)
            )
            from_left = shift(to_right, TILE_AXES, TILES, 1)
            from_right = shift(to_left, TILE_AXES, TILES, -1)
            piece, from_left, from_right = lax.optimization_barrier(
                (piece, from_left, from_right)
            )
            pieces = gather_pieces(piece)
    (object_out,) = call(
        object_kernel,
        [(2, HEIGHT, WIDTH)],
        scal,
        pair,
        plus,
        minus,
        around(pair, 2),
    )
    piece = exchange(piece.reshape(MODES, 4, 8, LANES), MODE_AXES)
    pieces = gather_pieces(piece.reshape(RINGS, 2, 8, LANES))
    (probe_out,) = call(probe_out_kernel, [(1, 2, SIDE, SIDE)], pieces, scalars=False)
    return object_out, probe_out


def solution(mesh):
    grid = Mesh(mesh.devices.reshape(2, 16, 2, 2, 4), TILE_AXES + MODE_AXES)
    return jax.shard_map(
        per_device,
        mesh=grid,
        in_specs=(
            P(None, None, TILE_AXES),
            P(MODE_AXES, None, None, None),
            P(TILE_AXES, None, None, None),
            P(TILE_AXES, None),
            P(TILE_AXES, None),
            P(TILE_AXES),
            P(TILE_AXES, None),
        ),
        out_specs=(P(None, None, TILE_AXES), P(MODE_AXES, None, None, None)),
        check_vma=False,
    )
```

```python
import math

import jax
import jax.numpy as jnp
import numpy as np
from jax import lax
from jax.experimental import pallas as pl
from jax.experimental.pallas import tpu as pltpu
from jax.sharding import Mesh
from jax.sharding import PartitionSpec as P

SOFT_FLOOR = 0.5
OBJECT_RATE = 1.0
OBJECT_DAMP = 0.5
PROBE_RATE = 1.0
PROBE_DAMP = 1.0

SIDE = 256
HEIGHT = 288
WIDTH = 512
WIDE = WIDTH + SIDE
MODES = 8
SLAB = SIDE // MODES
BAND = 2 * SLAB
STEPS = 3
TILES = 64
RINGS = 16
LANES = 128
COL_SPAN = SIDE + LANES
OUT_ROWS = 40
VMEM_LIMIT = 16 * 1024 * 1024

TILE_AXES = ("xlo", "z", "core")
MODE_AXES = ("xhi", "y")

ROW, COL, SLOT, LIVE, MODE, CORE, XLO, RING, HAS_NEXT, BAND_ID = range(10)

F32 = jnp.float32
BF16 = jnp.bfloat16


def slab_of(place):
    return place if place < MODES // 2 else 11 - place


def fourier_tables():
    index = np.arange(SIDE)
    angles = (index[:, None] * index[None, :] % SIDE) * (2.0 * math.pi / SIDE)
    both = np.stack([np.cos(angles), np.sin(angles)]) / math.sqrt(SIDE)
    high = both.astype(jnp.bfloat16)
    low = (both - high.astype(np.float64)).astype(jnp.bfloat16)
    return np.stack([high, low], axis=1)


def halves(value):
    high = value.astype(BF16)
    return high, (value - high.astype(F32)).astype(BF16)


def dot(left, right):
    return jnp.dot(left, right, preferred_element_type=F32)


def rows_transform(real, imag, tables, direction):
    high, low = halves(jnp.concatenate([real, imag], axis=0))

    def by(which):
        return (
            dot(high, tables[which, 0]) + dot(low, tables[which, 0]) + dot(high, tables[which, 1])
        )

    by_cos, by_sin = by(0), by(1)
    return (
        by_cos[:SIDE] + direction * by_sin[SIDE:],
        by_cos[SIDE:] - direction * by_sin[:SIDE],
    )


def columns_transform(real, imag, tables, direction):
    high, low = halves(jnp.concatenate([real, imag], axis=1))

    def by(which):
        return (
            dot(tables[which, 0], high) + dot(tables[which, 0], low) + dot(tables[which, 1], high)
        )

    by_cos, by_sin = by(0), by(1)
    return (
        by_cos[:, :SIDE] + direction * by_sin[:, SIDE:],
        by_cos[:, SIDE:] - direction * by_sin[:, :SIDE],
    )


def swap_blocks(parts):
    lanes = lax.broadcasted_iota(jnp.int32, (parts[0].shape[0], LANES), 1)
    grid = [[part[:, :LANES], part[:, LANES:]] for part in parts]
    grid = [[grid[(m & 3) | (h << 2)][m >> 2] for h in range(2)] for m in range(MODES)]
    for bit in (2, 1):
        shift = bit * SLAB
        low = (lanes & shift) == 0
        new = [None] * MODES
        for m in range(MODES):
            if m & bit:
                continue
            a, b = grid[m], grid[m | bit]
            new[m] = [jnp.where(low, a[h], pltpu.roll(b[h], shift, 1)) for h in range(2)]
            new[m | bit] = [
                jnp.where(low, pltpu.roll(a[h], LANES - shift, 1), b[h]) for h in range(2)
            ]
        grid = new
    return [jnp.concatenate(pair, axis=1) for pair in grid]


def stacked(pieces):
    return jnp.concatenate(list(pieces), axis=0)


def column_window(scal):
    col = scal[COL]
    block = jnp.minimum(col // LANES, WIDTH // LANES - 1)
    return pl.ds(pl.multiple_of(block * LANES, LANES), COL_SPAN), col - block * LANES


def take_patch(scal, band, view):
    cols, rest = column_window(scal)
    for part in range(2):
        block = band[part, :, cols]
        block = pltpu.roll(block, lax.rem(COL_SPAN - rest, COL_SPAN), 1)[:, :SIDE]
        view[part] = pltpu.roll(block, lax.rem(BAND - scal[ROW], BAND), 0)[:SLAB]


def forward(view, probe, tables, spectra):
    view_real = stacked([view[0]] * MODES)
    view_imag = stacked([view[1]] * MODES)
    probe_real = stacked(probe[mode, 0] for mode in range(MODES))
    probe_imag = stacked(probe[mode, 1] for mode in range(MODES))
    both = rows_transform(
        probe_real * view_real - probe_imag * view_imag,
        probe_real * view_imag + probe_imag * view_real,
        tables,
        1.0,
    )
    for part in range(2):
        blocks = [both[part][mode * SLAB : (mode + 1) * SLAB] for mode in range(MODES)]
        for place, block in enumerate(swap_blocks(blocks)):
            spectra[place, part] = block


def split_kernel(probe_in, pieces, sems):
    copies = []
    for place in range(MODES):
        rows = pl.ds(slab_of(place) * SLAB, SLAB)
        copies.append(
            pltpu.make_async_copy(probe_in.at[0, :, rows, :], pieces.at[place], sems.at[place])
        )
    for copy in copies:
        copy.start()
    for copy in copies:
        copy.wait()


def split_probe(probe_modes):
    anywhere = pl.BlockSpec(memory_space=pl.ANY)
    return pl.pallas_call(
        split_kernel,
        out_shape=jax.ShapeDtypeStruct((MODES, 2, SLAB, SIDE), F32),
        in_specs=[anywhere],
        out_specs=anywhere,
        scratch_shapes=[pltpu.SemaphoreType.DMA((MODES,))],
        name="split_kernel",
    )(probe_modes)


def first_kernel(scal, own, beside, probe, tables, band, view, shard, spectra):
    band[:, :, :WIDTH] = own[...]
    band[:, :, WIDTH:] = beside[...]
    take_patch(scal, band, view)
    mode = scal[RING] // 2
    rows = pl.ds(pl.multiple_of(scal[CORE] * 16 + scal[XLO] * 8, 8), 8)

    @pl.when(lax.rem(scal[RING], 2) == 0)
    def _():
        shard[...] = probe[mode, :, rows, :LANES]

    @pl.when(lax.rem(scal[RING], 2) == 1)
    def _():
        shard[...] = probe[mode, :, rows, LANES:]

    forward(view, probe, tables, spectra)


def next_kernel(view, pieces, tables, probe, spectra):
    for xlo in range(2):
        for core in range(2):
            row = core * 16 + xlo * 8
            for mode in range(MODES):
                probe[mode, :, row : row + 8, :LANES] = pieces[xlo, core, 2 * mode]
                probe[mode, :, row : row + 8, LANES:] = pieces[xlo, core, 2 * mode + 1]
    forward(view, probe, tables, spectra)


def counts_kernel(scal, measured, counts, flags):
    for place, which in enumerate((LIVE, CORE, XLO)):
        flags[place] = jnp.full((8, SIDE), scal[which].astype(F32))
    block = measured[0, scal[SLOT]].astype(F32)
    block = pltpu.roll(block, lax.rem(SIDE - scal[MODE] * SLAB, SIDE), 1)[:, :LANES]
    lanes = lax.broadcasted_iota(jnp.int32, block.shape, 1)
    block = jnp.where(lanes < SLAB, block, 0.0)
    block = block + pltpu.roll(block, SLAB, 1)
    counts[...] = block + pltpu.roll(block, 2 * SLAB, 1)


def ratio_kernel(spectra, counts, flags, tables, out):
    real = stacked(spectra[slab_of(index), 0] for index in range(MODES))
    imag = stacked(spectra[slab_of(index), 1] for index in range(MODES))
    far_real, far_imag = columns_transform(real, imag, tables, 1.0)
    power = far_real * far_real + far_imag * far_imag
    total = power[:, :LANES] + power[:, LANES:]
    total = total + pltpu.roll(total, 2 * SLAB, 1)
    total = total + pltpu.roll(total, SLAB, 1)
    ratio = jnp.sqrt((counts[...] + SOFT_FLOOR) / (total + SOFT_FLOOR)) - 1.0
    ratio = ratio * flags[0, 0:1, :LANES]
    ratio = jnp.concatenate([ratio, ratio], axis=1)
    both = columns_transform(far_real * ratio, far_imag * ratio, tables, -1.0)
    for part in range(2):
        for place in range(MODES):
            row = slab_of(place) * SLAB
            out[place, part] = both[part][row : row + SLAB]


def backward_kernel(spectra, view, flags, tables, chi, keep, send):
    real = stacked(swap_blocks([spectra[place, 0] for place in range(MODES)]))
    imag = stacked(swap_blocks([spectra[place, 1] for place in range(MODES)]))
    chi_real, chi_imag = rows_transform(real, imag, tables, -1.0)
    view_real, view_imag = view[0], view[1]
    sums = []
    for mode in range(MODES):
        real = chi_real[mode * SLAB : (mode + 1) * SLAB]
        imag = chi_imag[mode * SLAB : (mode + 1) * SLAB]
        chi[mode, 0] = real
        chi[mode, 1] = imag
        sums.append(view_real * real + view_imag * imag)
        sums.append(view_real * imag - view_imag * real)
    sums.append((view_real * view_real + view_imag * view_imag) * flags[0, 0:1, :])
    second = jnp.broadcast_to(flags[1, 0:1, :], (16, SIDE)) > 0.5
    for index, value in enumerate(sums):
        keep[index] = jnp.where(second, value[16:], value[:16])
        send[index] = jnp.where(second, value[:16], value[16:])


def halve_kernel(mine, theirs, flags, keep, send):
    second = jnp.broadcast_to(flags[2, 0:1, :], (8, SIDE)) > 0.5
    for index in range(2 * MODES + 1):
        value = mine[index] + theirs[index]
        keep[index] = jnp.where(second, value[8:], value[:8])
        send[index] = jnp.where(second, value[:8], value[8:])


def pack_kernel(mine, theirs, packed):
    for half in range(2):
        lanes = slice(half * LANES, (half + 1) * LANES)
        total = mine[:, :, lanes] + theirs[:, :, lanes]
        for mode in range(MODES):
            place = (2 * mode + half + RINGS // 2) % RINGS
            packed[place, 0] = total[2 * mode]
            packed[place, 1] = total[2 * mode + 1]
            packed[place, 2] = total[2 * MODES]


def step_kernel(chi, probe, step):
    real = imag = light = 0.0
    for mode in range(MODES):
        probe_real, probe_imag = probe[mode, 0], probe[mode, 1]
        real = real + (probe_real * chi[mode, 0] + probe_imag * chi[mode, 1])
        imag = imag + (probe_real * chi[mode, 1] - probe_imag * chi[mode, 0])
        light = light + (probe_real * probe_real + probe_imag * probe_imag)
    step[0] = OBJECT_RATE * real / (light + OBJECT_DAMP)
    step[1] = OBJECT_RATE * imag / (light + OBJECT_DAMP)


def place_kernel(scal, above, step, below, band, part_band, to_left, to_right):
    cols, rest = column_window(scal)
    height = 3 * SLAB
    part_band[...] = jnp.zeros_like(part_band)
    for part in range(2):
        block = stacked([above[part], step[part], below[part]])
        block = pltpu.roll(block, lax.rem(2 * SLAB + scal[ROW], height), 0)[:BAND]
        block = jnp.concatenate([block, jnp.zeros((BAND, LANES), F32)], axis=1)
        part_band[part, :, cols] = pltpu.roll(block, rest, 1)
    to_left[...] = part_band[:, :, :SIDE]
    to_right[...] = part_band[:, :, WIDTH:]
    part_band[:, :, :WIDTH] = part_band[:, :, :WIDTH] + band[:, :, :WIDTH]
    part_band[:, :, WIDTH:] = (
        part_band[:, :, WIDTH:] * scal[HAS_NEXT].astype(F32) + band[:, :, WIDTH:]
    )


def view_kernel(scal, part_band, from_left, from_right, band, view):
    band[:, :, :SIDE] = part_band[:, :, :SIDE] + from_left[...]
    band[:, :, SIDE:WIDTH] = part_band[:, :, SIDE:WIDTH]
    band[:, :, WIDTH:] = part_band[:, :, WIDTH:] + from_right[...]
    take_patch(scal, band, view)


def probe_kernel(sums, shard_in, shard, copies):
    total = sums[0]
    for ring in range(1, RINGS):
        total = total + sums[ring]
    new = shard_in[...] + PROBE_RATE * total[:2] / (total[2:] + PROBE_DAMP)
    shard[...] = new
    for ring in range(RINGS):
        copies[ring] = new


def out_rows_kernel(scal, part_band, from_left, rows_out):
    rows = pl.ds(pl.multiple_of(scal[BAND_ID] // 2 * 8, 8), OUT_ROWS)
    rows_out[:, :, :SIDE] = part_band[:, rows, :SIDE] + from_left[:, rows, :]
    rows_out[:, :, SIDE:] = part_band[:, rows, SIDE:WIDTH]


def pair_kernel(mine, theirs, pair):
    pair[0] = mine[...]
    pair[1] = theirs[...]


def object_kernel(scal, own, plus, minus, across, object_out):
    xhi, y = scal[MODE] // 4, lax.rem(scal[MODE], 4)
    for source, steps in ((own, 0), (plus, 3), (minus, 1), (across, 2)):
        for beyond in range(2):
            half = xhi if beyond == 0 else 1 - xhi
            column = lax.rem(y + steps, 4)
            slab = jnp.where(half == 0, column, 7 - column)
            rows = pl.ds(pl.multiple_of(slab * 9 // 2 * 8, 8), OUT_ROWS)
            object_out[:, rows, :] = source[beyond]


def probe_out_kernel(pieces, probe_out):
    for xlo in range(2):
        for core in range(2):
            for place in range(MODES):
                row = slab_of(place) * SLAB + core * 16 + xlo * 8
                probe_out[0, :, row : row + 8, :LANES] = pieces[xlo, core, 2 * place]
                probe_out[0, :, row : row + 8, LANES:] = pieces[xlo, core, 2 * place + 1]


def own_kernel(place, whole, own, left, sems):
    rows = pl.ds(pl.multiple_of(place[0] * SLAB, SLAB), BAND)
    first = pltpu.make_async_copy(whole.at[:, rows, :], own, sems.at[0])
    second = pltpu.make_async_copy(whole.at[:, rows, pl.ds(0, SIDE)], left, sems.at[1])
    first.start()
    second.start()
    first.wait()
    second.wait()


def take_own(mode, object_tiles, after):
    vmem = pl.BlockSpec(memory_space=pltpu.VMEM)
    anywhere = pl.BlockSpec(memory_space=pl.ANY)

    def body(place, whole, _, own, left, sems):
        own_kernel(place, whole, own, left, sems)

    return pl.pallas_call(
        body,
        out_shape=[
            jax.ShapeDtypeStruct((2, BAND, WIDTH), F32),
            jax.ShapeDtypeStruct((2, BAND, SIDE), F32),
        ],
        in_specs=[pl.BlockSpec(memory_space=pltpu.SMEM), anywhere, anywhere],
        out_specs=[vmem, vmem],
        scratch_shapes=[pltpu.SemaphoreType.DMA((2,))],
        compiler_params=pltpu.CompilerParams(vmem_limit_bytes=VMEM_LIMIT),
        name="own_kernel",
    )(mode.astype(jnp.int32).reshape(1), object_tiles, after)


def call(kernel, outs, *args, scalars=True, after=()):
    vmem = pl.BlockSpec(memory_space=pltpu.VMEM)
    in_specs = [vmem] * len(args) + [pl.BlockSpec(memory_space=pl.ANY)] * len(after)
    if scalars:
        in_specs[0] = pl.BlockSpec(memory_space=pltpu.SMEM)

    def body(*refs):
        kernel(*refs[: len(args)], *refs[len(args) + len(after) :])

    return pl.pallas_call(
        body,
        out_shape=[jax.ShapeDtypeStruct(shape, F32) for shape in outs],
        in_specs=in_specs,
        out_specs=[vmem] * len(outs),
        compiler_params=pltpu.CompilerParams(vmem_limit_bytes=VMEM_LIMIT),
        name=kernel.__name__,
    )(*args, *after)


def shift(value, axes, count, steps):
    first, last = max(0, -steps), min(count, count - steps)
    return lax.ppermute(value, axes, [(i, i + steps) for i in range(first, last)])


def other(value, axis):
    return lax.ppermute(value, axis, [(0, 1), (1, 0)])


def beside_slab(value, steps):
    first, last = max(0, -steps), min(MODES, MODES - steps)
    pairs = [(slab_of(i), slab_of(i + steps)) for i in range(first, last)]
    return lax.ppermute(value, MODE_AXES, pairs)


def exchange_far_first(value):
    order = [(i + RINGS // 2) % RINGS for i in range(RINGS)]
    return lax.all_to_all(value, "z", 0, 0, tiled=True, axis_index_groups=[order])


def exchange(value, axes):
    return lax.all_to_all(value, axes, 0, 0, tiled=True)


def gather_pieces(piece):
    return lax.all_gather(piece, ("xlo", "core")).reshape(2, 2, RINGS, 2, 8, LANES)


def around(value, steps):
    return lax.ppermute(value, "y", [(i, (i + steps) % 4) for i in range(4)])


def per_device(
    object_tiles, probe_modes, measured, row_offset, col_offset, live_counts, visit_order
):
    tables = jnp.asarray(fourier_tables())
    slots = visit_order[0]
    tile = lax.axis_index(TILE_AXES)
    mode = lax.axis_index(MODE_AXES)
    slab = jnp.where(mode < MODES // 2, mode, 11 - mode)
    pieces = split_probe(probe_modes)
    probe = exchange(pieces, MODE_AXES)
    own, left = take_own(slab, object_tiles, pieces)
    beside = shift(left, TILE_AXES, TILES, -1)
    places = [
        mode,
        lax.axis_index("core"),
        lax.axis_index("xlo"),
        lax.axis_index("z"),
        (tile < TILES - 1).astype(jnp.int32),
        slab,
    ]
    chosen = slots[:, None] == jnp.arange(STEPS, dtype=jnp.int32)[None, :]
    per_step = [
        jnp.sum(jnp.where(chosen, row_offset, 0), axis=1),
        jnp.sum(jnp.where(chosen, col_offset, 0), axis=1),
        slots,
        (slots < live_counts[0]).astype(jnp.int32),
    ]
    scalars = jnp.stack(
        per_step + [jnp.broadcast_to(place, (STEPS,)) for place in places], axis=1
    )
    slabs = (MODES, 2, SLAB, SIDE)
    slab_pair = (2, SLAB, SIDE)
    band_shape = (2, BAND, WIDE)
    edge = (2, BAND, SIDE)
    counts_shapes = [(SIDE, LANES), (3, 8, SIDE)]
    counts, flags = call(counts_kernel, counts_shapes, scalars[0], measured)
    for step in range(STEPS):
        scal = scalars[step]
        final = step == STEPS - 1
        if step == 0:
            band, view, shard, spectra = call(
                first_kernel,
                [band_shape, slab_pair, (2, 8, LANES), slabs],
                scal,
                own,
                beside,
                probe,
                tables,
                after=(counts,),
            )
        else:
            probe, spectra = call(
                next_kernel,
                [slabs, slabs],
                view,
                pieces,
                tables,
                scalars=False,
                after=(counts,),
            )
        spectra = exchange(spectra, MODE_AXES)
        (spectra,) = call(
            ratio_kernel, [slabs], spectra, counts, flags, tables, scalars=False
        )
        spectra = exchange(spectra, MODE_AXES)
        chi, keep, send = call(
            backward_kernel,
            [slabs] + [(2 * MODES + 1, 16, SIDE)] * 2,
            spectra,
            view,
            flags,
            tables,
            scalars=False,
        )
        received = other(send, "core")
        keep, send = call(
            halve_kernel, [(2 * MODES + 1, 8, SIDE)] * 2, keep, received, flags, scalars=False
        )
        received = other(send, "xlo")
        (object_step,) = call(
            step_kernel, [slab_pair], chi, probe, scalars=False, after=(keep,)
        )
        above = beside_slab(object_step, 1)
        below = beside_slab(object_step, -1)
        (packed,) = call(
            pack_kernel,
            [(RINGS, 3, 8, LANES)],
            keep,
            received,
            scalars=False,
            after=(above, below) if final else (object_step,),
        )
        sums = exchange_far_first(packed)
        if not final:
            counts, flags = call(
                counts_kernel, counts_shapes, scalars[step + 1], measured, after=(packed,)
            )
        placing = [scal, above, object_step, below, band]
        if final:
            part_band, _, to_right = call(
                place_kernel, [band_shape, edge, edge], *placing, after=(packed,)
            )
            from_left = shift(to_right, TILE_AXES, TILES, 1)
            (rows_out,) = call(
                out_rows_kernel, [(2, OUT_ROWS, WIDTH)], scal, part_band, from_left
            )
            far_rows = other(rows_out, "xhi")
        shard, shards = call(
            probe_kernel,
            [(2, 8, LANES), (RINGS, 2, 8, LANES)],
            sums,
            shard,
            scalars=False,
            after=(rows_out,) if final else (above, below, counts),
        )
        piece = exchange(shards, "z")
        if final:
            piece, far_rows = lax.optimization_barrier((piece, far_rows))
        else:
            part_band, to_left, to_right = call(
                place_kernel, [band_shape, edge, edge], *placing, after=(shards,)
            )
            from_left = shift(to_right, TILE_AXES, TILES, 1)
            from_right = shift(to_left, TILE_AXES, TILES, -1)
            band, view = call(
                view_kernel,
                [band_shape, slab_pair],
                scalars[step + 1],
                part_band,
                from_left,
                from_right,
            )
            piece, view = lax.optimization_barrier((piece, view))
            pieces = gather_pieces(piece)
    (pair,) = call(
        pair_kernel,
        [(2, 2, OUT_ROWS, WIDTH)],
        rows_out,
        far_rows,
        scalars=False,
        after=(piece,),
    )
    (object_out,) = call(
        object_kernel,
        [(2, HEIGHT, WIDTH)],
        scal,
        pair,
        around(pair, 1),
        around(pair, -1),
        around(pair, 2),
    )
    piece = exchange(piece.reshape(MODES, 4, 8, LANES), MODE_AXES)
    pieces = gather_pieces(piece.reshape(RINGS, 2, 8, LANES))
    (probe_out,) = call(probe_out_kernel, [(1, 2, SIDE, SIDE)], pieces, scalars=False)
    return object_out, probe_out


def solution(mesh):
    grid = Mesh(mesh.devices.reshape(2, 16, 2, 2, 4), TILE_AXES + MODE_AXES)
    return jax.shard_map(
        per_device,
        mesh=grid,
        in_specs=(
            P(None, None, TILE_AXES),
            P(MODE_AXES, None, None, None),
            P(TILE_AXES, None, None, None),
            P(TILE_AXES, None),
            P(TILE_AXES, None),
            P(TILE_AXES),
            P(TILE_AXES, None),
        ),
        out_specs=(P(None, None, TILE_AXES), P(MODE_AXES, None, None, None)),
        check_vma=False,
    )
```

```python
import math

import jax
import jax.numpy as jnp
import numpy as np
from jax import lax
from jax.experimental import pallas as pl
from jax.experimental.pallas import tpu as pltpu
from jax.sharding import Mesh
from jax.sharding import PartitionSpec as P

SOFT_FLOOR = 0.5
OBJECT_RATE = 1.0
OBJECT_DAMP = 0.5
PROBE_RATE = 1.0
PROBE_DAMP = 1.0

SIDE = 256
HEIGHT = 288
WIDTH = 512
WIDE = WIDTH + SIDE
MODES = 8
SLAB = SIDE // MODES
BAND = 2 * SLAB
STEPS = 3
TILES = 64
RINGS = 16
LANES = 128
COL_SPAN = SIDE + LANES
OUT_ROWS = 40
VMEM_LIMIT = 16 * 1024 * 1024

TILE_AXES = ("xlo", "z", "core")
MODE_AXES = ("xhi", "y")

ROW, COL, SLOT, LIVE, MODE, CORE, XLO, RING, HAS_NEXT, BAND_ID = range(10)

F32 = jnp.float32
BF16 = jnp.bfloat16


def slab_of(place):
    return place if place < MODES // 2 else 11 - place


def fourier_tables():
    index = np.arange(SIDE)
    angles = (index[:, None] * index[None, :] % SIDE) * (2.0 * math.pi / SIDE)
    both = np.stack([np.cos(angles), np.sin(angles)]) / math.sqrt(SIDE)
    high = both.astype(jnp.bfloat16)
    low = (both - high.astype(np.float64)).astype(jnp.bfloat16)
    return np.stack([high, low], axis=1)


def halves(value):
    high = value.astype(BF16)
    return high, (value - high.astype(F32)).astype(BF16)


def dot(left, right):
    return jnp.dot(left, right, preferred_element_type=F32)


def rows_transform(real, imag, tables, direction):
    high, low = halves(jnp.concatenate([real, imag], axis=0))

    def by(which):
        return (
            dot(high, tables[which, 0]) + dot(low, tables[which, 0]) + dot(high, tables[which, 1])
        )

    by_cos, by_sin = by(0), by(1)
    return (
        by_cos[:SIDE] + direction * by_sin[SIDE:],
        by_cos[SIDE:] - direction * by_sin[:SIDE],
    )


def columns_transform(real, imag, tables, direction):
    high, low = halves(jnp.concatenate([real, imag], axis=1))

    def by(which):
        return (
            dot(tables[which, 0], high) + dot(tables[which, 0], low) + dot(tables[which, 1], high)
        )

    by_cos, by_sin = by(0), by(1)
    return (
        by_cos[:, :SIDE] + direction * by_sin[:, SIDE:],
        by_cos[:, SIDE:] - direction * by_sin[:, :SIDE],
    )


def swap_blocks(parts):
    lanes = lax.broadcasted_iota(jnp.int32, (parts[0].shape[0], LANES), 1)
    grid = [[part[:, :LANES], part[:, LANES:]] for part in parts]
    grid = [[grid[(m & 3) | (h << 2)][m >> 2] for h in range(2)] for m in range(MODES)]
    for bit in (2, 1):
        shift = bit * SLAB
        low = (lanes & shift) == 0
        new = [None] * MODES
        for m in range(MODES):
            if m & bit:
                continue
            a, b = grid[m], grid[m | bit]
            new[m] = [jnp.where(low, a[h], pltpu.roll(b[h], shift, 1)) for h in range(2)]
            new[m | bit] = [
                jnp.where(low, pltpu.roll(a[h], LANES - shift, 1), b[h]) for h in range(2)
            ]
        grid = new
    return [jnp.concatenate(pair, axis=1) for pair in grid]


def stacked(pieces):
    return jnp.concatenate(list(pieces), axis=0)


def column_window(scal):
    col = scal[COL]
    block = jnp.minimum(col // LANES, WIDTH // LANES - 1)
    return pl.ds(pl.multiple_of(block * LANES, LANES), COL_SPAN), col - block * LANES


def take_patch(scal, band, view):
    cols, rest = column_window(scal)
    for part in range(2):
        block = band[part, :, cols]
        block = pltpu.roll(block, lax.rem(COL_SPAN - rest, COL_SPAN), 1)[:, :SIDE]
        view[part] = pltpu.roll(block, lax.rem(BAND - scal[ROW], BAND), 0)[:SLAB]


def forward(view, probe, tables, spectra):
    view_real = stacked([view[0]] * MODES)
    view_imag = stacked([view[1]] * MODES)
    probe_real = stacked(probe[mode, 0] for mode in range(MODES))
    probe_imag = stacked(probe[mode, 1] for mode in range(MODES))
    both = rows_transform(
        probe_real * view_real - probe_imag * view_imag,
        probe_real * view_imag + probe_imag * view_real,
        tables,
        1.0,
    )
    for part in range(2):
        blocks = [both[part][mode * SLAB : (mode + 1) * SLAB] for mode in range(MODES)]
        for place, block in enumerate(swap_blocks(blocks)):
            spectra[place, part] = block


def split_kernel(probe_in, pieces):
    for place in range(MODES):
        row = slab_of(place) * SLAB
        pieces[place] = probe_in[0, :, row : row + SLAB, :]


def first_kernel(scal, own, beside, probe, tables, band, view, shard, spectra):
    band[:, :, :WIDTH] = own[...]
    band[:, :, WIDTH:] = beside[...]
    take_patch(scal, band, view)
    mode = scal[RING] // 2
    rows = pl.ds(pl.multiple_of(scal[CORE] * 16 + scal[XLO] * 8, 8), 8)

    @pl.when(lax.rem(scal[RING], 2) == 0)
    def _():
        shard[...] = probe[mode, :, rows, :LANES]

    @pl.when(lax.rem(scal[RING], 2) == 1)
    def _():
        shard[...] = probe[mode, :, rows, LANES:]

    forward(view, probe, tables, spectra)


def far_place(ring):
    return (ring + RINGS // 2) % RINGS


def next_kernel(view, pieces, tables, probe, spectra):
    for xlo in range(2):
        for core in range(2):
            row = core * 16 + xlo * 8
            for mode in range(MODES):
                for half in range(2):
                    lanes = slice(half * LANES, (half + 1) * LANES)
                    piece = pieces[xlo, core, 2 * mode + half]
                    probe[mode, :, row : row + 8, lanes] = piece
    forward(view, probe, tables, spectra)


def counts_kernel(scal, measured, counts, flags):
    for place, which in enumerate((LIVE, CORE, XLO)):
        flags[place] = jnp.full((8, SIDE), scal[which].astype(F32))
    block = measured[0, scal[SLOT]].astype(F32)
    block = pltpu.roll(block, lax.rem(SIDE - scal[MODE] * SLAB, SIDE), 1)[:, :LANES]
    lanes = lax.broadcasted_iota(jnp.int32, block.shape, 1)
    block = jnp.where(lanes < SLAB, block, 0.0)
    block = block + pltpu.roll(block, SLAB, 1)
    counts[...] = block + pltpu.roll(block, 2 * SLAB, 1)


def ratio_kernel(spectra, counts, flags, tables, out):
    real = stacked(spectra[slab_of(index), 0] for index in range(MODES))
    imag = stacked(spectra[slab_of(index), 1] for index in range(MODES))
    far_real, far_imag = columns_transform(real, imag, tables, 1.0)
    power = far_real * far_real + far_imag * far_imag
    total = power[:, :LANES] + power[:, LANES:]
    total = total + pltpu.roll(total, 2 * SLAB, 1)
    total = total + pltpu.roll(total, SLAB, 1)
    ratio = jnp.sqrt((counts[...] + SOFT_FLOOR) / (total + SOFT_FLOOR)) - 1.0
    ratio = ratio * flags[0, 0:1, :LANES]
    ratio = jnp.concatenate([ratio, ratio], axis=1)
    both = columns_transform(far_real * ratio, far_imag * ratio, tables, -1.0)
    for part in range(2):
        for place in range(MODES):
            row = slab_of(place) * SLAB
            out[place, part] = both[part][row : row + SLAB]


def backward_kernel(spectra, view, flags, tables, chi, keep, send):
    real = stacked(swap_blocks([spectra[place, 0] for place in range(MODES)]))
    imag = stacked(swap_blocks([spectra[place, 1] for place in range(MODES)]))
    chi_real, chi_imag = rows_transform(real, imag, tables, -1.0)
    view_real, view_imag = view[0], view[1]
    sums = []
    for mode in range(MODES):
        real = chi_real[mode * SLAB : (mode + 1) * SLAB]
        imag = chi_imag[mode * SLAB : (mode + 1) * SLAB]
        chi[mode, 0] = real
        chi[mode, 1] = imag
        sums.append(view_real * real + view_imag * imag)
        sums.append(view_real * imag - view_imag * real)
    sums.append((view_real * view_real + view_imag * view_imag) * flags[0, 0:1, :])
    second = jnp.broadcast_to(flags[1, 0:1, :], (16, SIDE)) > 0.5
    for index, value in enumerate(sums):
        keep[index] = jnp.where(second, value[16:], value[:16])
        send[index] = jnp.where(second, value[:16], value[16:])


def halve_kernel(mine, theirs, flags, keep, send):
    second = jnp.broadcast_to(flags[2, 0:1, :], (8, SIDE)) > 0.5
    for index in range(2 * MODES + 1):
        value = mine[index] + theirs[index]
        keep[index] = jnp.where(second, value[8:], value[:8])
        send[index] = jnp.where(second, value[:8], value[8:])


def pack_kernel(mine, theirs, packed):
    for half in range(2):
        lanes = slice(half * LANES, (half + 1) * LANES)
        total = mine[:, :, lanes] + theirs[:, :, lanes]
        for mode in range(MODES):
            place = far_place(2 * mode + half)
            packed[place, 0] = total[2 * mode]
            packed[place, 1] = total[2 * mode + 1]
            packed[place, 2] = total[2 * MODES]


def step_kernel(chi, probe, step):
    real = imag = light = 0.0
    for mode in range(MODES):
        probe_real, probe_imag = probe[mode, 0], probe[mode, 1]
        real = real + (probe_real * chi[mode, 0] + probe_imag * chi[mode, 1])
        imag = imag + (probe_real * chi[mode, 1] - probe_imag * chi[mode, 0])
        light = light + (probe_real * probe_real + probe_imag * probe_imag)
    step[0] = OBJECT_RATE * real / (light + OBJECT_DAMP)
    step[1] = OBJECT_RATE * imag / (light + OBJECT_DAMP)


def place_kernel(scal, above, step, below, band, part_band, to_left, to_right):
    cols, rest = column_window(scal)
    height = 3 * SLAB
    part_band[...] = jnp.zeros_like(part_band)
    for part in range(2):
        block = stacked([above[part], step[part], below[part]])
        block = pltpu.roll(block, lax.rem(2 * SLAB + scal[ROW], height), 0)[:BAND]
        block = jnp.concatenate([block, jnp.zeros((BAND, LANES), F32)], axis=1)
        part_band[part, :, cols] = pltpu.roll(block, rest, 1)
    to_left[...] = part_band[:, :, :SIDE]
    to_right[...] = part_band[:, :, WIDTH:]
    part_band[:, :, :WIDTH] = part_band[:, :, :WIDTH] + band[:, :, :WIDTH]
    part_band[:, :, WIDTH:] = (
        part_band[:, :, WIDTH:] * scal[HAS_NEXT].astype(F32) + band[:, :, WIDTH:]
    )


def view_kernel(scal, part_band, from_left, from_right, band, view):
    band[:, :, :SIDE] = part_band[:, :, :SIDE] + from_left[...]
    band[:, :, SIDE:WIDTH] = part_band[:, :, SIDE:WIDTH]
    band[:, :, WIDTH:] = part_band[:, :, WIDTH:] + from_right[...]
    take_patch(scal, band, view)


def probe_kernel(sums, shard_in, shard, copies):
    total = sums[0]
    for ring in range(1, RINGS):
        total = total + sums[ring]
    new = shard_in[...] + PROBE_RATE * total[:2] / (total[2:] + PROBE_DAMP)
    shard[...] = new
    for ring in range(RINGS):
        copies[ring] = new


def out_rows_kernel(scal, part_band, from_left, rows_out):
    rows = pl.ds(pl.multiple_of(scal[BAND_ID] // 2 * 8, 8), OUT_ROWS)
    rows_out[:, :, :SIDE] = part_band[:, rows, :SIDE] + from_left[:, rows, :]
    rows_out[:, :, SIDE:] = part_band[:, rows, SIDE:WIDTH]


def tail_kernel(piece, rows_out, tail):
    for place in range(MODES):
        for half in range(2):
            for part in range(2):
                row = (half * 2 + part) * 8
                tail[place, row : row + 8] = piece[2 * place + half, part]
        for part in range(2):
            for block in range(WIDTH // LANES):
                row = 32 + (part * 4 + block) * OUT_ROWS
                lanes = slice(block * LANES, (block + 1) * LANES)
                tail[place, row : row + OUT_ROWS] = rows_out[part, :, lanes]


def object_kernel(tail, object_out):
    for place in range(MODES):
        first = slab_of(place) * 9 // 2 * 8
        for part in range(2):
            for block in range(WIDTH // LANES):
                row = 32 + (part * 4 + block) * OUT_ROWS
                lanes = slice(block * LANES, (block + 1) * LANES)
                object_out[part, first : first + OUT_ROWS, lanes] = tail[
                    place, row : row + OUT_ROWS
                ]


def probe_out_kernel(pieces, probe_out):
    for xlo in range(2):
        for core in range(2):
            for place in range(MODES):
                first = slab_of(place) * SLAB + core * 16 + xlo * 8
                for half in range(2):
                    lanes = slice(half * LANES, (half + 1) * LANES)
                    for part in range(2):
                        row = (half * 2 + part) * 8
                        probe_out[0, part, first : first + 8, lanes] = pieces[
                            xlo, core, place, row : row + 8
                        ]


def own_kernel(place, whole, own, left, sems):
    rows = pl.ds(pl.multiple_of(place[0] * SLAB, SLAB), BAND)
    first = pltpu.make_async_copy(whole.at[:, rows, :], own, sems.at[0])
    second = pltpu.make_async_copy(whole.at[:, rows, pl.ds(0, SIDE)], left, sems.at[1])
    first.start()
    second.start()
    first.wait()
    second.wait()


def take_own(mode, object_tiles, after):
    vmem = pl.BlockSpec(memory_space=pltpu.VMEM)
    anywhere = pl.BlockSpec(memory_space=pl.ANY)

    def body(place, whole, _, own, left, sems):
        own_kernel(place, whole, own, left, sems)

    return pl.pallas_call(
        body,
        out_shape=[
            jax.ShapeDtypeStruct((2, BAND, WIDTH), F32),
            jax.ShapeDtypeStruct((2, BAND, SIDE), F32),
        ],
        in_specs=[pl.BlockSpec(memory_space=pltpu.SMEM), anywhere, anywhere],
        out_specs=[vmem, vmem],
        scratch_shapes=[pltpu.SemaphoreType.DMA((2,))],
        compiler_params=pltpu.CompilerParams(vmem_limit_bytes=VMEM_LIMIT),
        name="own_kernel",
    )(mode.astype(jnp.int32).reshape(1), object_tiles, after)


def call(kernel, outs, *args, scalars=True, after=()):
    vmem = pl.BlockSpec(memory_space=pltpu.VMEM)
    in_specs = [vmem] * len(args) + [pl.BlockSpec(memory_space=pl.ANY)] * len(after)

    def body(*refs):
        taken = list(refs[: len(args)])
        if scalars:
            taken[0] = [taken[0][0, index] for index in range(BAND_ID + 1)]
        kernel(*taken, *refs[len(args) + len(after) :])

    return pl.pallas_call(
        body,
        out_shape=[jax.ShapeDtypeStruct(shape, F32) for shape in outs],
        in_specs=in_specs,
        out_specs=[vmem] * len(outs),
        compiler_params=pltpu.CompilerParams(vmem_limit_bytes=VMEM_LIMIT),
        name=kernel.__name__,
    )(*args, *after)


def shift(value, axes, count, steps):
    first, last = max(0, -steps), min(count, count - steps)
    return lax.ppermute(value, axes, [(i, i + steps) for i in range(first, last)])


def other(value, axis):
    return lax.ppermute(value, axis, [(0, 1), (1, 0)])


def beside_slab(value, steps):
    first, last = max(0, -steps), min(MODES, MODES - steps)
    pairs = [(slab_of(i), slab_of(i + steps)) for i in range(first, last)]
    return lax.ppermute(value, MODE_AXES, pairs)


def exchange_rings(value):
    groups = [[far_place(ring) for ring in range(RINGS)]]
    return lax.all_to_all(value, "z", 0, 0, tiled=True, axis_index_groups=groups)


def exchange(value, axes):
    return lax.all_to_all(value, axes, 0, 0, tiled=True)


def gather_pieces(piece):
    gathered = lax.all_gather(piece, ("xlo", "core"))
    return gathered.reshape((2, 2) + piece.shape)


def per_device(
    object_tiles, probe_modes, measured, row_offset, col_offset, live_counts, visit_order
):
    tables = jnp.asarray(fourier_tables())
    slots = visit_order[0]
    tile = lax.axis_index(TILE_AXES)
    mode = lax.axis_index(MODE_AXES)
    slab = jnp.where(mode < MODES // 2, mode, 11 - mode)
    (pieces,) = call(split_kernel, [(MODES, 2, SLAB, SIDE)], probe_modes, scalars=False)
    probe = exchange(pieces, MODE_AXES)
    own, left = take_own(slab, object_tiles, pieces)
    beside = shift(left, TILE_AXES, TILES, -1)
    places = [
        mode,
        lax.axis_index("core"),
        lax.axis_index("xlo"),
        lax.axis_index("z"),
        (tile < TILES - 1).astype(jnp.int32),
        slab,
    ]
    chosen = slots[:, None] == jnp.arange(STEPS, dtype=jnp.int32)[None, :]
    per_step = [
        jnp.sum(jnp.where(chosen, row_offset, 0), axis=1),
        jnp.sum(jnp.where(chosen, col_offset, 0), axis=1),
        slots,
        (slots < live_counts[0]).astype(jnp.int32),
    ]
    scalars = jnp.stack(
        per_step + [jnp.broadcast_to(place, (STEPS,)) for place in places], axis=1
    )
    slabs = (MODES, 2, SLAB, SIDE)
    slab_pair = (2, SLAB, SIDE)
    band_shape = (2, BAND, WIDE)
    edge = (2, BAND, SIDE)
    counts_shapes = [(SIDE, LANES), (3, 8, SIDE)]
    counts, flags = call(counts_kernel, counts_shapes, scalars[:1], measured)
    for step in range(STEPS):
        scal = scalars[step : step + 1]
        final = step == STEPS - 1
        if step == 0:
            band, view, shard, spectra = call(
                first_kernel,
                [band_shape, slab_pair, (2, 8, LANES), slabs],
                scal,
                own,
                beside,
                probe,
                tables,
                after=(counts,),
            )
        else:
            probe, spectra = call(
                next_kernel,
                [slabs, slabs],
                view,
                pieces,
                tables,
                scalars=False,
                after=(counts,),
            )
        spectra = exchange(spectra, MODE_AXES)
        (spectra,) = call(
            ratio_kernel, [slabs], spectra, counts, flags, tables, scalars=False
        )
        spectra = exchange(spectra, MODE_AXES)
        chi, keep, send = call(
            backward_kernel,
            [slabs] + [(2 * MODES + 1, 16, SIDE)] * 2,
            spectra,
            view,
            flags,
            tables,
            scalars=False,
        )
        received = other(send, "core")
        keep, send = call(
            halve_kernel, [(2 * MODES + 1, 8, SIDE)] * 2, keep, received, flags, scalars=False
        )
        received = other(send, "xlo")
        (object_step,) = call(
            step_kernel, [slab_pair], chi, probe, scalars=False, after=(keep,)
        )
        above = beside_slab(object_step, 1)
        below = beside_slab(object_step, -1)
        (packed,) = call(
            pack_kernel,
            [(RINGS, 3, 8, LANES)],
            keep,
            received,
            scalars=False,
            after=(above, below),
        )
        sums = exchange_rings(packed)
        part_band, to_left, to_right = call(
            place_kernel,
            [band_shape, edge, edge],
            scal,
            above,
            object_step,
            below,
            band,
            after=(packed,),
        )
        from_left = shift(to_right, TILE_AXES, TILES, 1)
        if final:
            (rows_out,) = call(
                out_rows_kernel, [(2, OUT_ROWS, WIDTH)], scal, part_band, from_left
            )
            before = (rows_out,)
        else:
            from_right = shift(to_left, TILE_AXES, TILES, -1)
            next_scal = scalars[step + 1 : step + 2]
            counts, flags = call(
                counts_kernel, counts_shapes, next_scal, measured, after=(packed,)
            )
            band, view = call(
                view_kernel,
                [band_shape, slab_pair],
                next_scal,
                part_band,
                from_left,
                from_right,
            )
            before = (view, counts)
        shard, shards = call(
            probe_kernel,
            [(2, 8, LANES), (RINGS, 2, 8, LANES)],
            sums,
            shard,
            scalars=False,
            after=before,
        )
        piece = exchange(shards, "z")
        if not final:
            pieces = gather_pieces(piece)
    tail_rows = 32 + 8 * OUT_ROWS
    (tail,) = call(
        tail_kernel, [(MODES, tail_rows, LANES)], piece, rows_out, scalars=False
    )
    tail = exchange(tail, MODE_AXES)
    pieces = gather_pieces(tail[:, :32])
    (object_out,) = call(object_kernel, [(2, HEIGHT, WIDTH)], tail, scalars=False)
    (probe_out,) = call(probe_out_kernel, [(1, 2, SIDE, SIDE)], pieces, scalars=False)
    return object_out, probe_out


def solution(mesh):
    grid = Mesh(mesh.devices.reshape(2, 16, 2, 2, 4), TILE_AXES + MODE_AXES)
    return jax.shard_map(
        per_device,
        mesh=grid,
        in_specs=(
            P(None, None, TILE_AXES),
            P(MODE_AXES, None, None, None),
            P(TILE_AXES, None, None, None),
            P(TILE_AXES, None),
            P(TILE_AXES, None),
            P(TILE_AXES),
            P(TILE_AXES, None),
        ),
        out_specs=(P(None, None, TILE_AXES), P(MODE_AXES, None, None, None)),
        check_vma=False,
    )
```

```python
import math

import jax
import jax.numpy as jnp
import numpy as np
from jax import lax
from jax.experimental import pallas as pl
from jax.experimental.pallas import tpu as pltpu
from jax.sharding import Mesh
from jax.sharding import PartitionSpec as P

SOFT_FLOOR = 0.5
OBJECT_RATE = 1.0
OBJECT_DAMP = 0.5
PROBE_RATE = 1.0
PROBE_DAMP = 1.0

SIDE = 256
HEIGHT = 288
WIDTH = 512
WIDE = WIDTH + SIDE
MODES = 8
SLAB = SIDE // MODES
BAND = 2 * SLAB
STEPS = 3
TILES = 64
RINGS = 16
LANES = 128
COL_SPAN = SIDE + LANES
OUT_ROWS = 40
VMEM_LIMIT = 16 * 1024 * 1024

TILE_AXES = ("xlo", "z", "core")
MODE_AXES = ("xhi", "y")

ROW, COL, SLOT, LIVE, MODE, CORE, XLO, RING, HAS_NEXT, BAND_ID = range(10)

F32 = jnp.float32
BF16 = jnp.bfloat16


def slab_of(place):
    return place if place < MODES // 2 else 11 - place


def fourier_tables():
    index = np.arange(SIDE)
    angles = (index[:, None] * index[None, :] % SIDE) * (2.0 * math.pi / SIDE)
    both = np.stack([np.cos(angles), np.sin(angles)]) / math.sqrt(SIDE)
    high = both.astype(jnp.bfloat16)
    low = (both - high.astype(np.float64)).astype(jnp.bfloat16)
    return np.stack([high, low], axis=1)


def halves(value):
    high = value.astype(BF16)
    return high, (value - high.astype(F32)).astype(BF16)


def dot(left, right):
    return jnp.dot(left, right, preferred_element_type=F32)


def rows_transform(real, imag, tables, direction):
    high, low = halves(jnp.concatenate([real, imag], axis=0))

    def by(which):
        return (
            dot(high, tables[which, 0]) + dot(low, tables[which, 0]) + dot(high, tables[which, 1])
        )

    by_cos, by_sin = by(0), by(1)
    return (
        by_cos[:SIDE] + direction * by_sin[SIDE:],
        by_cos[SIDE:] - direction * by_sin[:SIDE],
    )


def columns_transform(real, imag, tables, direction):
    high, low = halves(jnp.concatenate([real, imag], axis=1))

    def by(which):
        return (
            dot(tables[which, 0], high) + dot(tables[which, 0], low) + dot(tables[which, 1], high)
        )

    by_cos, by_sin = by(0), by(1)
    return (
        by_cos[:, :SIDE] + direction * by_sin[:, SIDE:],
        by_cos[:, SIDE:] - direction * by_sin[:, :SIDE],
    )


def swap_blocks(parts):
    lanes = lax.broadcasted_iota(jnp.int32, (parts[0].shape[0], LANES), 1)
    grid = [[part[:, :LANES], part[:, LANES:]] for part in parts]
    grid = [[grid[(m & 3) | (h << 2)][m >> 2] for h in range(2)] for m in range(MODES)]
    for bit in (2, 1):
        shift = bit * SLAB
        low = (lanes & shift) == 0
        new = [None] * MODES
        for m in range(MODES):
            if m & bit:
                continue
            a, b = grid[m], grid[m | bit]
            new[m] = [jnp.where(low, a[h], pltpu.roll(b[h], shift, 1)) for h in range(2)]
            new[m | bit] = [
                jnp.where(low, pltpu.roll(a[h], LANES - shift, 1), b[h]) for h in range(2)
            ]
        grid = new
    return [jnp.concatenate(pair, axis=1) for pair in grid]


def stacked(pieces):
    return jnp.concatenate(list(pieces), axis=0)


def column_window(scal):
    col = scal[COL]
    block = jnp.minimum(col // LANES, WIDTH // LANES - 1)
    return pl.ds(pl.multiple_of(block * LANES, LANES), COL_SPAN), col - block * LANES


def take_patch(scal, band, view):
    cols, rest = column_window(scal)
    for part in range(2):
        block = band[part, :, cols]
        block = pltpu.roll(block, lax.rem(COL_SPAN - rest, COL_SPAN), 1)[:, :SIDE]
        view[part] = pltpu.roll(block, lax.rem(BAND - scal[ROW], BAND), 0)[:SLAB]


def forward(view, probe, tables, spectra):
    view_real = stacked([view[0]] * MODES)
    view_imag = stacked([view[1]] * MODES)
    probe_real = stacked(probe[mode, 0] for mode in range(MODES))
    probe_imag = stacked(probe[mode, 1] for mode in range(MODES))
    both = rows_transform(
        probe_real * view_real - probe_imag * view_imag,
        probe_real * view_imag + probe_imag * view_real,
        tables,
        1.0,
    )
    for part in range(2):
        blocks = [both[part][mode * SLAB : (mode + 1) * SLAB] for mode in range(MODES)]
        for place, block in enumerate(swap_blocks(blocks)):
            spectra[place, part] = block


def split_kernel(probe_in, pieces):
    for place in range(MODES):
        row = slab_of(place) * SLAB
        pieces[place] = probe_in[0, :, row : row + SLAB, :]


def first_kernel(scal, own, beside, probe, tables, band, view, shard, spectra):
    band[:, :, :WIDTH] = own[...]
    band[:, :, WIDTH:] = beside[...]
    take_patch(scal, band, view)
    mode = scal[RING] // 2
    rows = pl.ds(pl.multiple_of(scal[CORE] * 16 + scal[XLO] * 8, 8), 8)

    @pl.when(lax.rem(scal[RING], 2) == 0)
    def _():
        shard[...] = probe[mode, :, rows, :LANES]

    @pl.when(lax.rem(scal[RING], 2) == 1)
    def _():
        shard[...] = probe[mode, :, rows, LANES:]

    forward(view, probe, tables, spectra)


def far_place(ring):
    return (ring + RINGS // 2) % RINGS


def next_kernel(view, pieces, tables, probe, spectra):
    for xlo in range(2):
        for core in range(2):
            row = core * 16 + xlo * 8
            for mode in range(MODES):
                for half in range(2):
                    lanes = slice(half * LANES, (half + 1) * LANES)
                    piece = pieces[xlo, core, 2 * mode + half]
                    probe[mode, :, row : row + 8, lanes] = piece
    forward(view, probe, tables, spectra)


def counts_kernel(scal, measured, counts, flags):
    for place, which in enumerate((LIVE, CORE, XLO)):
        flags[place] = jnp.full((8, SIDE), scal[which].astype(F32))
    block = measured[0, scal[SLOT]].astype(F32)
    block = pltpu.roll(block, lax.rem(SIDE - scal[MODE] * SLAB, SIDE), 1)[:, :LANES]
    lanes = lax.broadcasted_iota(jnp.int32, block.shape, 1)
    block = jnp.where(lanes < SLAB, block, 0.0)
    block = block + pltpu.roll(block, SLAB, 1)
    counts[...] = block + pltpu.roll(block, 2 * SLAB, 1)


def ratio_kernel(spectra, counts, flags, tables, out):
    real = stacked(spectra[slab_of(index), 0] for index in range(MODES))
    imag = stacked(spectra[slab_of(index), 1] for index in range(MODES))
    far_real, far_imag = columns_transform(real, imag, tables, 1.0)
    power = far_real * far_real + far_imag * far_imag
    total = power[:, :LANES] + power[:, LANES:]
    total = total + pltpu.roll(total, 2 * SLAB, 1)
    total = total + pltpu.roll(total, SLAB, 1)
    ratio = jnp.sqrt((counts[...] + SOFT_FLOOR) / (total + SOFT_FLOOR)) - 1.0
    ratio = ratio * flags[0, 0:1, :LANES]
    ratio = jnp.concatenate([ratio, ratio], axis=1)
    both = columns_transform(far_real * ratio, far_imag * ratio, tables, -1.0)
    for part in range(2):
        for place in range(MODES):
            row = slab_of(place) * SLAB
            out[place, part] = both[part][row : row + SLAB]


def backward_kernel(spectra, view, flags, tables, chi, keep, send):
    real = stacked(swap_blocks([spectra[place, 0] for place in range(MODES)]))
    imag = stacked(swap_blocks([spectra[place, 1] for place in range(MODES)]))
    chi_real, chi_imag = rows_transform(real, imag, tables, -1.0)
    view_real, view_imag = view[0], view[1]
    sums = []
    for mode in range(MODES):
        real = chi_real[mode * SLAB : (mode + 1) * SLAB]
        imag = chi_imag[mode * SLAB : (mode + 1) * SLAB]
        chi[mode, 0] = real
        chi[mode, 1] = imag
        sums.append(view_real * real + view_imag * imag)
        sums.append(view_real * imag - view_imag * real)
    sums.append((view_real * view_real + view_imag * view_imag) * flags[0, 0:1, :])
    second = jnp.broadcast_to(flags[1, 0:1, :], (16, SIDE)) > 0.5
    for index, value in enumerate(sums):
        keep[index] = jnp.where(second, value[16:], value[:16])
        send[index] = jnp.where(second, value[:16], value[16:])


def halve_kernel(mine, theirs, flags, keep, send):
    second = jnp.broadcast_to(flags[2, 0:1, :], (8, SIDE)) > 0.5
    for index in range(2 * MODES + 1):
        value = mine[index] + theirs[index]
        keep[index] = jnp.where(second, value[8:], value[:8])
        send[index] = jnp.where(second, value[:8], value[8:])


def pack_kernel(mine, theirs, packed):
    for half in range(2):
        lanes = slice(half * LANES, (half + 1) * LANES)
        total = mine[:, :, lanes] + theirs[:, :, lanes]
        for mode in range(MODES):
            place = far_place(2 * mode + half)
            packed[place, 0] = total[2 * mode]
            packed[place, 1] = total[2 * mode + 1]
            packed[place, 2] = total[2 * MODES]


def step_kernel(chi, probe, step):
    real = imag = light = 0.0
    for mode in range(MODES):
        probe_real, probe_imag = probe[mode, 0], probe[mode, 1]
        real = real + (probe_real * chi[mode, 0] + probe_imag * chi[mode, 1])
        imag = imag + (probe_real * chi[mode, 1] - probe_imag * chi[mode, 0])
        light = light + (probe_real * probe_real + probe_imag * probe_imag)
    step[0] = OBJECT_RATE * real / (light + OBJECT_DAMP)
    step[1] = OBJECT_RATE * imag / (light + OBJECT_DAMP)


def place_kernel(scal, above, step, below, band, part_band, to_left, to_right):
    cols, rest = column_window(scal)
    height = 3 * SLAB
    part_band[...] = jnp.zeros_like(part_band)
    for part in range(2):
        block = stacked([above[part], step[part], below[part]])
        block = pltpu.roll(block, lax.rem(2 * SLAB + scal[ROW], height), 0)[:BAND]
        block = jnp.concatenate([block, jnp.zeros((BAND, LANES), F32)], axis=1)
        part_band[part, :, cols] = pltpu.roll(block, rest, 1)
    to_left[...] = part_band[:, :, :SIDE]
    to_right[...] = part_band[:, :, WIDTH:]
    part_band[:, :, :WIDTH] = part_band[:, :, :WIDTH] + band[:, :, :WIDTH]
    part_band[:, :, WIDTH:] = (
        part_band[:, :, WIDTH:] * scal[HAS_NEXT].astype(F32) + band[:, :, WIDTH:]
    )


def view_kernel(scal, part_band, from_left, from_right, band, view):
    band[:, :, :SIDE] = part_band[:, :, :SIDE] + from_left[...]
    band[:, :, SIDE:WIDTH] = part_band[:, :, SIDE:WIDTH]
    band[:, :, WIDTH:] = part_band[:, :, WIDTH:] + from_right[...]
    take_patch(scal, band, view)


def probe_kernel(sums, shard_in, shard, copies):
    total = sums[0]
    for ring in range(1, RINGS):
        total = total + sums[ring]
    new = shard_in[...] + PROBE_RATE * total[:2] / (total[2:] + PROBE_DAMP)
    shard[...] = new
    for ring in range(RINGS):
        copies[ring] = new


def out_rows_kernel(scal, part_band, from_left, rows_out):
    rows = pl.ds(pl.multiple_of(scal[BAND_ID] // 2 * 8, 8), OUT_ROWS)
    rows_out[:, :, :SIDE] = part_band[:, rows, :SIDE] + from_left[:, rows, :]
    rows_out[:, :, SIDE:] = part_band[:, rows, SIDE:WIDTH]


def tail_kernel(piece, rows_out, tail):
    for place in range(MODES):
        for half in range(2):
            for part in range(2):
                row = (half * 2 + part) * 8
                tail[place, row : row + 8] = piece[2 * place + half, part]
        for part in range(2):
            for block in range(WIDTH // LANES):
                row = 32 + (part * 4 + block) * OUT_ROWS
                lanes = slice(block * LANES, (block + 1) * LANES)
                tail[place, row : row + OUT_ROWS] = rows_out[part, :, lanes]


def object_kernel(tail, object_out):
    for place in range(MODES):
        first = slab_of(place) * 9 // 2 * 8
        for part in range(2):
            for block in range(WIDTH // LANES):
                row = 32 + (part * 4 + block) * OUT_ROWS
                lanes = slice(block * LANES, (block + 1) * LANES)
                object_out[part, first : first + OUT_ROWS, lanes] = tail[
                    place, row : row + OUT_ROWS
                ]


def probe_out_kernel(pieces, probe_out):
    for xlo in range(2):
        for core in range(2):
            for place in range(MODES):
                first = slab_of(place) * SLAB + core * 16 + xlo * 8
                for half in range(2):
                    lanes = slice(half * LANES, (half + 1) * LANES)
                    for part in range(2):
                        row = (half * 2 + part) * 8
                        probe_out[0, part, first : first + 8, lanes] = pieces[
                            xlo, core, place, row : row + 8
                        ]


def own_kernel(place, whole, own, left, sems):
    rows = pl.ds(pl.multiple_of(place[0] * SLAB, SLAB), BAND)
    first = pltpu.make_async_copy(whole.at[:, rows, :], own, sems.at[0])
    second = pltpu.make_async_copy(whole.at[:, rows, pl.ds(0, SIDE)], left, sems.at[1])
    first.start()
    second.start()
    first.wait()
    second.wait()


def take_own(mode, object_tiles, after):
    vmem = pl.BlockSpec(memory_space=pltpu.VMEM)
    anywhere = pl.BlockSpec(memory_space=pl.ANY)

    def body(place, whole, _, own, left, sems):
        own_kernel(place, whole, own, left, sems)

    return pl.pallas_call(
        body,
        out_shape=[
            jax.ShapeDtypeStruct((2, BAND, WIDTH), F32),
            jax.ShapeDtypeStruct((2, BAND, SIDE), F32),
        ],
        in_specs=[pl.BlockSpec(memory_space=pltpu.SMEM), anywhere, anywhere],
        out_specs=[vmem, vmem],
        scratch_shapes=[pltpu.SemaphoreType.DMA((2,))],
        compiler_params=pltpu.CompilerParams(vmem_limit_bytes=VMEM_LIMIT),
        name="own_kernel",
    )(mode.astype(jnp.int32).reshape(1), object_tiles, after)


def call(kernel, outs, *args, scalars=True, after=()):
    vmem = pl.BlockSpec(memory_space=pltpu.VMEM)
    in_specs = [vmem] * len(args) + [pl.BlockSpec(memory_space=pl.ANY)] * len(after)

    def body(*refs):
        taken = list(refs[: len(args)])
        if scalars:
            taken[0] = [taken[0][0, index] for index in range(BAND_ID + 1)]
        kernel(*taken, *refs[len(args) + len(after) :])

    return pl.pallas_call(
        body,
        out_shape=[jax.ShapeDtypeStruct(shape, F32) for shape in outs],
        in_specs=in_specs,
        out_specs=[vmem] * len(outs),
        compiler_params=pltpu.CompilerParams(vmem_limit_bytes=VMEM_LIMIT),
        name=kernel.__name__,
    )(*args, *after)


def shift(value, axes, count, steps):
    first, last = max(0, -steps), min(count, count - steps)
    return lax.ppermute(value, axes, [(i, i + steps) for i in range(first, last)])


def other(value, axis):
    return lax.ppermute(value, axis, [(0, 1), (1, 0)])


def beside_slab(value, steps):
    first, last = max(0, -steps), min(MODES, MODES - steps)
    pairs = [(slab_of(i), slab_of(i + steps)) for i in range(first, last)]
    return lax.ppermute(value, MODE_AXES, pairs)


def exchange_rings(value):
    groups = [[far_place(ring) for ring in range(RINGS)]]
    return lax.all_to_all(value, "z", 0, 0, tiled=True, axis_index_groups=groups)


def exchange(value, axes):
    return lax.all_to_all(value, axes, 0, 0, tiled=True)


def gather_pieces(piece):
    gathered = lax.all_gather(piece, ("xlo", "core"))
    return gathered.reshape((2, 2) + piece.shape)


def per_device(
    object_tiles, probe_modes, measured, row_offset, col_offset, live_counts, visit_order
):
    tables = jnp.asarray(fourier_tables())
    slots = visit_order[0]
    tile = lax.axis_index(TILE_AXES)
    mode = lax.axis_index(MODE_AXES)
    slab = jnp.where(mode < MODES // 2, mode, 11 - mode)
    (pieces,) = call(split_kernel, [(MODES, 2, SLAB, SIDE)], probe_modes, scalars=False)
    probe = exchange(pieces, MODE_AXES)
    own, left = take_own(slab, object_tiles, pieces)
    beside = shift(left, TILE_AXES, TILES, -1)
    places = [
        mode,
        lax.axis_index("core"),
        lax.axis_index("xlo"),
        lax.axis_index("z"),
        (tile < TILES - 1).astype(jnp.int32),
        slab,
    ]
    chosen = slots[:, None] == jnp.arange(STEPS, dtype=jnp.int32)[None, :]
    per_step = [
        jnp.sum(jnp.where(chosen, row_offset, 0), axis=1),
        jnp.sum(jnp.where(chosen, col_offset, 0), axis=1),
        slots,
        (slots < live_counts[0]).astype(jnp.int32),
    ]
    scalars = jnp.stack(
        per_step + [jnp.broadcast_to(place, (STEPS,)) for place in places], axis=1
    )
    slabs = (MODES, 2, SLAB, SIDE)
    slab_pair = (2, SLAB, SIDE)
    band_shape = (2, BAND, WIDE)
    edge = (2, BAND, SIDE)
    counts_shapes = [(SIDE, LANES), (3, 8, SIDE)]
    counts, flags = call(counts_kernel, counts_shapes, scalars[:1], measured)
    for step in range(STEPS):
        scal = scalars[step : step + 1]
        final = step == STEPS - 1
        if step == 0:
            band, view, shard, spectra = call(
                first_kernel,
                [band_shape, slab_pair, (2, 8, LANES), slabs],
                scal,
                own,
                beside,
                probe,
                tables,
                after=(counts,),
            )
        else:
            probe, spectra = call(
                next_kernel,
                [slabs, slabs],
                view,
                pieces,
                tables,
                scalars=False,
                after=(counts,),
            )
        spectra = exchange(spectra, MODE_AXES)
        (spectra,) = call(
            ratio_kernel, [slabs], spectra, counts, flags, tables, scalars=False
        )
        spectra = exchange(spectra, MODE_AXES)
        chi, keep, send = call(
            backward_kernel,
            [slabs] + [(2 * MODES + 1, 16, SIDE)] * 2,
            spectra,
            view,
            flags,
            tables,
            scalars=False,
        )
        received = other(send, "core")
        keep, send = call(
            halve_kernel, [(2 * MODES + 1, 8, SIDE)] * 2, keep, received, flags, scalars=False
        )
        received = other(send, "xlo")
        (object_step,) = call(
            step_kernel, [slab_pair], chi, probe, scalars=False, after=(keep,)
        )
        above = beside_slab(object_step, 1)
        below = beside_slab(object_step, -1)
        (packed,) = call(
            pack_kernel,
            [(RINGS, 3, 8, LANES)],
            keep,
            received,
            scalars=False,
            after=(above, below) if final else (object_step,),
        )
        sums = exchange_rings(packed)
        placing = [scal, above, object_step, below, band]
        if final:
            part_band, _, to_right = call(
                place_kernel, [band_shape, edge, edge], *placing, after=(packed,)
            )
            from_left = shift(to_right, TILE_AXES, TILES, 1)
            (rows_out,) = call(
                out_rows_kernel, [(2, OUT_ROWS, WIDTH)], scal, part_band, from_left
            )
            before = (rows_out,)
        else:
            next_scal = scalars[step + 1 : step + 2]
            counts, flags = call(
                counts_kernel, counts_shapes, next_scal, measured, after=(packed,)
            )
            before = (above, below, counts)
        shard, shards = call(
            probe_kernel,
            [(2, 8, LANES), (RINGS, 2, 8, LANES)],
            sums,
            shard,
            scalars=False,
            after=before,
        )
        piece = exchange(shards, "z")
        if not final:
            part_band, to_left, to_right = call(
                place_kernel, [band_shape, edge, edge], *placing, after=(shards,)
            )
            from_left = shift(to_right, TILE_AXES, TILES, 1)
            from_right = shift(to_left, TILE_AXES, TILES, -1)
            band, view = call(
                view_kernel,
                [band_shape, slab_pair],
                next_scal,
                part_band,
                from_left,
                from_right,
            )
            piece, view = lax.optimization_barrier((piece, view))
            pieces = gather_pieces(piece)
    tail_rows = 32 + 8 * OUT_ROWS
    (tail,) = call(
        tail_kernel, [(MODES, tail_rows, LANES)], piece, rows_out, scalars=False
    )
    tail = exchange(tail, MODE_AXES)
    pieces = gather_pieces(tail[:, :32])
    (object_out,) = call(object_kernel, [(2, HEIGHT, WIDTH)], tail, scalars=False)
    (probe_out,) = call(probe_out_kernel, [(1, 2, SIDE, SIDE)], pieces, scalars=False)
    return object_out, probe_out


def solution(mesh):
    grid = Mesh(mesh.devices.reshape(2, 16, 2, 2, 4), TILE_AXES + MODE_AXES)
    return jax.shard_map(
        per_device,
        mesh=grid,
        in_specs=(
            P(None, None, TILE_AXES),
            P(MODE_AXES, None, None, None),
            P(TILE_AXES, None, None, None),
            P(TILE_AXES, None),
            P(TILE_AXES, None),
            P(TILE_AXES),
            P(TILE_AXES, None),
        ),
        out_specs=(P(None, None, TILE_AXES), P(MODE_AXES, None, None, None)),
        check_vma=False,
    )
```

```python
import math

import jax
import jax.numpy as jnp
import numpy as np
from jax import lax
from jax.experimental import pallas as pl
from jax.experimental.pallas import tpu as pltpu
from jax.sharding import Mesh
from jax.sharding import PartitionSpec as P

SOFT_FLOOR = 0.5
OBJECT_RATE = 1.0
OBJECT_DAMP = 0.5
PROBE_RATE = 1.0
PROBE_DAMP = 1.0

SIDE = 256
HEIGHT = 288
WIDTH = 512
WIDE = WIDTH + SIDE
MODES = 8
SLAB = SIDE // MODES
BAND = 2 * SLAB
STEPS = 3
TILES = 64
RINGS = 16
LANES = 128
COL_SPAN = SIDE + LANES
OUT_ROWS = 40
PROBE_ROWS = 64
VMEM_LIMIT = 16 * 1024 * 1024

TILE_AXES = ("xlo", "z", "core")
MODE_AXES = ("xhi", "y")

ROW, COL, SLOT, LIVE, MODE, CORE, XLO, RING, HAS_NEXT, BAND_ID = range(10)

F32 = jnp.float32
BF16 = jnp.bfloat16


def slab_of(place):
    return place if place < MODES // 2 else 11 - place


def fourier_tables():
    index = np.arange(SIDE)
    angles = (index[:, None] * index[None, :] % SIDE) * (2.0 * math.pi / SIDE)
    both = np.stack([np.cos(angles), np.sin(angles)]) / math.sqrt(SIDE)
    high = both.astype(jnp.bfloat16)
    low = (both - high.astype(np.float64)).astype(jnp.bfloat16)
    return np.stack([high, low], axis=1)


def halves(value):
    high = value.astype(BF16)
    return high, (value - high.astype(F32)).astype(BF16)


def dot(left, right):
    return jnp.dot(left, right, preferred_element_type=F32)


def rows_transform(real, imag, tables, direction):
    high, low = halves(jnp.concatenate([real, imag], axis=0))

    def by(which):
        return (
            dot(high, tables[which, 0]) + dot(low, tables[which, 0]) + dot(high, tables[which, 1])
        )

    by_cos, by_sin = by(0), by(1)
    return (
        by_cos[:SIDE] + direction * by_sin[SIDE:],
        by_cos[SIDE:] - direction * by_sin[:SIDE],
    )


def columns_transform(real, imag, tables, direction):
    high, low = halves(jnp.concatenate([real, imag], axis=1))

    def by(which):
        return (
            dot(tables[which, 0], high) + dot(tables[which, 0], low) + dot(tables[which, 1], high)
        )

    by_cos, by_sin = by(0), by(1)
    return (
        by_cos[:, :SIDE] + direction * by_sin[:, SIDE:],
        by_cos[:, SIDE:] - direction * by_sin[:, :SIDE],
    )


def swap_blocks(parts):
    lanes = lax.broadcasted_iota(jnp.int32, (parts[0].shape[0], LANES), 1)
    grid = [[part[:, :LANES], part[:, LANES:]] for part in parts]
    grid = [[grid[(m & 3) | (h << 2)][m >> 2] for h in range(2)] for m in range(MODES)]
    for bit in (2, 1):
        shift = bit * SLAB
        low = (lanes & shift) == 0
        new = [None] * MODES
        for m in range(MODES):
            if m & bit:
                continue
            a, b = grid[m], grid[m | bit]
            new[m] = [jnp.where(low, a[h], pltpu.roll(b[h], shift, 1)) for h in range(2)]
            new[m | bit] = [
                jnp.where(low, pltpu.roll(a[h], LANES - shift, 1), b[h]) for h in range(2)
            ]
        grid = new
    return [jnp.concatenate(pair, axis=1) for pair in grid]


def stacked(pieces):
    return jnp.concatenate(list(pieces), axis=0)


def column_window(scal):
    col = scal[COL]
    block = jnp.minimum(col // LANES, WIDTH // LANES - 1)
    return pl.ds(pl.multiple_of(block * LANES, LANES), COL_SPAN), col - block * LANES


def take_patch(scal, band, view):
    cols, rest = column_window(scal)
    for part in range(2):
        block = band[part, :, cols]
        block = pltpu.roll(block, lax.rem(COL_SPAN - rest, COL_SPAN), 1)[:, :SIDE]
        view[part] = pltpu.roll(block, lax.rem(BAND - scal[ROW], BAND), 0)[:SLAB]


def forward(view, probe, tables, spectra):
    view_real = stacked([view[0]] * MODES)
    view_imag = stacked([view[1]] * MODES)
    probe_real = stacked(probe[mode, 0] for mode in range(MODES))
    probe_imag = stacked(probe[mode, 1] for mode in range(MODES))
    both = rows_transform(
        probe_real * view_real - probe_imag * view_imag,
        probe_real * view_imag + probe_imag * view_real,
        tables,
        1.0,
    )
    for part in range(2):
        blocks = [both[part][mode * SLAB : (mode + 1) * SLAB] for mode in range(MODES)]
        for place, block in enumerate(swap_blocks(blocks)):
            spectra[place, part] = block


def split_kernel(probe_in, pieces):
    for place in range(MODES):
        row = slab_of(place) * SLAB
        pieces[place] = probe_in[0, :, row : row + SLAB, :]


def first_kernel(scal, own, beside, probe, tables, band, view, shard, spectra):
    band[:, :, :WIDTH] = own[...]
    band[:, :, WIDTH:] = beside[...]
    take_patch(scal, band, view)
    mode = scal[RING] // 2
    rows = pl.ds(pl.multiple_of(scal[CORE] * 16 + scal[XLO] * 8, 8), 8)

    @pl.when(lax.rem(scal[RING], 2) == 0)
    def _():
        shard[...] = probe[mode, :, rows, :LANES]

    @pl.when(lax.rem(scal[RING], 2) == 1)
    def _():
        shard[...] = probe[mode, :, rows, LANES:]

    forward(view, probe, tables, spectra)


def far_place(ring):
    return (ring + RINGS // 2) % RINGS


def next_kernel(view, pieces, tables, probe, spectra):
    for xlo in range(2):
        for core in range(2):
            row = core * 16 + xlo * 8
            for mode in range(MODES):
                for half in range(2):
                    lanes = slice(half * LANES, (half + 1) * LANES)
                    piece = pieces[core, xlo, 2 * mode + half]
                    probe[mode, :, row : row + 8, lanes] = piece
    forward(view, probe, tables, spectra)


def counts_kernel(scal, measured, counts, flags):
    for place, which in enumerate((LIVE, CORE, XLO)):
        flags[place] = jnp.full((8, SIDE), scal[which].astype(F32))
    block = measured[0, scal[SLOT]].astype(F32)
    block = pltpu.roll(block, lax.rem(SIDE - scal[MODE] * SLAB, SIDE), 1)[:, :LANES]
    lanes = lax.broadcasted_iota(jnp.int32, block.shape, 1)
    block = jnp.where(lanes < SLAB, block, 0.0)
    block = block + pltpu.roll(block, SLAB, 1)
    counts[...] = block + pltpu.roll(block, 2 * SLAB, 1)


def ratio_kernel(spectra, counts, flags, tables, out):
    real = stacked(spectra[slab_of(index), 0] for index in range(MODES))
    imag = stacked(spectra[slab_of(index), 1] for index in range(MODES))
    far_real, far_imag = columns_transform(real, imag, tables, 1.0)
    power = far_real * far_real + far_imag * far_imag
    total = power[:, :LANES] + power[:, LANES:]
    total = total + pltpu.roll(total, 2 * SLAB, 1)
    total = total + pltpu.roll(total, SLAB, 1)
    ratio = jnp.sqrt((counts[...] + SOFT_FLOOR) / (total + SOFT_FLOOR)) - 1.0
    ratio = ratio * flags[0, 0:1, :LANES]
    ratio = jnp.concatenate([ratio, ratio], axis=1)
    both = columns_transform(far_real * ratio, far_imag * ratio, tables, -1.0)
    for part in range(2):
        for place in range(MODES):
            row = slab_of(place) * SLAB
            out[place, part] = both[part][row : row + SLAB]


def backward_kernel(spectra, view, flags, tables, chi, keep, send):
    real = stacked(swap_blocks([spectra[place, 0] for place in range(MODES)]))
    imag = stacked(swap_blocks([spectra[place, 1] for place in range(MODES)]))
    chi_real, chi_imag = rows_transform(real, imag, tables, -1.0)
    view_real, view_imag = view[0], view[1]
    sums = []
    for mode in range(MODES):
        real = chi_real[mode * SLAB : (mode + 1) * SLAB]
        imag = chi_imag[mode * SLAB : (mode + 1) * SLAB]
        chi[mode, 0] = real
        chi[mode, 1] = imag
        sums.append(view_real * real + view_imag * imag)
        sums.append(view_real * imag - view_imag * real)
    sums.append((view_real * view_real + view_imag * view_imag) * flags[0, 0:1, :])
    second = jnp.broadcast_to(flags[1, 0:1, :], (16, SIDE)) > 0.5
    for index, value in enumerate(sums):
        keep[index] = jnp.where(second, value[16:], value[:16])
        send[index] = jnp.where(second, value[:16], value[16:])


def halve_kernel(mine, theirs, flags, keep, send):
    second = jnp.broadcast_to(flags[2, 0:1, :], (8, SIDE)) > 0.5
    for index in range(2 * MODES + 1):
        value = mine[index] + theirs[index]
        keep[index] = jnp.where(second, value[8:], value[:8])
        send[index] = jnp.where(second, value[:8], value[8:])


def pack_kernel(mine, theirs, packed):
    for half in range(2):
        lanes = slice(half * LANES, (half + 1) * LANES)
        total = mine[:, :, lanes] + theirs[:, :, lanes]
        for mode in range(MODES):
            place = far_place(2 * mode + half)
            packed[place, 0] = total[2 * mode]
            packed[place, 1] = total[2 * mode + 1]
            packed[place, 2] = total[2 * MODES]


def step_kernel(chi, probe, step):
    real = imag = light = 0.0
    for mode in range(MODES):
        probe_real, probe_imag = probe[mode, 0], probe[mode, 1]
        real = real + (probe_real * chi[mode, 0] + probe_imag * chi[mode, 1])
        imag = imag + (probe_real * chi[mode, 1] - probe_imag * chi[mode, 0])
        light = light + (probe_real * probe_real + probe_imag * probe_imag)
    step[0] = OBJECT_RATE * real / (light + OBJECT_DAMP)
    step[1] = OBJECT_RATE * imag / (light + OBJECT_DAMP)


def place_kernel(scal, above, step, below, band, part_band, to_left, to_right):
    cols, rest = column_window(scal)
    height = 3 * SLAB
    part_band[...] = jnp.zeros_like(part_band)
    for part in range(2):
        block = stacked([above[part], step[part], below[part]])
        block = pltpu.roll(block, lax.rem(2 * SLAB + scal[ROW], height), 0)[:BAND]
        block = jnp.concatenate([block, jnp.zeros((BAND, LANES), F32)], axis=1)
        part_band[part, :, cols] = pltpu.roll(block, rest, 1)
    to_left[...] = part_band[:, :, :SIDE]
    to_right[...] = part_band[:, :, WIDTH:]
    part_band[:, :, :WIDTH] = part_band[:, :, :WIDTH] + band[:, :, :WIDTH]
    part_band[:, :, WIDTH:] = (
        part_band[:, :, WIDTH:] * scal[HAS_NEXT].astype(F32) + band[:, :, WIDTH:]
    )


def view_kernel(scal, part_band, from_left, from_right, band, view):
    band[:, :, :SIDE] = part_band[:, :, :SIDE] + from_left[...]
    band[:, :, SIDE:WIDTH] = part_band[:, :, SIDE:WIDTH]
    band[:, :, WIDTH:] = part_band[:, :, WIDTH:] + from_right[...]
    take_patch(scal, band, view)


def probe_kernel(sums, shard_in, shard, copies):
    total = sums[0]
    for ring in range(1, RINGS):
        total = total + sums[ring]
    new = shard_in[...] + PROBE_RATE * total[:2] / (total[2:] + PROBE_DAMP)
    shard[...] = new
    for place in range(2 * RINGS):
        copies[place] = new


def out_rows_kernel(scal, part_band, from_left, rows_out):
    rows = pl.ds(pl.multiple_of(scal[BAND_ID] // 2 * 8, 8), OUT_ROWS)
    rows_out[:, :, :SIDE] = part_band[:, rows, :SIDE] + from_left[:, rows, :]
    rows_out[:, :, SIDE:] = part_band[:, rows, SIDE:WIDTH]


def tail_kernel(piece, rows_out, tail):
    for place in range(MODES):
        for xlo in range(2):
            for half in range(2):
                for part in range(2):
                    row = ((xlo * 2 + half) * 2 + part) * 8
                    tail[place, row : row + 8] = piece[xlo * RINGS + 2 * place + half, part]
        for part in range(2):
            for block in range(WIDTH // LANES):
                row = PROBE_ROWS + (part * 4 + block) * OUT_ROWS
                lanes = slice(block * LANES, (block + 1) * LANES)
                tail[place, row : row + OUT_ROWS] = rows_out[part, :, lanes]


def object_kernel(tail, object_out):
    for place in range(MODES):
        first = slab_of(place) * 9 // 2 * 8
        for part in range(2):
            for block in range(WIDTH // LANES):
                row = PROBE_ROWS + (part * 4 + block) * OUT_ROWS
                lanes = slice(block * LANES, (block + 1) * LANES)
                object_out[part, first : first + OUT_ROWS, lanes] = tail[
                    place, row : row + OUT_ROWS
                ]


def probe_out_kernel(pieces, probe_out):
    for xlo in range(2):
        for core in range(2):
            for place in range(MODES):
                first = slab_of(place) * SLAB + core * 16 + xlo * 8
                for half in range(2):
                    lanes = slice(half * LANES, (half + 1) * LANES)
                    for part in range(2):
                        row = ((xlo * 2 + half) * 2 + part) * 8
                        probe_out[0, part, first : first + 8, lanes] = pieces[
                            core, place, row : row + 8
                        ]


def own_kernel(place, whole, own, left, sems):
    rows = pl.ds(pl.multiple_of(place[0] * SLAB, SLAB), BAND)
    first = pltpu.make_async_copy(whole.at[:, rows, :], own, sems.at[0])
    second = pltpu.make_async_copy(whole.at[:, rows, pl.ds(0, SIDE)], left, sems.at[1])
    first.start()
    second.start()
    first.wait()
    second.wait()


def take_own(mode, object_tiles, after):
    vmem = pl.BlockSpec(memory_space=pltpu.VMEM)
    anywhere = pl.BlockSpec(memory_space=pl.ANY)

    def body(place, whole, _, own, left, sems):
        own_kernel(place, whole, own, left, sems)

    return pl.pallas_call(
        body,
        out_shape=[
            jax.ShapeDtypeStruct((2, BAND, WIDTH), F32),
            jax.ShapeDtypeStruct((2, BAND, SIDE), F32),
        ],
        in_specs=[pl.BlockSpec(memory_space=pltpu.SMEM), anywhere, anywhere],
        out_specs=[vmem, vmem],
        scratch_shapes=[pltpu.SemaphoreType.DMA((2,))],
        compiler_params=pltpu.CompilerParams(vmem_limit_bytes=VMEM_LIMIT),
        name="own_kernel",
    )(mode.astype(jnp.int32).reshape(1), object_tiles, after)


def call(kernel, outs, *args, scalars=True, after=()):
    vmem = pl.BlockSpec(memory_space=pltpu.VMEM)
    in_specs = [vmem] * len(args) + [pl.BlockSpec(memory_space=pl.ANY)] * len(after)

    def body(*refs):
        taken = list(refs[: len(args)])
        if scalars:
            taken[0] = [taken[0][0, index] for index in range(BAND_ID + 1)]
        kernel(*taken, *refs[len(args) + len(after) :])

    return pl.pallas_call(
        body,
        out_shape=[jax.ShapeDtypeStruct(shape, F32) for shape in outs],
        in_specs=in_specs,
        out_specs=[vmem] * len(outs),
        compiler_params=pltpu.CompilerParams(vmem_limit_bytes=VMEM_LIMIT),
        name=kernel.__name__,
    )(*args, *after)


def shift(value, axes, count, steps):
    first, last = max(0, -steps), min(count, count - steps)
    return lax.ppermute(value, axes, [(i, i + steps) for i in range(first, last)])


def other(value, axis):
    return lax.ppermute(value, axis, [(0, 1), (1, 0)])


def beside_slab(value, steps):
    first, last = max(0, -steps), min(MODES, MODES - steps)
    pairs = [(slab_of(i), slab_of(i + steps)) for i in range(first, last)]
    return lax.ppermute(value, MODE_AXES, pairs)


def exchange_rings(value):
    groups = [[far_place(ring) for ring in range(RINGS)]]
    return lax.all_to_all(value, "z", 0, 0, tiled=True, axis_index_groups=groups)


def exchange(value, axes):
    return lax.all_to_all(value, axes, 0, 0, tiled=True)


def per_device(
    object_tiles, probe_modes, measured, row_offset, col_offset, live_counts, visit_order
):
    tables = jnp.asarray(fourier_tables())
    slots = visit_order[0]
    tile = lax.axis_index(TILE_AXES)
    mode = lax.axis_index(MODE_AXES)
    slab = jnp.where(mode < MODES // 2, mode, 11 - mode)
    (pieces,) = call(split_kernel, [(MODES, 2, SLAB, SIDE)], probe_modes, scalars=False)
    probe = exchange(pieces, MODE_AXES)
    own, left = take_own(slab, object_tiles, pieces)
    beside = shift(left, TILE_AXES, TILES, -1)
    places = [
        mode,
        lax.axis_index("core"),
        lax.axis_index("xlo"),
        lax.axis_index("z"),
        (tile < TILES - 1).astype(jnp.int32),
        slab,
    ]
    chosen = slots[:, None] == jnp.arange(STEPS, dtype=jnp.int32)[None, :]
    per_step = [
        jnp.sum(jnp.where(chosen, row_offset, 0), axis=1),
        jnp.sum(jnp.where(chosen, col_offset, 0), axis=1),
        slots,
        (slots < live_counts[0]).astype(jnp.int32),
    ]
    scalars = jnp.stack(
        per_step + [jnp.broadcast_to(place, (STEPS,)) for place in places], axis=1
    )
    slabs = (MODES, 2, SLAB, SIDE)
    slab_pair = (2, SLAB, SIDE)
    band_shape = (2, BAND, WIDE)
    edge = (2, BAND, SIDE)
    counts_shapes = [(SIDE, LANES), (3, 8, SIDE)]
    counts, flags = call(counts_kernel, counts_shapes, scalars[:1], measured)
    for step in range(STEPS):
        scal = scalars[step : step + 1]
        final = step == STEPS - 1
        if step == 0:
            band, view, shard, spectra = call(
                first_kernel,
                [band_shape, slab_pair, (2, 8, LANES), slabs],
                scal,
                own,
                beside,
                probe,
                tables,
                after=(counts,),
            )
        else:
            probe, spectra = call(
                next_kernel,
                [slabs, slabs],
                view,
                pieces,
                tables,
                scalars=False,
                after=(counts,),
            )
        spectra = exchange(spectra, MODE_AXES)
        (spectra,) = call(
            ratio_kernel, [slabs], spectra, counts, flags, tables, scalars=False
        )
        spectra = exchange(spectra, MODE_AXES)
        chi, keep, send = call(
            backward_kernel,
            [slabs] + [(2 * MODES + 1, 16, SIDE)] * 2,
            spectra,
            view,
            flags,
            tables,
            scalars=False,
        )
        received = other(send, "core")
        keep, send = call(
            halve_kernel, [(2 * MODES + 1, 8, SIDE)] * 2, keep, received, flags, scalars=False
        )
        received = other(send, "xlo")
        (object_step,) = call(
            step_kernel, [slab_pair], chi, probe, scalars=False, after=(keep,)
        )
        above = beside_slab(object_step, 1)
        below = beside_slab(object_step, -1)
        (packed,) = call(
            pack_kernel,
            [(RINGS, 3, 8, LANES)],
            keep,
            received,
            scalars=False,
            after=(above, below) if final else (object_step,),
        )
        sums = exchange_rings(packed)
        placing = [scal, above, object_step, below, band]
        if final:
            part_band, _, to_right = call(
                place_kernel, [band_shape, edge, edge], *placing, after=(packed,)
            )
            from_left = shift(to_right, TILE_AXES, TILES, 1)
            (rows_out,) = call(
                out_rows_kernel, [(2, OUT_ROWS, WIDTH)], scal, part_band, from_left
            )
            before = (rows_out,)
        else:
            next_scal = scalars[step + 1 : step + 2]
            counts, flags = call(
                counts_kernel, counts_shapes, next_scal, measured, after=(packed,)
            )
            before = (above, below, counts)
        shard, shards = call(
            probe_kernel,
            [(2, 8, LANES), (2 * RINGS, 2, 8, LANES)],
            sums,
            shard,
            scalars=False,
            after=before,
        )
        piece = exchange(shards, ("xlo", "z"))
        if not final:
            part_band, to_left, to_right = call(
                place_kernel, [band_shape, edge, edge], *placing, after=(shards,)
            )
            from_left = shift(to_right, TILE_AXES, TILES, 1)
            from_right = shift(to_left, TILE_AXES, TILES, -1)
            band, view = call(
                view_kernel,
                [band_shape, slab_pair],
                next_scal,
                part_band,
                from_left,
                from_right,
            )
            piece, view = lax.optimization_barrier((piece, view))
            pieces = lax.all_gather(piece, "core").reshape(2, 2, RINGS, 2, 8, LANES)
    tail_rows = PROBE_ROWS + 8 * OUT_ROWS
    (tail,) = call(
        tail_kernel, [(MODES, tail_rows, LANES)], piece, rows_out, scalars=False
    )
    tail = exchange(tail, MODE_AXES)
    pieces = lax.all_gather(tail[:, :PROBE_ROWS], "core")
    (object_out,) = call(object_kernel, [(2, HEIGHT, WIDTH)], tail, scalars=False)
    (probe_out,) = call(probe_out_kernel, [(1, 2, SIDE, SIDE)], pieces, scalars=False)
    return object_out, probe_out


def solution(mesh):
    grid = Mesh(mesh.devices.reshape(2, 16, 2, 2, 4), TILE_AXES + MODE_AXES)
    return jax.shard_map(
        per_device,
        mesh=grid,
        in_specs=(
            P(None, None, TILE_AXES),
            P(MODE_AXES, None, None, None),
            P(TILE_AXES, None, None, None),
            P(TILE_AXES, None),
            P(TILE_AXES, None),
            P(TILE_AXES),
            P(TILE_AXES, None),
        ),
        out_specs=(P(None, None, TILE_AXES), P(MODE_AXES, None, None, None)),
        check_vma=False,
    )
```

```python
import math

import jax
import jax.numpy as jnp
import numpy as np
from jax import lax
from jax.experimental import pallas as pl
from jax.experimental.pallas import tpu as pltpu
from jax.sharding import Mesh
from jax.sharding import PartitionSpec as P

SOFT_FLOOR = 0.5
OBJECT_RATE = 1.0
OBJECT_DAMP = 0.5
PROBE_RATE = 1.0
PROBE_DAMP = 1.0

SIDE = 256
HEIGHT = 288
WIDTH = 512
WIDE = WIDTH + SIDE
MODES = 8
SLAB = SIDE // MODES
BAND = 2 * SLAB
STEPS = 3
TILES = 64
RINGS = 16
LANES = 128
COL_SPAN = SIDE + LANES
OUT_ROWS = 40
MESSAGE = 2 * MODES + 1
VMEM_LIMIT = 16 * 1024 * 1024

TILE_AXES = ("xlo", "z", "core")
MODE_AXES = ("xhi", "y")

ROW, COL, SLOT, LIVE, MODE, CORE, XLO, RING, HAS_NEXT, BAND_ID = range(10)

F32 = jnp.float32
BF16 = jnp.bfloat16


def slab_of(place):
    return place if place < MODES // 2 else 11 - place


def fourier_tables():
    index = np.arange(SIDE)
    angles = (index[:, None] * index[None, :] % SIDE) * (2.0 * math.pi / SIDE)
    both = np.stack([np.cos(angles), np.sin(angles)]) / math.sqrt(SIDE)
    high = both.astype(jnp.bfloat16)
    low = (both - high.astype(np.float64)).astype(jnp.bfloat16)
    return np.stack([high, low], axis=1)


def halves(value):
    high = value.astype(BF16)
    return high, (value - high.astype(F32)).astype(BF16)


def dot(left, right):
    return jnp.dot(left, right, preferred_element_type=F32)


def rows_transform(real, imag, tables, direction):
    high, low = halves(jnp.concatenate([real, imag], axis=0))

    def by(which):
        return (
            dot(high, tables[which, 0]) + dot(low, tables[which, 0]) + dot(high, tables[which, 1])
        )

    by_cos, by_sin = by(0), by(1)
    return (
        by_cos[:SIDE] + direction * by_sin[SIDE:],
        by_cos[SIDE:] - direction * by_sin[:SIDE],
    )


def columns_transform(real, imag, tables, direction):
    high, low = halves(jnp.concatenate([real, imag], axis=1))

    def by(which):
        return (
            dot(tables[which, 0], high) + dot(tables[which, 0], low) + dot(tables[which, 1], high)
        )

    by_cos, by_sin = by(0), by(1)
    return (
        by_cos[:, :SIDE] + direction * by_sin[:, SIDE:],
        by_cos[:, SIDE:] - direction * by_sin[:, :SIDE],
    )


def swap_blocks(parts):
    lanes = lax.broadcasted_iota(jnp.int32, (parts[0].shape[0], LANES), 1)
    grid = [[part[:, :LANES], part[:, LANES:]] for part in parts]
    grid = [[grid[(m & 3) | (h << 2)][m >> 2] for h in range(2)] for m in range(MODES)]
    for bit in (2, 1):
        shift = bit * SLAB
        low = (lanes & shift) == 0
        new = [None] * MODES
        for m in range(MODES):
            if m & bit:
                continue
            a, b = grid[m], grid[m | bit]
            new[m] = [jnp.where(low, a[h], pltpu.roll(b[h], shift, 1)) for h in range(2)]
            new[m | bit] = [
                jnp.where(low, pltpu.roll(a[h], LANES - shift, 1), b[h]) for h in range(2)
            ]
        grid = new
    return [jnp.concatenate(pair, axis=1) for pair in grid]


def stacked(pieces):
    return jnp.concatenate(list(pieces), axis=0)


def column_window(scal):
    col = scal[COL]
    block = jnp.minimum(col // LANES, WIDTH // LANES - 1)
    return pl.ds(pl.multiple_of(block * LANES, LANES), COL_SPAN), col - block * LANES


def take_patch(scal, band, view):
    cols, rest = column_window(scal)
    for part in range(2):
        block = band[part, :, cols]
        block = pltpu.roll(block, lax.rem(COL_SPAN - rest, COL_SPAN), 1)[:, :SIDE]
        view[part] = pltpu.roll(block, lax.rem(BAND - scal[ROW], BAND), 0)[:SLAB]


def forward(view, probe, tables, spectra):
    view_real = stacked([view[0]] * MODES)
    view_imag = stacked([view[1]] * MODES)
    probe_real = stacked(probe[mode, 0] for mode in range(MODES))
    probe_imag = stacked(probe[mode, 1] for mode in range(MODES))
    both = rows_transform(
        probe_real * view_real - probe_imag * view_imag,
        probe_real * view_imag + probe_imag * view_real,
        tables,
        1.0,
    )
    for part in range(2):
        blocks = [both[part][mode * SLAB : (mode + 1) * SLAB] for mode in range(MODES)]
        for place, block in enumerate(swap_blocks(blocks)):
            spectra[place, part] = block


def split_kernel(probe_in, pieces):
    for place in range(MODES):
        row = slab_of(place) * SLAB
        pieces[place] = probe_in[0, :, row : row + SLAB, :]


def first_kernel(scal, own, beside, probe, tables, band, view, shard, spectra):
    band[:, :, :WIDTH] = own[...]
    band[:, :, WIDTH:] = beside[...]
    take_patch(scal, band, view)
    rows = pl.ds(pl.multiple_of(scal[CORE] * 16 + scal[XLO] * 8, 8), 8)
    wanted = lax.broadcasted_iota(jnp.int32, (8, LANES), 0) == scal[RING] // 2
    second = lax.rem(scal[RING], 2) == 1
    for mode in range(MODES):
        for part in range(2):
            block = jnp.where(second, probe[mode, part, rows, LANES:], probe[mode, part, rows, :LANES])
            index = 2 * mode + part
            shard[index : index + 1] = jnp.sum(
                jnp.where(wanted, block, 0.0), axis=0, keepdims=True
            )
    forward(view, probe, tables, spectra)


def next_kernel(view, pieces, tables, probe, spectra):
    for xlo in range(2):
        for core in range(2):
            row = core * 16 + xlo * 8
            for index in range(2 * MODES):
                for half in range(2):
                    lanes = slice(half * LANES, (half + 1) * LANES)
                    piece = pieces[xlo, core, pl.ds(RINGS * half + index, 8, stride=2 * RINGS), :]
                    probe[index // 2, index % 2, row : row + 8, lanes] = piece
    forward(view, probe, tables, spectra)


def counts_kernel(scal, measured, counts, flags):
    for place, which in enumerate((LIVE, CORE, XLO)):
        flags[place] = jnp.full((8, SIDE), scal[which].astype(F32))
    block = measured[0, scal[SLOT]].astype(F32)
    block = pltpu.roll(block, lax.rem(SIDE - scal[MODE] * SLAB, SIDE), 1)[:, :LANES]
    lanes = lax.broadcasted_iota(jnp.int32, block.shape, 1)
    block = jnp.where(lanes < SLAB, block, 0.0)
    block = block + pltpu.roll(block, SLAB, 1)
    counts[...] = block + pltpu.roll(block, 2 * SLAB, 1)


def ratio_kernel(spectra, counts, flags, tables, out):
    real = stacked(spectra[slab_of(index), 0] for index in range(MODES))
    imag = stacked(spectra[slab_of(index), 1] for index in range(MODES))
    far_real, far_imag = columns_transform(real, imag, tables, 1.0)
    power = far_real * far_real + far_imag * far_imag
    total = power[:, :LANES] + power[:, LANES:]
    total = total + pltpu.roll(total, 2 * SLAB, 1)
    total = total + pltpu.roll(total, SLAB, 1)
    ratio = jnp.sqrt((counts[...] + SOFT_FLOOR) / (total + SOFT_FLOOR)) - 1.0
    ratio = ratio * flags[0, 0:1, :LANES]
    ratio = jnp.concatenate([ratio, ratio], axis=1)
    both = columns_transform(far_real * ratio, far_imag * ratio, tables, -1.0)
    for part in range(2):
        for place in range(MODES):
            row = slab_of(place) * SLAB
            out[place, part] = both[part][row : row + SLAB]


def backward_kernel(spectra, view, flags, tables, chi, keep, send):
    real = stacked(swap_blocks([spectra[place, 0] for place in range(MODES)]))
    imag = stacked(swap_blocks([spectra[place, 1] for place in range(MODES)]))
    chi_real, chi_imag = rows_transform(real, imag, tables, -1.0)
    view_real, view_imag = view[0], view[1]
    sums = []
    for mode in range(MODES):
        real = chi_real[mode * SLAB : (mode + 1) * SLAB]
        imag = chi_imag[mode * SLAB : (mode + 1) * SLAB]
        chi[mode, 0] = real
        chi[mode, 1] = imag
        sums.append(view_real * real + view_imag * imag)
        sums.append(view_real * imag - view_imag * real)
    sums.append((view_real * view_real + view_imag * view_imag) * flags[0, 0:1, :])
    second = jnp.broadcast_to(flags[1, 0:1, :], (16, SIDE)) > 0.5
    for index, value in enumerate(sums):
        keep[index] = jnp.where(second, value[16:], value[:16])
        send[index] = jnp.where(second, value[:16], value[16:])


def halve_kernel(mine, theirs, flags, keep, send):
    second = jnp.broadcast_to(flags[2, 0:1, :], (8, SIDE)) > 0.5
    for index in range(2 * MODES + 1):
        value = mine[index] + theirs[index]
        keep[index] = jnp.where(second, value[8:], value[:8])
        send[index] = jnp.where(second, value[:8], value[8:])


def pack_kernel(mine, theirs, packed):
    for index in range(MESSAGE):
        total = pltpu.roll(mine[index] + theirs[index], RINGS // 4, 0)
        for half in range(2):
            rows = pl.ds(MESSAGE * half + index, 8, stride=2 * MESSAGE)
            packed[rows, :] = total[:, half * LANES : (half + 1) * LANES]


def step_kernel(chi, probe, step):
    real = imag = light = 0.0
    for mode in range(MODES):
        probe_real, probe_imag = probe[mode, 0], probe[mode, 1]
        real = real + (probe_real * chi[mode, 0] + probe_imag * chi[mode, 1])
        imag = imag + (probe_real * chi[mode, 1] - probe_imag * chi[mode, 0])
        light = light + (probe_real * probe_real + probe_imag * probe_imag)
    step[0] = OBJECT_RATE * real / (light + OBJECT_DAMP)
    step[1] = OBJECT_RATE * imag / (light + OBJECT_DAMP)


def place_kernel(scal, above, step, below, band, part_band, to_left, to_right):
    cols, rest = column_window(scal)
    height = 3 * SLAB
    part_band[...] = jnp.zeros_like(part_band)
    for part in range(2):
        block = stacked([above[part], step[part], below[part]])
        block = pltpu.roll(block, lax.rem(2 * SLAB + scal[ROW], height), 0)[:BAND]
        block = jnp.concatenate([block, jnp.zeros((BAND, LANES), F32)], axis=1)
        part_band[part, :, cols] = pltpu.roll(block, rest, 1)
    to_left[...] = part_band[:, :, :SIDE]
    to_right[...] = part_band[:, :, WIDTH:]
    part_band[:, :, :WIDTH] = part_band[:, :, :WIDTH] + band[:, :, :WIDTH]
    part_band[:, :, WIDTH:] = (
        part_band[:, :, WIDTH:] * scal[HAS_NEXT].astype(F32) + band[:, :, WIDTH:]
    )


def view_kernel(scal, part_band, from_left, from_right, band, view):
    band[:, :, :SIDE] = part_band[:, :, :SIDE] + from_left[...]
    band[:, :, SIDE:WIDTH] = part_band[:, :, SIDE:WIDTH]
    band[:, :, WIDTH:] = part_band[:, :, WIDTH:] + from_right[...]
    take_patch(scal, band, view)


def probe_kernel(sums, shard_in, shard, copies):
    total = sums[:MESSAGE]
    for ring in range(1, RINGS):
        total = total + sums[ring * MESSAGE : (ring + 1) * MESSAGE]
    rows = 2 * MODES
    new = shard_in[...] + PROBE_RATE * total[:rows] / (total[rows:] + PROBE_DAMP)
    shard[...] = new
    for ring in range(RINGS):
        copies[ring] = new


def out_rows_kernel(scal, part_band, from_left, rows_out):
    rows = pl.ds(pl.multiple_of(scal[BAND_ID] // 2 * 8, 8), OUT_ROWS)
    rows_out[:, :, :SIDE] = part_band[:, rows, :SIDE] + from_left[:, rows, :]
    rows_out[:, :, SIDE:] = part_band[:, rows, SIDE:WIDTH]


def tail_kernel(piece, rows_out, tail):
    for place in range(MODES):
        for half in range(2):
            for part in range(2):
                row = (half * 2 + part) * 8
                rows = pl.ds(RINGS * half + 2 * place + part, 8, stride=2 * RINGS)
                tail[place, row : row + 8] = piece[rows, :]
        for part in range(2):
            for block in range(WIDTH // LANES):
                row = 32 + (part * 4 + block) * OUT_ROWS
                lanes = slice(block * LANES, (block + 1) * LANES)
                tail[place, row : row + OUT_ROWS] = rows_out[part, :, lanes]


def object_kernel(tail, object_out):
    for place in range(MODES):
        first = slab_of(place) * 9 // 2 * 8
        for part in range(2):
            for block in range(WIDTH // LANES):
                row = 32 + (part * 4 + block) * OUT_ROWS
                lanes = slice(block * LANES, (block + 1) * LANES)
                object_out[part, first : first + OUT_ROWS, lanes] = tail[
                    place, row : row + OUT_ROWS
                ]


def probe_out_kernel(pieces, probe_out):
    for xlo in range(2):
        for core in range(2):
            for place in range(MODES):
                first = slab_of(place) * SLAB + core * 16 + xlo * 8
                for half in range(2):
                    lanes = slice(half * LANES, (half + 1) * LANES)
                    for part in range(2):
                        row = (half * 2 + part) * 8
                        probe_out[0, part, first : first + 8, lanes] = pieces[
                            xlo, core, place, row : row + 8
                        ]


def own_kernel(place, whole, own, left, sems):
    rows = pl.ds(pl.multiple_of(place[0] * SLAB, SLAB), BAND)
    first = pltpu.make_async_copy(whole.at[:, rows, :], own, sems.at[0])
    second = pltpu.make_async_copy(whole.at[:, rows, pl.ds(0, SIDE)], left, sems.at[1])
    first.start()
    second.start()
    first.wait()
    second.wait()


def take_own(mode, object_tiles, after):
    vmem = pl.BlockSpec(memory_space=pltpu.VMEM)
    anywhere = pl.BlockSpec(memory_space=pl.ANY)

    def body(place, whole, _, own, left, sems):
        own_kernel(place, whole, own, left, sems)

    return pl.pallas_call(
        body,
        out_shape=[
            jax.ShapeDtypeStruct((2, BAND, WIDTH), F32),
            jax.ShapeDtypeStruct((2, BAND, SIDE), F32),
        ],
        in_specs=[pl.BlockSpec(memory_space=pltpu.SMEM), anywhere, anywhere],
        out_specs=[vmem, vmem],
        scratch_shapes=[pltpu.SemaphoreType.DMA((2,))],
        compiler_params=pltpu.CompilerParams(vmem_limit_bytes=VMEM_LIMIT),
        name="own_kernel",
    )(mode.astype(jnp.int32).reshape(1), object_tiles, after)


def call(kernel, outs, *args, scalars=True, after=()):
    vmem = pl.BlockSpec(memory_space=pltpu.VMEM)
    in_specs = [vmem] * len(args) + [pl.BlockSpec(memory_space=pl.ANY)] * len(after)

    def body(*refs):
        taken = list(refs[: len(args)])
        if scalars:
            taken[0] = [taken[0][0, index] for index in range(BAND_ID + 1)]
        kernel(*taken, *refs[len(args) + len(after) :])

    return pl.pallas_call(
        body,
        out_shape=[jax.ShapeDtypeStruct(shape, F32) for shape in outs],
        in_specs=in_specs,
        out_specs=[vmem] * len(outs),
        compiler_params=pltpu.CompilerParams(vmem_limit_bytes=VMEM_LIMIT),
        name=kernel.__name__,
    )(*args, *after)


def shift(value, axes, count, steps):
    first, last = max(0, -steps), min(count, count - steps)
    return lax.ppermute(value, axes, [(i, i + steps) for i in range(first, last)])


def other(value, axis):
    return lax.ppermute(value, axis, [(0, 1), (1, 0)])


def beside_slab(value, steps):
    first, last = max(0, -steps), min(MODES, MODES - steps)
    pairs = [(slab_of(i), slab_of(i + steps)) for i in range(first, last)]
    return lax.ppermute(value, MODE_AXES, pairs)


def exchange_rings(value):
    groups = [[(ring + RINGS // 2) % RINGS for ring in range(RINGS)]]
    value = value.reshape(RINGS, 1, MESSAGE * LANES)
    value = lax.all_to_all(value, "z", 0, 0, tiled=True, axis_index_groups=groups)
    return value.reshape(RINGS * MESSAGE, LANES)


def exchange(value, axes):
    return lax.all_to_all(value, axes, 0, 0, tiled=True)


def gather_pieces(piece):
    gathered = lax.all_gather(piece, ("xlo", "core"))
    return gathered.reshape((2, 2) + piece.shape)


def per_device(
    object_tiles, probe_modes, measured, row_offset, col_offset, live_counts, visit_order
):
    tables = jnp.asarray(fourier_tables())
    slots = visit_order[0]
    tile = lax.axis_index(TILE_AXES)
    mode = lax.axis_index(MODE_AXES)
    slab = jnp.where(mode < MODES // 2, mode, 11 - mode)
    (pieces,) = call(split_kernel, [(MODES, 2, SLAB, SIDE)], probe_modes, scalars=False)
    probe = exchange(pieces, MODE_AXES)
    own, left = take_own(slab, object_tiles, pieces)
    beside = shift(left, TILE_AXES, TILES, -1)
    places = [
        mode,
        lax.axis_index("core"),
        lax.axis_index("xlo"),
        lax.axis_index("z"),
        (tile < TILES - 1).astype(jnp.int32),
        slab,
    ]
    chosen = slots[:, None] == jnp.arange(STEPS, dtype=jnp.int32)[None, :]
    per_step = [
        jnp.sum(jnp.where(chosen, row_offset, 0), axis=1),
        jnp.sum(jnp.where(chosen, col_offset, 0), axis=1),
        slots,
        (slots < live_counts[0]).astype(jnp.int32),
    ]
    scalars = jnp.stack(
        per_step + [jnp.broadcast_to(place, (STEPS,)) for place in places], axis=1
    )
    slabs = (MODES, 2, SLAB, SIDE)
    slab_pair = (2, SLAB, SIDE)
    band_shape = (2, BAND, WIDE)
    edge = (2, BAND, SIDE)
    counts_shapes = [(SIDE, LANES), (3, 8, SIDE)]
    counts, flags = call(counts_kernel, counts_shapes, scalars[:1], measured)
    for step in range(STEPS):
        scal = scalars[step : step + 1]
        final = step == STEPS - 1
        if step == 0:
            band, view, shard, spectra = call(
                first_kernel,
                [band_shape, slab_pair, (2 * MODES, LANES), slabs],
                scal,
                own,
                beside,
                probe,
                tables,
                after=(counts,),
            )
        else:
            probe, spectra = call(
                next_kernel,
                [slabs, slabs],
                view,
                pieces,
                tables,
                scalars=False,
                after=(counts,),
            )
        spectra = exchange(spectra, MODE_AXES)
        (spectra,) = call(
            ratio_kernel, [slabs], spectra, counts, flags, tables, scalars=False
        )
        spectra = exchange(spectra, MODE_AXES)
        chi, keep, send = call(
            backward_kernel,
            [slabs] + [(2 * MODES + 1, 16, SIDE)] * 2,
            spectra,
            view,
            flags,
            tables,
            scalars=False,
        )
        received = other(send, "core")
        keep, send = call(
            halve_kernel, [(2 * MODES + 1, 8, SIDE)] * 2, keep, received, flags, scalars=False
        )
        received = other(send, "xlo")
        (object_step,) = call(
            step_kernel, [slab_pair], chi, probe, scalars=False, after=(keep,)
        )
        above = beside_slab(object_step, 1)
        below = beside_slab(object_step, -1)
        (packed,) = call(
            pack_kernel,
            [(RINGS * MESSAGE, LANES)],
            keep,
            received,
            scalars=False,
            after=(above, below) if final else (object_step,),
        )
        sums = exchange_rings(packed)
        placing = [scal, above, object_step, below, band]
        if final:
            part_band, _, to_right = call(
                place_kernel, [band_shape, edge, edge], *placing, after=(packed,)
            )
            from_left = shift(to_right, TILE_AXES, TILES, 1)
            (rows_out,) = call(
                out_rows_kernel, [(2, OUT_ROWS, WIDTH)], scal, part_band, from_left
            )
            before = (rows_out,)
        else:
            next_scal = scalars[step + 1 : step + 2]
            counts, flags = call(
                counts_kernel, counts_shapes, next_scal, measured, after=(packed,)
            )
            before = (above, below, counts)
        shard, shards = call(
            probe_kernel,
            [(2 * MODES, LANES), (RINGS, 2 * MODES, LANES)],
            sums,
            shard,
            scalars=False,
            after=before,
        )
        piece = exchange(shards, "z")
        if not final:
            part_band, to_left, to_right = call(
                place_kernel, [band_shape, edge, edge], *placing, after=(shards,)
            )
            from_left = shift(to_right, TILE_AXES, TILES, 1)
            from_right = shift(to_left, TILE_AXES, TILES, -1)
            band, view = call(
                view_kernel,
                [band_shape, slab_pair],
                next_scal,
                part_band,
                from_left,
                from_right,
            )
            piece, view = lax.optimization_barrier((piece, view))
            pieces = gather_pieces(piece.reshape(2 * MODES * RINGS, LANES))
    tail_rows = 32 + 8 * OUT_ROWS
    (tail,) = call(
        tail_kernel,
        [(MODES, tail_rows, LANES)],
        piece.reshape(2 * MODES * RINGS, LANES),
        rows_out,
        scalars=False,
    )
    tail = exchange(tail, MODE_AXES)
    pieces = gather_pieces(tail[:, :32])
    (object_out,) = call(object_kernel, [(2, HEIGHT, WIDTH)], tail, scalars=False)
    (probe_out,) = call(probe_out_kernel, [(1, 2, SIDE, SIDE)], pieces, scalars=False)
    return object_out, probe_out


def solution(mesh):
    grid = Mesh(mesh.devices.reshape(2, 16, 2, 2, 4), TILE_AXES + MODE_AXES)
    return jax.shard_map(
        per_device,
        mesh=grid,
        in_specs=(
            P(None, None, TILE_AXES),
            P(MODE_AXES, None, None, None),
            P(TILE_AXES, None, None, None),
            P(TILE_AXES, None),
            P(TILE_AXES, None),
            P(TILE_AXES),
            P(TILE_AXES, None),
        ),
        out_specs=(P(None, None, TILE_AXES), P(MODE_AXES, None, None, None)),
        check_vma=False,
    )
```

```python
import math

import jax
import jax.numpy as jnp
import numpy as np
from jax import lax
from jax.experimental import pallas as pl
from jax.experimental.pallas import tpu as pltpu
from jax.sharding import Mesh
from jax.sharding import PartitionSpec as P

SOFT_FLOOR = 0.5
OBJECT_RATE = 1.0
OBJECT_DAMP = 0.5
PROBE_RATE = 1.0
PROBE_DAMP = 1.0

SIDE = 256
HEIGHT = 288
WIDTH = 512
WIDE = WIDTH + SIDE
MODES = 8
SLAB = SIDE // MODES
BAND = 2 * SLAB
STEPS = 3
TILES = 64
RINGS = 16
LANES = 128
COL_SPAN = SIDE + LANES
OUT_ROWS = 40
MESSAGE = 2 * MODES + 1
VMEM_LIMIT = 16 * 1024 * 1024

TILE_AXES = ("xlo", "z", "core")
MODE_AXES = ("xhi", "y")

ROW, COL, SLOT, LIVE, MODE, CORE, XLO, RING, HAS_NEXT, BAND_ID = range(10)

F32 = jnp.float32
BF16 = jnp.bfloat16


def slab_of(place):
    return place if place < MODES // 2 else 11 - place


def fourier_tables():
    index = np.arange(SIDE)
    angles = (index[:, None] * index[None, :] % SIDE) * (2.0 * math.pi / SIDE)
    cosine, sine = np.cos(angles) / math.sqrt(SIDE), np.sin(angles) / math.sqrt(SIDE)
    exact = np.stack([cosine, cosine + sine, cosine - sine])
    high = exact.astype(jnp.bfloat16)
    low = (exact - high.astype(np.float64)).astype(jnp.bfloat16)
    return np.stack([high, low], axis=1)


def halves(value):
    high = value.astype(BF16)
    return high, (value - high.astype(F32)).astype(BF16)


def dot(left, right):
    return jnp.dot(left, right, preferred_element_type=F32)


def transform(real, imag, by, direction):
    turned = direction * imag
    shared = by(0, real + turned)
    return shared - by(2, turned), direction * (shared - by(1, real))


def rows_transform(real, imag, tables, direction):
    def by(which, value):
        high, low = halves(value)
        return (
            dot(high, tables[which, 0]) + dot(low, tables[which, 0]) + dot(high, tables[which, 1])
        )

    return transform(real, imag, by, direction)


def columns_transform(real, imag, tables, direction):
    def by(which, value):
        high, low = halves(value)
        return (
            dot(tables[which, 0], high) + dot(tables[which, 0], low) + dot(tables[which, 1], high)
        )

    return transform(real, imag, by, direction)


def swap_blocks(parts):
    lanes = lax.broadcasted_iota(jnp.int32, (parts[0].shape[0], LANES), 1)
    grid = [[part[:, :LANES], part[:, LANES:]] for part in parts]
    grid = [[grid[(m & 3) | (h << 2)][m >> 2] for h in range(2)] for m in range(MODES)]
    for bit in (2, 1):
        shift = bit * SLAB
        low = (lanes & shift) == 0
        new = [None] * MODES
        for m in range(MODES):
            if m & bit:
                continue
            a, b = grid[m], grid[m | bit]
            new[m] = [jnp.where(low, a[h], pltpu.roll(b[h], shift, 1)) for h in range(2)]
            new[m | bit] = [
                jnp.where(low, pltpu.roll(a[h], LANES - shift, 1), b[h]) for h in range(2)
            ]
        grid = new
    return [jnp.concatenate(pair, axis=1) for pair in grid]


def stacked(pieces):
    return jnp.concatenate(list(pieces), axis=0)


def column_window(scal):
    col = scal[COL]
    block = jnp.minimum(col // LANES, WIDTH // LANES - 1)
    return pl.ds(pl.multiple_of(block * LANES, LANES), COL_SPAN), col - block * LANES


def take_patch(scal, band, view):
    cols, rest = column_window(scal)
    for part in range(2):
        block = band[part, :, cols]
        block = pltpu.roll(block, lax.rem(COL_SPAN - rest, COL_SPAN), 1)[:, :SIDE]
        view[part] = pltpu.roll(block, lax.rem(BAND - scal[ROW], BAND), 0)[:SLAB]


def forward(view, probe, tables, spectra):
    view_real = stacked([view[0]] * MODES)
    view_imag = stacked([view[1]] * MODES)
    probe_real = stacked(probe[mode, 0] for mode in range(MODES))
    probe_imag = stacked(probe[mode, 1] for mode in range(MODES))
    both = rows_transform(
        probe_real * view_real - probe_imag * view_imag,
        probe_real * view_imag + probe_imag * view_real,
        tables,
        1.0,
    )
    for part in range(2):
        blocks = [both[part][mode * SLAB : (mode + 1) * SLAB] for mode in range(MODES)]
        for place, block in enumerate(swap_blocks(blocks)):
            spectra[place, part] = block


def split_kernel(probe_in, pieces):
    for place in range(MODES):
        row = slab_of(place) * SLAB
        pieces[place] = probe_in[0, :, row : row + SLAB, :]


def first_kernel(scal, own, beside, probe, tables, band, view, shard, spectra):
    band[:, :, :WIDTH] = own[...]
    band[:, :, WIDTH:] = beside[...]
    take_patch(scal, band, view)
    rows = pl.ds(pl.multiple_of(scal[CORE] * 16 + scal[XLO] * 8, 8), 8)
    wanted = lax.broadcasted_iota(jnp.int32, (8, LANES), 0) == scal[RING] // 2
    second = lax.rem(scal[RING], 2) == 1
    for mode in range(MODES):
        for part in range(2):
            block = jnp.where(second, probe[mode, part, rows, LANES:], probe[mode, part, rows, :LANES])
            index = 2 * mode + part
            shard[index : index + 1] = jnp.sum(
                jnp.where(wanted, block, 0.0), axis=0, keepdims=True
            )
    forward(view, probe, tables, spectra)


def next_kernel(view, pieces, tables, probe, spectra):
    for xlo in range(2):
        for core in range(2):
            row = core * 16 + xlo * 8
            for index in range(2 * MODES):
                for half in range(2):
                    lanes = slice(half * LANES, (half + 1) * LANES)
                    piece = pieces[xlo, core, pl.ds(RINGS * half + index, 8, stride=2 * RINGS), :]
                    probe[index // 2, index % 2, row : row + 8, lanes] = piece
    forward(view, probe, tables, spectra)


def counts_kernel(scal, measured, counts, flags):
    for place, which in enumerate((LIVE, CORE, XLO)):
        flags[place] = jnp.full((8, SIDE), scal[which].astype(F32))
    block = measured[0, scal[SLOT]].astype(F32)
    block = pltpu.roll(block, lax.rem(SIDE - scal[MODE] * SLAB, SIDE), 1)[:, :LANES]
    lanes = lax.broadcasted_iota(jnp.int32, block.shape, 1)
    block = jnp.where(lanes < SLAB, block, 0.0)
    block = block + pltpu.roll(block, SLAB, 1)
    counts[...] = block + pltpu.roll(block, 2 * SLAB, 1)


def ratio_kernel(spectra, counts, flags, tables, out):
    real = stacked(spectra[slab_of(index), 0] for index in range(MODES))
    imag = stacked(spectra[slab_of(index), 1] for index in range(MODES))
    far_real, far_imag = columns_transform(real, imag, tables, 1.0)
    power = far_real * far_real + far_imag * far_imag
    total = power[:, :LANES] + power[:, LANES:]
    total = total + pltpu.roll(total, 2 * SLAB, 1)
    total = total + pltpu.roll(total, SLAB, 1)
    ratio = jnp.sqrt((counts[...] + SOFT_FLOOR) / (total + SOFT_FLOOR)) - 1.0
    ratio = ratio * flags[0, 0:1, :LANES]
    ratio = jnp.concatenate([ratio, ratio], axis=1)
    both = columns_transform(far_real * ratio, far_imag * ratio, tables, -1.0)
    for part in range(2):
        for place in range(MODES):
            row = slab_of(place) * SLAB
            out[place, part] = both[part][row : row + SLAB]


def backward_kernel(spectra, view, flags, tables, chi, keep, send):
    real = stacked(swap_blocks([spectra[place, 0] for place in range(MODES)]))
    imag = stacked(swap_blocks([spectra[place, 1] for place in range(MODES)]))
    chi_real, chi_imag = rows_transform(real, imag, tables, -1.0)
    view_real, view_imag = view[0], view[1]
    sums = []
    for mode in range(MODES):
        real = chi_real[mode * SLAB : (mode + 1) * SLAB]
        imag = chi_imag[mode * SLAB : (mode + 1) * SLAB]
        chi[mode, 0] = real
        chi[mode, 1] = imag
        sums.append(view_real * real + view_imag * imag)
        sums.append(view_real * imag - view_imag * real)
    sums.append((view_real * view_real + view_imag * view_imag) * flags[0, 0:1, :])
    second = jnp.broadcast_to(flags[1, 0:1, :], (16, SIDE)) > 0.5
    for index, value in enumerate(sums):
        keep[index] = jnp.where(second, value[16:], value[:16])
        send[index] = jnp.where(second, value[:16], value[16:])


def halve_kernel(mine, theirs, flags, keep, send):
    second = jnp.broadcast_to(flags[2, 0:1, :], (8, SIDE)) > 0.5
    for index in range(2 * MODES + 1):
        value = mine[index] + theirs[index]
        keep[index] = jnp.where(second, value[8:], value[:8])
        send[index] = jnp.where(second, value[:8], value[8:])


def pack_kernel(mine, theirs, packed):
    for index in range(MESSAGE):
        total = pltpu.roll(mine[index] + theirs[index], RINGS // 4, 0)
        for half in range(2):
            rows = pl.ds(MESSAGE * half + index, 8, stride=2 * MESSAGE)
            packed[rows, :] = total[:, half * LANES : (half + 1) * LANES]


def step_kernel(chi, probe, step):
    real = imag = light = 0.0
    for mode in range(MODES):
        probe_real, probe_imag = probe[mode, 0], probe[mode, 1]
        real = real + (probe_real * chi[mode, 0] + probe_imag * chi[mode, 1])
        imag = imag + (probe_real * chi[mode, 1] - probe_imag * chi[mode, 0])
        light = light + (probe_real * probe_real + probe_imag * probe_imag)
    step[0] = OBJECT_RATE * real / (light + OBJECT_DAMP)
    step[1] = OBJECT_RATE * imag / (light + OBJECT_DAMP)


def place_kernel(scal, above, step, below, band, part_band, to_left, to_right):
    cols, rest = column_window(scal)
    height = 3 * SLAB
    part_band[...] = jnp.zeros_like(part_band)
    for part in range(2):
        block = stacked([above[part], step[part], below[part]])
        block = pltpu.roll(block, lax.rem(2 * SLAB + scal[ROW], height), 0)[:BAND]
        block = jnp.concatenate([block, jnp.zeros((BAND, LANES), F32)], axis=1)
        part_band[part, :, cols] = pltpu.roll(block, rest, 1)
    to_left[...] = part_band[:, :, :SIDE]
    to_right[...] = part_band[:, :, WIDTH:]
    part_band[:, :, :WIDTH] = part_band[:, :, :WIDTH] + band[:, :, :WIDTH]
    part_band[:, :, WIDTH:] = (
        part_band[:, :, WIDTH:] * scal[HAS_NEXT].astype(F32) + band[:, :, WIDTH:]
    )


def view_kernel(scal, part_band, from_left, from_right, band, view):
    band[:, :, :SIDE] = part_band[:, :, :SIDE] + from_left[...]
    band[:, :, SIDE:WIDTH] = part_band[:, :, SIDE:WIDTH]
    band[:, :, WIDTH:] = part_band[:, :, WIDTH:] + from_right[...]
    take_patch(scal, band, view)


def probe_kernel(sums, shard_in, shard, copies):
    total = sums[:MESSAGE]
    for ring in range(1, RINGS):
        total = total + sums[ring * MESSAGE : (ring + 1) * MESSAGE]
    rows = 2 * MODES
    new = shard_in[...] + PROBE_RATE * total[:rows] / (total[rows:] + PROBE_DAMP)
    shard[...] = new
    for ring in range(RINGS):
        copies[ring] = new


def out_rows_kernel(scal, part_band, from_left, rows_out):
    rows = pl.ds(pl.multiple_of(scal[BAND_ID] // 2 * 8, 8), OUT_ROWS)
    rows_out[:, :, :SIDE] = part_band[:, rows, :SIDE] + from_left[:, rows, :]
    rows_out[:, :, SIDE:] = part_band[:, rows, SIDE:WIDTH]


def tail_kernel(piece, rows_out, tail):
    for place in range(MODES):
        for half in range(2):
            for part in range(2):
                row = (half * 2 + part) * 8
                rows = pl.ds(RINGS * half + 2 * place + part, 8, stride=2 * RINGS)
                tail[place, row : row + 8] = piece[rows, :]
        for part in range(2):
            for block in range(WIDTH // LANES):
                row = 32 + (part * 4 + block) * OUT_ROWS
                lanes = slice(block * LANES, (block + 1) * LANES)
                tail[place, row : row + OUT_ROWS] = rows_out[part, :, lanes]


def object_kernel(tail, object_out):
    for place in range(MODES):
        first = slab_of(place) * 9 // 2 * 8
        for part in range(2):
            for block in range(WIDTH // LANES):
                row = 32 + (part * 4 + block) * OUT_ROWS
                lanes = slice(block * LANES, (block + 1) * LANES)
                object_out[part, first : first + OUT_ROWS, lanes] = tail[
                    place, row : row + OUT_ROWS
                ]


def probe_out_kernel(pieces, probe_out):
    for xlo in range(2):
        for core in range(2):
            for place in range(MODES):
                first = slab_of(place) * SLAB + core * 16 + xlo * 8
                for half in range(2):
                    lanes = slice(half * LANES, (half + 1) * LANES)
                    for part in range(2):
                        row = (half * 2 + part) * 8
                        probe_out[0, part, first : first + 8, lanes] = pieces[
                            xlo, core, place, row : row + 8
                        ]


def own_kernel(place, whole, own, left, sems):
    rows = pl.ds(pl.multiple_of(place[0] * SLAB, SLAB), BAND)
    first = pltpu.make_async_copy(whole.at[:, rows, :], own, sems.at[0])
    second = pltpu.make_async_copy(whole.at[:, rows, pl.ds(0, SIDE)], left, sems.at[1])
    first.start()
    second.start()
    first.wait()
    second.wait()


def take_own(mode, object_tiles, after):
    vmem = pl.BlockSpec(memory_space=pltpu.VMEM)
    anywhere = pl.BlockSpec(memory_space=pl.ANY)

    def body(place, whole, _, own, left, sems):
        own_kernel(place, whole, own, left, sems)

    return pl.pallas_call(
        body,
        out_shape=[
            jax.ShapeDtypeStruct((2, BAND, WIDTH), F32),
            jax.ShapeDtypeStruct((2, BAND, SIDE), F32),
        ],
        in_specs=[pl.BlockSpec(memory_space=pltpu.SMEM), anywhere, anywhere],
        out_specs=[vmem, vmem],
        scratch_shapes=[pltpu.SemaphoreType.DMA((2,))],
        compiler_params=pltpu.CompilerParams(vmem_limit_bytes=VMEM_LIMIT),
        name="own_kernel",
    )(mode.astype(jnp.int32).reshape(1), object_tiles, after)


def call(kernel, outs, *args, scalars=True, after=()):
    vmem = pl.BlockSpec(memory_space=pltpu.VMEM)
    in_specs = [vmem] * len(args) + [pl.BlockSpec(memory_space=pl.ANY)] * len(after)

    def body(*refs):
        taken = list(refs[: len(args)])
        if scalars:
            taken[0] = [taken[0][0, index] for index in range(BAND_ID + 1)]
        kernel(*taken, *refs[len(args) + len(after) :])

    return pl.pallas_call(
        body,
        out_shape=[jax.ShapeDtypeStruct(shape, F32) for shape in outs],
        in_specs=in_specs,
        out_specs=[vmem] * len(outs),
        compiler_params=pltpu.CompilerParams(vmem_limit_bytes=VMEM_LIMIT),
        name=kernel.__name__,
    )(*args, *after)


def shift(value, axes, count, steps):
    first, last = max(0, -steps), min(count, count - steps)
    return lax.ppermute(value, axes, [(i, i + steps) for i in range(first, last)])


def other(value, axis):
    return lax.ppermute(value, axis, [(0, 1), (1, 0)])


def beside_slab(value, steps):
    first, last = max(0, -steps), min(MODES, MODES - steps)
    pairs = [(slab_of(i), slab_of(i + steps)) for i in range(first, last)]
    return lax.ppermute(value, MODE_AXES, pairs)


def exchange_rings(value):
    groups = [[(ring + RINGS // 2) % RINGS for ring in range(RINGS)]]
    value = value.reshape(RINGS, 1, MESSAGE * LANES)
    value = lax.all_to_all(value, "z", 0, 0, tiled=True, axis_index_groups=groups)
    return value.reshape(RINGS * MESSAGE, LANES)


def exchange(value, axes):
    return lax.all_to_all(value, axes, 0, 0, tiled=True)


def gather_pieces(piece):
    gathered = lax.all_gather(piece, ("xlo", "core"))
    return gathered.reshape((2, 2) + piece.shape)


def per_device(
    object_tiles, probe_modes, measured, row_offset, col_offset, live_counts, visit_order
):
    tables = jnp.asarray(fourier_tables())
    slots = visit_order[0]
    tile = lax.axis_index(TILE_AXES)
    mode = lax.axis_index(MODE_AXES)
    slab = jnp.where(mode < MODES // 2, mode, 11 - mode)
    (pieces,) = call(split_kernel, [(MODES, 2, SLAB, SIDE)], probe_modes, scalars=False)
    probe = exchange(pieces, MODE_AXES)
    own, left = take_own(slab, object_tiles, pieces)
    beside = shift(left, TILE_AXES, TILES, -1)
    places = [
        mode,
        lax.axis_index("core"),
        lax.axis_index("xlo"),
        lax.axis_index("z"),
        (tile < TILES - 1).astype(jnp.int32),
        slab,
    ]
    chosen = slots[:, None] == jnp.arange(STEPS, dtype=jnp.int32)[None, :]
    per_step = [
        jnp.sum(jnp.where(chosen, row_offset, 0), axis=1),
        jnp.sum(jnp.where(chosen, col_offset, 0), axis=1),
        slots,
        (slots < live_counts[0]).astype(jnp.int32),
    ]
    scalars = jnp.stack(
        per_step + [jnp.broadcast_to(place, (STEPS,)) for place in places], axis=1
    )
    slabs = (MODES, 2, SLAB, SIDE)
    slab_pair = (2, SLAB, SIDE)
    band_shape = (2, BAND, WIDE)
    edge = (2, BAND, SIDE)
    counts_shapes = [(SIDE, LANES), (3, 8, SIDE)]
    counts, flags = call(counts_kernel, counts_shapes, scalars[:1], measured)
    for step in range(STEPS):
        scal = scalars[step : step + 1]
        final = step == STEPS - 1
        if step == 0:
            band, view, shard, spectra = call(
                first_kernel,
                [band_shape, slab_pair, (2 * MODES, LANES), slabs],
                scal,
                own,
                beside,
                probe,
                tables,
                after=(counts,),
            )
        else:
            probe, spectra = call(
                next_kernel,
                [slabs, slabs],
                view,
                pieces,
                tables,
                scalars=False,
                after=(counts,),
            )
        spectra = exchange(spectra, MODE_AXES)
        (spectra,) = call(
            ratio_kernel, [slabs], spectra, counts, flags, tables, scalars=False
        )
        spectra = exchange(spectra, MODE_AXES)
        chi, keep, send = call(
            backward_kernel,
            [slabs] + [(2 * MODES + 1, 16, SIDE)] * 2,
            spectra,
            view,
            flags,
            tables,
            scalars=False,
        )
        received = other(send, "core")
        keep, send = call(
            halve_kernel, [(2 * MODES + 1, 8, SIDE)] * 2, keep, received, flags, scalars=False
        )
        received = other(send, "xlo")
        (object_step,) = call(
            step_kernel, [slab_pair], chi, probe, scalars=False, after=(keep,)
        )
        above = beside_slab(object_step, 1)
        below = beside_slab(object_step, -1)
        if not final:
            next_scal = scalars[step + 1 : step + 2]
            counts, flags = call(
                counts_kernel, counts_shapes, next_scal, measured, after=(keep,)
            )
        (packed,) = call(
            pack_kernel,
            [(RINGS * MESSAGE, LANES)],
            keep,
            received,
            scalars=False,
            after=(above, below) if final else (object_step, counts),
        )
        sums = exchange_rings(packed)
        placing = [scal, above, object_step, below, band]
        if final:
            part_band, _, to_right = call(
                place_kernel, [band_shape, edge, edge], *placing, after=(packed,)
            )
            from_left = shift(to_right, TILE_AXES, TILES, 1)
            (rows_out,) = call(
                out_rows_kernel, [(2, OUT_ROWS, WIDTH)], scal, part_band, from_left
            )
            before = (rows_out,)
        else:
            before = (above, below)
        shard, shards = call(
            probe_kernel,
            [(2 * MODES, LANES), (RINGS, 2 * MODES, LANES)],
            sums,
            shard,
            scalars=False,
            after=before,
        )
        piece = exchange(shards, "z")
        if not final:
            part_band, to_left, to_right = call(
                place_kernel, [band_shape, edge, edge], *placing, after=(shards,)
            )
            from_left = shift(to_right, TILE_AXES, TILES, 1)
            from_right = shift(to_left, TILE_AXES, TILES, -1)
            band, view = call(
                view_kernel,
                [band_shape, slab_pair],
                next_scal,
                part_band,
                from_left,
                from_right,
            )
            piece, view = lax.optimization_barrier((piece, view))
            pieces = gather_pieces(piece.reshape(2 * MODES * RINGS, LANES))
    tail_rows = 32 + 8 * OUT_ROWS
    (tail,) = call(
        tail_kernel,
        [(MODES, tail_rows, LANES)],
        piece.reshape(2 * MODES * RINGS, LANES),
        rows_out,
        scalars=False,
    )
    tail = exchange(tail, MODE_AXES)
    pieces = gather_pieces(tail[:, :32])
    (object_out,) = call(object_kernel, [(2, HEIGHT, WIDTH)], tail, scalars=False)
    (probe_out,) = call(probe_out_kernel, [(1, 2, SIDE, SIDE)], pieces, scalars=False)
    return object_out, probe_out


def solution(mesh):
    grid = Mesh(mesh.devices.reshape(2, 16, 2, 2, 4), TILE_AXES + MODE_AXES)
    return jax.shard_map(
        per_device,
        mesh=grid,
        in_specs=(
            P(None, None, TILE_AXES),
            P(MODE_AXES, None, None, None),
            P(TILE_AXES, None, None, None),
            P(TILE_AXES, None),
            P(TILE_AXES, None),
            P(TILE_AXES),
            P(TILE_AXES, None),
        ),
        out_specs=(P(None, None, TILE_AXES), P(MODE_AXES, None, None, None)),
        check_vma=False,
    )
```

```python
import math

import jax
import jax.numpy as jnp
import numpy as np
from jax import lax
from jax.experimental import pallas as pl
from jax.experimental.pallas import tpu as pltpu
from jax.sharding import Mesh
from jax.sharding import PartitionSpec as P

SOFT_FLOOR = 0.5
OBJECT_RATE = 1.0
OBJECT_DAMP = 0.5
PROBE_RATE = 1.0
PROBE_DAMP = 1.0

SIDE = 256
HEIGHT = 288
WIDTH = 512
WIDE = WIDTH + SIDE
MODES = 8
SLAB = SIDE // MODES
BAND = 2 * SLAB
STEPS = 3
TILES = 64
RINGS = 16
LANES = 128
COL_SPAN = SIDE + LANES
OUT_ROWS = 40
MESSAGE = 2 * MODES + 1
VMEM_LIMIT = 16 * 1024 * 1024

TILE_AXES = ("xlo", "z", "core")
MODE_AXES = ("xhi", "y")

ROW, COL, SLOT, LIVE, MODE, CORE, XLO, RING, HAS_NEXT, BAND_ID = range(10)

F32 = jnp.float32
BF16 = jnp.bfloat16


def slab_of(place):
    return place if place < MODES // 2 else 11 - place


def fourier_tables():
    index = np.arange(SIDE)
    angles = (index[:, None] * index[None, :] % SIDE) * (2.0 * math.pi / SIDE)
    cosine, sine = np.cos(angles) / math.sqrt(SIDE), np.sin(angles) / math.sqrt(SIDE)
    exact = np.stack([cosine, cosine + sine, cosine - sine])
    high = exact.astype(jnp.bfloat16)
    low = (exact - high.astype(np.float64)).astype(jnp.bfloat16)
    return np.stack([high, low], axis=1)


def halves(value):
    high = value.astype(BF16)
    return high, (value - high.astype(F32)).astype(BF16)


def dot(left, right):
    return jnp.dot(left, right, preferred_element_type=F32)


def transform(real, imag, by, direction):
    turned = direction * imag
    shared = by(0, real + turned)
    return shared - by(2, turned), direction * (shared - by(1, real))


def rows_transform(real, imag, tables, direction):
    def by(which, value):
        high, low = halves(value)
        return (
            dot(high, tables[which, 0]) + dot(low, tables[which, 0]) + dot(high, tables[which, 1])
        )

    return transform(real, imag, by, direction)


def columns_transform(real, imag, tables, direction):
    def by(which, value):
        high, low = halves(value)
        return (
            dot(tables[which, 0], high) + dot(tables[which, 0], low) + dot(tables[which, 1], high)
        )

    return transform(real, imag, by, direction)


def swap_blocks(parts):
    lanes = lax.broadcasted_iota(jnp.int32, (parts[0].shape[0], LANES), 1)
    grid = [[part[:, :LANES], part[:, LANES:]] for part in parts]
    grid = [[grid[(m & 3) | (h << 2)][m >> 2] for h in range(2)] for m in range(MODES)]
    for bit in (2, 1):
        shift = bit * SLAB
        low = (lanes & shift) == 0
        new = [None] * MODES
        for m in range(MODES):
            if m & bit:
                continue
            a, b = grid[m], grid[m | bit]
            new[m] = [jnp.where(low, a[h], pltpu.roll(b[h], shift, 1)) for h in range(2)]
            new[m | bit] = [
                jnp.where(low, pltpu.roll(a[h], LANES - shift, 1), b[h]) for h in range(2)
            ]
        grid = new
    return [jnp.concatenate(pair, axis=1) for pair in grid]


def stacked(pieces):
    return jnp.concatenate(list(pieces), axis=0)


def column_window(scal):
    col = scal[COL]
    block = jnp.minimum(col // LANES, WIDTH // LANES - 1)
    return pl.ds(pl.multiple_of(block * LANES, LANES), COL_SPAN), col - block * LANES


def take_patch(scal, band, view):
    cols, rest = column_window(scal)
    for part in range(2):
        block = band[part, :, cols]
        block = pltpu.roll(block, lax.rem(COL_SPAN - rest, COL_SPAN), 1)[:, :SIDE]
        view[part] = pltpu.roll(block, lax.rem(BAND - scal[ROW], BAND), 0)[:SLAB]


def forward(view, probe, tables, spectra):
    view_real = stacked([view[0]] * MODES)
    view_imag = stacked([view[1]] * MODES)
    probe_real = stacked(probe[mode, 0] for mode in range(MODES))
    probe_imag = stacked(probe[mode, 1] for mode in range(MODES))
    both = rows_transform(
        probe_real * view_real - probe_imag * view_imag,
        probe_real * view_imag + probe_imag * view_real,
        tables,
        1.0,
    )
    for part in range(2):
        blocks = [both[part][mode * SLAB : (mode + 1) * SLAB] for mode in range(MODES)]
        for place, block in enumerate(swap_blocks(blocks)):
            spectra[place, part] = block


def split_kernel(probe_in, pieces):
    for place in range(MODES):
        row = slab_of(place) * SLAB
        pieces[place] = probe_in[0, :, row : row + SLAB, :]


def first_kernel(scal, own, beside, probe, tables, band, view, shard, spectra):
    band[:, :, :WIDTH] = own[...]
    band[:, :, WIDTH:] = beside[...]
    take_patch(scal, band, view)
    rows = pl.ds(pl.multiple_of(scal[CORE] * 16 + scal[XLO] * 8, 8), 8)
    wanted = lax.broadcasted_iota(jnp.int32, (8, LANES), 0) == scal[RING] // 2
    second = lax.rem(scal[RING], 2) == 1
    for mode in range(MODES):
        for part in range(2):
            block = jnp.where(second, probe[mode, part, rows, LANES:], probe[mode, part, rows, :LANES])
            index = 2 * mode + part
            shard[index : index + 1] = jnp.sum(
                jnp.where(wanted, block, 0.0), axis=0, keepdims=True
            )
    forward(view, probe, tables, spectra)


def next_kernel(view, pieces, tables, probe, spectra):
    for xlo in range(2):
        for core in range(2):
            row = core * 16 + xlo * 8
            for index in range(2 * MODES):
                for half in range(2):
                    lanes = slice(half * LANES, (half + 1) * LANES)
                    piece = pieces[xlo, core, pl.ds(RINGS * half + index, 8, stride=2 * RINGS), :]
                    probe[index // 2, index % 2, row : row + 8, lanes] = piece
    forward(view, probe, tables, spectra)


def counts_kernel(scal, measured, counts, flags):
    for place, which in enumerate((LIVE, CORE, XLO)):
        flags[place] = jnp.full((8, SIDE), scal[which].astype(F32))
    block = measured[0, scal[SLOT]].astype(F32)
    block = pltpu.roll(block, lax.rem(SIDE - scal[MODE] * SLAB, SIDE), 1)[:, :LANES]
    lanes = lax.broadcasted_iota(jnp.int32, block.shape, 1)
    block = jnp.where(lanes < SLAB, block, 0.0)
    block = block + pltpu.roll(block, SLAB, 1)
    counts[...] = block + pltpu.roll(block, 2 * SLAB, 1)


def ratio_kernel(spectra, counts, flags, tables, out):
    real = stacked(spectra[slab_of(index), 0] for index in range(MODES))
    imag = stacked(spectra[slab_of(index), 1] for index in range(MODES))
    far_real, far_imag = columns_transform(real, imag, tables, 1.0)
    power = far_real * far_real + far_imag * far_imag
    total = power[:, :LANES] + power[:, LANES:]
    total = total + pltpu.roll(total, 2 * SLAB, 1)
    total = total + pltpu.roll(total, SLAB, 1)
    ratio = jnp.sqrt((counts[...] + SOFT_FLOOR) / (total + SOFT_FLOOR)) - 1.0
    ratio = ratio * flags[0, 0:1, :LANES]
    ratio = jnp.concatenate([ratio, ratio], axis=1)
    both = columns_transform(far_real * ratio, far_imag * ratio, tables, -1.0)
    for part in range(2):
        for place in range(MODES):
            row = slab_of(place) * SLAB
            out[place, part] = both[part][row : row + SLAB]


def backward_kernel(spectra, view, flags, tables, chi, keep, send):
    real = stacked(swap_blocks([spectra[place, 0] for place in range(MODES)]))
    imag = stacked(swap_blocks([spectra[place, 1] for place in range(MODES)]))
    chi_real, chi_imag = rows_transform(real, imag, tables, -1.0)
    view_real, view_imag = view[0], view[1]
    sums = []
    for mode in range(MODES):
        real = chi_real[mode * SLAB : (mode + 1) * SLAB]
        imag = chi_imag[mode * SLAB : (mode + 1) * SLAB]
        chi[mode, 0] = real
        chi[mode, 1] = imag
        sums.append(view_real * real + view_imag * imag)
        sums.append(view_real * imag - view_imag * real)
    sums.append((view_real * view_real + view_imag * view_imag) * flags[0, 0:1, :])
    second = jnp.broadcast_to(flags[1, 0:1, :], (16, SIDE)) > 0.5
    for index, value in enumerate(sums):
        keep[index] = jnp.where(second, value[16:], value[:16])
        send[index] = jnp.where(second, value[:16], value[16:])


def halve_kernel(mine, theirs, flags, keep, send):
    second = jnp.broadcast_to(flags[2, 0:1, :], (8, SIDE)) > 0.5
    for index in range(2 * MODES + 1):
        value = mine[index] + theirs[index]
        keep[index] = jnp.where(second, value[8:], value[:8])
        send[index] = jnp.where(second, value[:8], value[8:])


def pack_kernel(mine, theirs, packed):
    for index in range(MESSAGE):
        total = pltpu.roll(mine[index] + theirs[index], RINGS // 4, 0)
        for half in range(2):
            rows = pl.ds(MESSAGE * half + index, 8, stride=2 * MESSAGE)
            packed[rows, :] = total[:, half * LANES : (half + 1) * LANES]


def step_kernel(chi, probe, step):
    real = imag = light = 0.0
    for mode in range(MODES):
        probe_real, probe_imag = probe[mode, 0], probe[mode, 1]
        real = real + (probe_real * chi[mode, 0] + probe_imag * chi[mode, 1])
        imag = imag + (probe_real * chi[mode, 1] - probe_imag * chi[mode, 0])
        light = light + (probe_real * probe_real + probe_imag * probe_imag)
    step[0] = OBJECT_RATE * real / (light + OBJECT_DAMP)
    step[1] = OBJECT_RATE * imag / (light + OBJECT_DAMP)


def place_kernel(scal, above, step, below, band, part_band, to_left, to_right):
    cols, rest = column_window(scal)
    height = 3 * SLAB
    part_band[...] = jnp.zeros_like(part_band)
    for part in range(2):
        block = stacked([above[part], step[part], below[part]])
        block = pltpu.roll(block, lax.rem(2 * SLAB + scal[ROW], height), 0)[:BAND]
        block = jnp.concatenate([block, jnp.zeros((BAND, LANES), F32)], axis=1)
        part_band[part, :, cols] = pltpu.roll(block, rest, 1)
    to_left[...] = part_band[:, :, :SIDE]
    to_right[...] = part_band[:, :, WIDTH:]
    part_band[:, :, :WIDTH] = part_band[:, :, :WIDTH] + band[:, :, :WIDTH]
    part_band[:, :, WIDTH:] = (
        part_band[:, :, WIDTH:] * scal[HAS_NEXT].astype(F32) + band[:, :, WIDTH:]
    )


def view_kernel(scal, part_band, from_left, from_right, band, view):
    band[:, :, :SIDE] = part_band[:, :, :SIDE] + from_left[...]
    band[:, :, SIDE:WIDTH] = part_band[:, :, SIDE:WIDTH]
    band[:, :, WIDTH:] = part_band[:, :, WIDTH:] + from_right[...]
    take_patch(scal, band, view)


def probe_kernel(sums, shard_in, shard, copies):
    total = sums[:MESSAGE]
    for ring in range(1, RINGS):
        total = total + sums[ring * MESSAGE : (ring + 1) * MESSAGE]
    rows = 2 * MODES
    new = shard_in[...] + PROBE_RATE * total[:rows] / (total[rows:] + PROBE_DAMP)
    shard[...] = new
    for ring in range(RINGS):
        copies[ring] = new


def out_rows_kernel(scal, part_band, from_left, rows_out):
    rows = pl.ds(pl.multiple_of(scal[BAND_ID] // 2 * 8, 8), OUT_ROWS)
    rows_out[:, :, :SIDE] = part_band[:, rows, :SIDE] + from_left[:, rows, :]
    rows_out[:, :, SIDE:] = part_band[:, rows, SIDE:WIDTH]


def tail_kernel(piece, tail):
    for place in range(MODES):
        for half in range(2):
            for part in range(2):
                row = (half * 2 + part) * 8
                rows = pl.ds(RINGS * half + 2 * place + part, 8, stride=2 * RINGS)
                tail[place, row : row + 8] = piece[rows, :]


def spread_kernel(rows_out, spread):
    for place in range(MODES):
        for part in range(2):
            for block in range(WIDTH // LANES):
                row = (part * 4 + block) * OUT_ROWS
                lanes = slice(block * LANES, (block + 1) * LANES)
                spread[place, row : row + OUT_ROWS] = rows_out[part, :, lanes]


def object_kernel(spread, object_out):
    for place in range(MODES):
        first = slab_of(place) * 9 // 2 * 8
        for part in range(2):
            for block in range(WIDTH // LANES):
                row = (part * 4 + block) * OUT_ROWS
                lanes = slice(block * LANES, (block + 1) * LANES)
                object_out[part, first : first + OUT_ROWS, lanes] = spread[
                    place, row : row + OUT_ROWS
                ]


def probe_out_kernel(pieces, probe_out):
    for xlo in range(2):
        for core in range(2):
            for place in range(MODES):
                first = slab_of(place) * SLAB + core * 16 + xlo * 8
                for half in range(2):
                    lanes = slice(half * LANES, (half + 1) * LANES)
                    for part in range(2):
                        row = (half * 2 + part) * 8
                        probe_out[0, part, first : first + 8, lanes] = pieces[
                            xlo, core, place, row : row + 8
                        ]


def own_kernel(place, whole, own, left, sems):
    rows = pl.ds(pl.multiple_of(place[0] * SLAB, SLAB), BAND)
    first = pltpu.make_async_copy(whole.at[:, rows, :], own, sems.at[0])
    second = pltpu.make_async_copy(whole.at[:, rows, pl.ds(0, SIDE)], left, sems.at[1])
    first.start()
    second.start()
    first.wait()
    second.wait()


def take_own(mode, object_tiles, after):
    vmem = pl.BlockSpec(memory_space=pltpu.VMEM)
    anywhere = pl.BlockSpec(memory_space=pl.ANY)

    def body(place, whole, _, own, left, sems):
        own_kernel(place, whole, own, left, sems)

    return pl.pallas_call(
        body,
        out_shape=[
            jax.ShapeDtypeStruct((2, BAND, WIDTH), F32),
            jax.ShapeDtypeStruct((2, BAND, SIDE), F32),
        ],
        in_specs=[pl.BlockSpec(memory_space=pltpu.SMEM), anywhere, anywhere],
        out_specs=[vmem, vmem],
        scratch_shapes=[pltpu.SemaphoreType.DMA((2,))],
        compiler_params=pltpu.CompilerParams(vmem_limit_bytes=VMEM_LIMIT),
        name="own_kernel",
    )(mode.astype(jnp.int32).reshape(1), object_tiles, after)


def call(kernel, outs, *args, scalars=True, after=()):
    vmem = pl.BlockSpec(memory_space=pltpu.VMEM)
    in_specs = [vmem] * len(args) + [pl.BlockSpec(memory_space=pl.ANY)] * len(after)

    def body(*refs):
        taken = list(refs[: len(args)])
        if scalars:
            taken[0] = [taken[0][0, index] for index in range(BAND_ID + 1)]
        kernel(*taken, *refs[len(args) + len(after) :])

    return pl.pallas_call(
        body,
        out_shape=[jax.ShapeDtypeStruct(shape, F32) for shape in outs],
        in_specs=in_specs,
        out_specs=[vmem] * len(outs),
        compiler_params=pltpu.CompilerParams(vmem_limit_bytes=VMEM_LIMIT),
        name=kernel.__name__,
    )(*args, *after)


def shift(value, axes, count, steps):
    first, last = max(0, -steps), min(count, count - steps)
    return lax.ppermute(value, axes, [(i, i + steps) for i in range(first, last)])


def other(value, axis):
    return lax.ppermute(value, axis, [(0, 1), (1, 0)])


def beside_slab(value, steps):
    first, last = max(0, -steps), min(MODES, MODES - steps)
    pairs = [(slab_of(i), slab_of(i + steps)) for i in range(first, last)]
    return lax.ppermute(value, MODE_AXES, pairs)


def exchange_rings(value):
    groups = [[(ring + RINGS // 2) % RINGS for ring in range(RINGS)]]
    value = value.reshape(RINGS, 1, MESSAGE * LANES)
    value = lax.all_to_all(value, "z", 0, 0, tiled=True, axis_index_groups=groups)
    return value.reshape(RINGS * MESSAGE, LANES)


def exchange(value, axes):
    return lax.all_to_all(value, axes, 0, 0, tiled=True)


def gather_pieces(piece):
    gathered = lax.all_gather(piece, ("xlo", "core"))
    return gathered.reshape((2, 2) + piece.shape)


def per_device(
    object_tiles, probe_modes, measured, row_offset, col_offset, live_counts, visit_order
):
    tables = jnp.asarray(fourier_tables())
    slots = visit_order[0]
    tile = lax.axis_index(TILE_AXES)
    mode = lax.axis_index(MODE_AXES)
    slab = jnp.where(mode < MODES // 2, mode, 11 - mode)
    (pieces,) = call(split_kernel, [(MODES, 2, SLAB, SIDE)], probe_modes, scalars=False)
    probe = exchange(pieces, MODE_AXES)
    own, left = take_own(slab, object_tiles, pieces)
    beside = shift(left, TILE_AXES, TILES, -1)
    places = [
        mode,
        lax.axis_index("core"),
        lax.axis_index("xlo"),
        lax.axis_index("z"),
        (tile < TILES - 1).astype(jnp.int32),
        slab,
    ]
    chosen = slots[:, None] == jnp.arange(STEPS, dtype=jnp.int32)[None, :]
    per_step = [
        jnp.sum(jnp.where(chosen, row_offset, 0), axis=1),
        jnp.sum(jnp.where(chosen, col_offset, 0), axis=1),
        slots,
        (slots < live_counts[0]).astype(jnp.int32),
    ]
    scalars = jnp.stack(
        per_step + [jnp.broadcast_to(place, (STEPS,)) for place in places], axis=1
    )
    slabs = (MODES, 2, SLAB, SIDE)
    slab_pair = (2, SLAB, SIDE)
    band_shape = (2, BAND, WIDE)
    edge = (2, BAND, SIDE)
    counts_shapes = [(SIDE, LANES), (3, 8, SIDE)]
    counts, flags = call(counts_kernel, counts_shapes, scalars[:1], measured)
    for step in range(STEPS):
        scal = scalars[step : step + 1]
        final = step == STEPS - 1
        if step == 0:
            band, view, shard, spectra = call(
                first_kernel,
                [band_shape, slab_pair, (2 * MODES, LANES), slabs],
                scal,
                own,
                beside,
                probe,
                tables,
                after=(counts,),
            )
        else:
            probe, spectra = call(
                next_kernel,
                [slabs, slabs],
                view,
                pieces,
                tables,
                scalars=False,
                after=(counts,),
            )
        spectra = exchange(spectra, MODE_AXES)
        (spectra,) = call(
            ratio_kernel, [slabs], spectra, counts, flags, tables, scalars=False
        )
        spectra = exchange(spectra, MODE_AXES)
        chi, keep, send = call(
            backward_kernel,
            [slabs] + [(2 * MODES + 1, 16, SIDE)] * 2,
            spectra,
            view,
            flags,
            tables,
            scalars=False,
        )
        received = other(send, "core")
        keep, send = call(
            halve_kernel, [(2 * MODES + 1, 8, SIDE)] * 2, keep, received, flags, scalars=False
        )
        received = other(send, "xlo")
        (object_step,) = call(
            step_kernel, [slab_pair], chi, probe, scalars=False, after=(keep,)
        )
        above = beside_slab(object_step, 1)
        below = beside_slab(object_step, -1)
        if not final:
            next_scal = scalars[step + 1 : step + 2]
            counts, flags = call(
                counts_kernel, counts_shapes, next_scal, measured, after=(keep,)
            )
        (packed,) = call(
            pack_kernel,
            [(RINGS * MESSAGE, LANES)],
            keep,
            received,
            scalars=False,
            after=(above, below) if final else (object_step, counts),
        )
        sums = exchange_rings(packed)
        placing = [scal, above, object_step, below, band]
        if final:
            part_band, _, to_right = call(
                place_kernel, [band_shape, edge, edge], *placing, after=(packed,)
            )
            from_left = shift(to_right, TILE_AXES, TILES, 1)
            (rows_out,) = call(
                out_rows_kernel, [(2, OUT_ROWS, WIDTH)], scal, part_band, from_left
            )
            (spread,) = call(
                spread_kernel, [(MODES, 8 * OUT_ROWS, LANES)], rows_out, scalars=False
            )
            before = (spread,)
        else:
            before = (above, below)
        shard, shards = call(
            probe_kernel,
            [(2 * MODES, LANES), (RINGS, 2 * MODES, LANES)],
            sums,
            shard,
            scalars=False,
            after=before,
        )
        if final:
            spread = exchange(spread, MODE_AXES)
            piece = lax.all_gather(shard, "z")
        else:
            piece = exchange(shards, "z")
            part_band, to_left, to_right = call(
                place_kernel, [band_shape, edge, edge], *placing, after=(shards,)
            )
            from_left = shift(to_right, TILE_AXES, TILES, 1)
            from_right = shift(to_left, TILE_AXES, TILES, -1)
            band, view = call(
                view_kernel,
                [band_shape, slab_pair],
                next_scal,
                part_band,
                from_left,
                from_right,
            )
            piece, view = lax.optimization_barrier((piece, view))
            pieces = gather_pieces(piece.reshape(2 * MODES * RINGS, LANES))
    (tail,) = call(
        tail_kernel,
        [(MODES, 32, LANES)],
        piece.reshape(2 * MODES * RINGS, LANES),
        scalars=False,
        after=(spread,),
    )
    pieces = gather_pieces(exchange(tail, MODE_AXES))
    (object_out,) = call(object_kernel, [(2, HEIGHT, WIDTH)], spread, scalars=False)
    (probe_out,) = call(probe_out_kernel, [(1, 2, SIDE, SIDE)], pieces, scalars=False)
    return object_out, probe_out


def solution(mesh):
    grid = Mesh(mesh.devices.reshape(2, 16, 2, 2, 4), TILE_AXES + MODE_AXES)
    return jax.shard_map(
        per_device,
        mesh=grid,
        in_specs=(
            P(None, None, TILE_AXES),
            P(MODE_AXES, None, None, None),
            P(TILE_AXES, None, None, None),
            P(TILE_AXES, None),
            P(TILE_AXES, None),
            P(TILE_AXES),
            P(TILE_AXES, None),
        ),
        out_specs=(P(None, None, TILE_AXES), P(MODE_AXES, None, None, None)),
        check_vma=False,
    )
```

```python
import math

import jax
import jax.numpy as jnp
import numpy as np
from jax import lax
from jax.experimental import pallas as pl
from jax.experimental.pallas import tpu as pltpu
from jax.sharding import Mesh
from jax.sharding import PartitionSpec as P

SOFT_FLOOR = 0.5
OBJECT_RATE = 1.0
OBJECT_DAMP = 0.5
PROBE_RATE = 1.0
PROBE_DAMP = 1.0

SIDE = 256
HEIGHT = 288
WIDTH = 512
WIDE = WIDTH + SIDE
MODES = 8
SLAB = SIDE // MODES
BAND = 2 * SLAB
STEPS = 3
TILES = 64
RINGS = 16
LANES = 128
COL_SPAN = SIDE + LANES
OUT_ROWS = HEIGHT // MODES
MESSAGE = 2 * MODES + 1
VMEM_LIMIT = 16 * 1024 * 1024

TILE_AXES = ("xlo", "z", "core")
MODE_AXES = ("xhi", "y")

ROW, COL, SLOT, LIVE, MODE, CORE, XLO, RING, HAS_NEXT, BAND_ID = range(10)

F32 = jnp.float32
BF16 = jnp.bfloat16


def slab_of(place):
    return place if place < MODES // 2 else 11 - place


def fourier_tables():
    index = np.arange(SIDE)
    angles = (index[:, None] * index[None, :] % SIDE) * (2.0 * math.pi / SIDE)
    cosine, sine = np.cos(angles) / math.sqrt(SIDE), np.sin(angles) / math.sqrt(SIDE)
    exact = np.stack([cosine, cosine + sine, cosine - sine])
    high = exact.astype(jnp.bfloat16)
    low = (exact - high.astype(np.float64)).astype(jnp.bfloat16)
    return np.stack([high, low], axis=1)


def halves(value):
    high = value.astype(BF16)
    return high, (value - high.astype(F32)).astype(BF16)


def dot(left, right):
    return jnp.dot(left, right, preferred_element_type=F32)


def transform(real, imag, by, direction):
    turned = direction * imag
    shared = by(0, real + turned)
    return shared - by(2, turned), direction * (shared - by(1, real))


def rows_transform(real, imag, tables, direction):
    def by(which, value):
        high, low = halves(value)
        return (
            dot(high, tables[which, 0]) + dot(low, tables[which, 0]) + dot(high, tables[which, 1])
        )

    return transform(real, imag, by, direction)


def columns_transform(real, imag, tables, direction):
    def by(which, value):
        high, low = halves(value)
        return (
            dot(tables[which, 0], high) + dot(tables[which, 0], low) + dot(tables[which, 1], high)
        )

    return transform(real, imag, by, direction)


def swap_blocks(parts):
    lanes = lax.broadcasted_iota(jnp.int32, (parts[0].shape[0], LANES), 1)
    grid = [[part[:, :LANES], part[:, LANES:]] for part in parts]
    grid = [[grid[(m & 3) | (h << 2)][m >> 2] for h in range(2)] for m in range(MODES)]
    for bit in (2, 1):
        shift = bit * SLAB
        low = (lanes & shift) == 0
        new = [None] * MODES
        for m in range(MODES):
            if m & bit:
                continue
            a, b = grid[m], grid[m | bit]
            new[m] = [jnp.where(low, a[h], pltpu.roll(b[h], shift, 1)) for h in range(2)]
            new[m | bit] = [
                jnp.where(low, pltpu.roll(a[h], LANES - shift, 1), b[h]) for h in range(2)
            ]
        grid = new
    return [jnp.concatenate(pair, axis=1) for pair in grid]


def stacked(pieces):
    return jnp.concatenate(list(pieces), axis=0)


def column_window(scal):
    col = scal[COL]
    block = jnp.minimum(col // LANES, WIDTH // LANES - 1)
    return pl.ds(pl.multiple_of(block * LANES, LANES), COL_SPAN), col - block * LANES


def take_patch(scal, band, view):
    cols, rest = column_window(scal)
    for part in range(2):
        block = band[part, :, cols]
        block = pltpu.roll(block, lax.rem(COL_SPAN - rest, COL_SPAN), 1)[:, :SIDE]
        view[part] = pltpu.roll(block, lax.rem(BAND - scal[ROW], BAND), 0)[:SLAB]


def forward(view, probe, tables, spectra):
    view_real = stacked([view[0]] * MODES)
    view_imag = stacked([view[1]] * MODES)
    probe_real = stacked(probe[mode, 0] for mode in range(MODES))
    probe_imag = stacked(probe[mode, 1] for mode in range(MODES))
    both = rows_transform(
        probe_real * view_real - probe_imag * view_imag,
        probe_real * view_imag + probe_imag * view_real,
        tables,
        1.0,
    )
    for part in range(2):
        blocks = [both[part][mode * SLAB : (mode + 1) * SLAB] for mode in range(MODES)]
        for place, block in enumerate(swap_blocks(blocks)):
            spectra[place, part] = block


def split_kernel(probe_in, pieces):
    for place in range(MODES):
        row = slab_of(place) * SLAB
        pieces[place] = probe_in[0, :, row : row + SLAB, :]


def first_kernel(scal, own, beside, probe, tables, band, view, shard, spectra):
    band[:, :, :WIDTH] = own[...]
    band[:, :, WIDTH:] = beside[...]
    take_patch(scal, band, view)
    rows = pl.ds(pl.multiple_of(scal[CORE] * 16 + scal[XLO] * 8, 8), 8)
    wanted = lax.broadcasted_iota(jnp.int32, (8, LANES), 0) == scal[RING] // 2
    second = lax.rem(scal[RING], 2) == 1
    for mode in range(MODES):
        for part in range(2):
            block = jnp.where(second, probe[mode, part, rows, LANES:], probe[mode, part, rows, :LANES])
            index = 2 * mode + part
            shard[index : index + 1] = jnp.sum(
                jnp.where(wanted, block, 0.0), axis=0, keepdims=True
            )
    forward(view, probe, tables, spectra)


def next_kernel(view, pieces, tables, probe, spectra):
    for xlo in range(2):
        for core in range(2):
            row = core * 16 + xlo * 8
            for index in range(2 * MODES):
                for half in range(2):
                    lanes = slice(half * LANES, (half + 1) * LANES)
                    piece = pieces[xlo, core, pl.ds(RINGS * half + index, 8, stride=2 * RINGS), :]
                    probe[index // 2, index % 2, row : row + 8, lanes] = piece
    forward(view, probe, tables, spectra)


def counts_kernel(scal, measured, counts, flags):
    for place, which in enumerate((LIVE, CORE, XLO)):
        flags[place] = jnp.full((8, SIDE), scal[which].astype(F32))
    block = measured[0, scal[SLOT]].astype(F32)
    block = pltpu.roll(block, lax.rem(SIDE - scal[MODE] * SLAB, SIDE), 1)[:, :LANES]
    lanes = lax.broadcasted_iota(jnp.int32, block.shape, 1)
    block = jnp.where(lanes < SLAB, block, 0.0)
    block = block + pltpu.roll(block, SLAB, 1)
    counts[...] = block + pltpu.roll(block, 2 * SLAB, 1)


def ratio_kernel(spectra, counts, flags, tables, out):
    real = stacked(spectra[slab_of(index), 0] for index in range(MODES))
    imag = stacked(spectra[slab_of(index), 1] for index in range(MODES))
    far_real, far_imag = columns_transform(real, imag, tables, 1.0)
    power = far_real * far_real + far_imag * far_imag
    total = power[:, :LANES] + power[:, LANES:]
    total = total + pltpu.roll(total, 2 * SLAB, 1)
    total = total + pltpu.roll(total, SLAB, 1)
    ratio = jnp.sqrt((counts[...] + SOFT_FLOOR) / (total + SOFT_FLOOR)) - 1.0
    ratio = ratio * flags[0, 0:1, :LANES]
    ratio = jnp.concatenate([ratio, ratio], axis=1)
    both = columns_transform(far_real * ratio, far_imag * ratio, tables, -1.0)
    for part in range(2):
        for place in range(MODES):
            row = slab_of(place) * SLAB
            out[place, part] = both[part][row : row + SLAB]


def backward_kernel(spectra, view, flags, tables, chi, keep, send):
    real = stacked(swap_blocks([spectra[place, 0] for place in range(MODES)]))
    imag = stacked(swap_blocks([spectra[place, 1] for place in range(MODES)]))
    chi_real, chi_imag = rows_transform(real, imag, tables, -1.0)
    view_real, view_imag = view[0], view[1]
    sums = []
    for mode in range(MODES):
        real = chi_real[mode * SLAB : (mode + 1) * SLAB]
        imag = chi_imag[mode * SLAB : (mode + 1) * SLAB]
        chi[mode, 0] = real
        chi[mode, 1] = imag
        sums.append(view_real * real + view_imag * imag)
        sums.append(view_real * imag - view_imag * real)
    sums.append((view_real * view_real + view_imag * view_imag) * flags[0, 0:1, :])
    second = jnp.broadcast_to(flags[1, 0:1, :], (16, SIDE)) > 0.5
    for index, value in enumerate(sums):
        keep[index] = jnp.where(second, value[16:], value[:16])
        send[index] = jnp.where(second, value[:16], value[16:])


def halve_kernel(mine, theirs, flags, keep, send):
    second = jnp.broadcast_to(flags[2, 0:1, :], (8, SIDE)) > 0.5
    for index in range(2 * MODES + 1):
        value = mine[index] + theirs[index]
        keep[index] = jnp.where(second, value[8:], value[:8])
        send[index] = jnp.where(second, value[:8], value[8:])


def pack_kernel(mine, theirs, packed):
    for index in range(MESSAGE):
        total = pltpu.roll(mine[index] + theirs[index], RINGS // 4, 0)
        for half in range(2):
            rows = pl.ds(MESSAGE * half + index, 8, stride=2 * MESSAGE)
            packed[rows, :] = total[:, half * LANES : (half + 1) * LANES]


def step_kernel(chi, probe, step):
    real = imag = light = 0.0
    for mode in range(MODES):
        probe_real, probe_imag = probe[mode, 0], probe[mode, 1]
        real = real + (probe_real * chi[mode, 0] + probe_imag * chi[mode, 1])
        imag = imag + (probe_real * chi[mode, 1] - probe_imag * chi[mode, 0])
        light = light + (probe_real * probe_real + probe_imag * probe_imag)
    step[0] = OBJECT_RATE * real / (light + OBJECT_DAMP)
    step[1] = OBJECT_RATE * imag / (light + OBJECT_DAMP)


def place_kernel(scal, above, step, below, band, part_band, to_left, to_right):
    cols, rest = column_window(scal)
    height = 3 * SLAB
    part_band[...] = jnp.zeros_like(part_band)
    for part in range(2):
        block = stacked([above[part], step[part], below[part]])
        block = pltpu.roll(block, lax.rem(2 * SLAB + scal[ROW], height), 0)[:BAND]
        block = jnp.concatenate([block, jnp.zeros((BAND, LANES), F32)], axis=1)
        part_band[part, :, cols] = pltpu.roll(block, rest, 1)
    to_left[...] = part_band[:, :, :SIDE]
    to_right[...] = part_band[:, :, WIDTH:]
    part_band[:, :, :WIDTH] = part_band[:, :, :WIDTH] + band[:, :, :WIDTH]
    part_band[:, :, WIDTH:] = (
        part_band[:, :, WIDTH:] * scal[HAS_NEXT].astype(F32) + band[:, :, WIDTH:]
    )


def view_kernel(scal, part_band, from_left, from_right, band, view):
    band[:, :, :SIDE] = part_band[:, :, :SIDE] + from_left[...]
    band[:, :, SIDE:WIDTH] = part_band[:, :, SIDE:WIDTH]
    band[:, :, WIDTH:] = part_band[:, :, WIDTH:] + from_right[...]
    take_patch(scal, band, view)


def probe_kernel(sums, shard_in, shard, copies):
    total = sums[:MESSAGE]
    for ring in range(1, RINGS):
        total = total + sums[ring * MESSAGE : (ring + 1) * MESSAGE]
    rows = 2 * MODES
    new = shard_in[...] + PROBE_RATE * total[:rows] / (total[rows:] + PROBE_DAMP)
    shard[...] = new
    for ring in range(RINGS):
        copies[ring] = new


def out_rows_kernel(scal, part_band, from_left, rows_out):
    slab = scal[BAND_ID]
    odd = lax.rem(slab, 2) == 1
    rows = pl.ds(pl.multiple_of(slab // 2 * 8, 8), OUT_ROWS + 4)
    for part in range(2):
        edge = part_band[part, rows, :SIDE] + from_left[part, rows, :]
        block = jnp.concatenate([edge, part_band[part, rows, SIDE:WIDTH]], axis=1)
        block = jnp.where(odd, pltpu.roll(block, OUT_ROWS, 0), block)
        rows_out[part] = block[:OUT_ROWS]


def tail_kernel(piece, rows_out, tail):
    for place in range(MODES):
        for half in range(2):
            for part in range(2):
                row = (half * 2 + part) * 8
                rows = pl.ds(RINGS * half + 2 * place + part, 8, stride=2 * RINGS)
                tail[place, row : row + 8] = piece[rows, :]
        for part in range(2):
            for block in range(WIDTH // LANES):
                row = 32 + (part * 4 + block) * OUT_ROWS
                lanes = slice(block * LANES, (block + 1) * LANES)
                tail[place, row : row + OUT_ROWS] = rows_out[part, :, lanes]


def object_kernel(tail, object_out):
    for place in range(MODES):
        first = slab_of(place) * OUT_ROWS
        for part in range(2):
            for block in range(WIDTH // LANES):
                row = 32 + (part * 4 + block) * OUT_ROWS
                lanes = slice(block * LANES, (block + 1) * LANES)
                object_out[part, first : first + OUT_ROWS, lanes] = tail[
                    place, row : row + OUT_ROWS
                ]


def probe_out_kernel(pieces, probe_out):
    for xlo in range(2):
        for core in range(2):
            for place in range(MODES):
                first = slab_of(place) * SLAB + core * 16 + xlo * 8
                for half in range(2):
                    lanes = slice(half * LANES, (half + 1) * LANES)
                    for part in range(2):
                        row = (half * 2 + part) * 8
                        probe_out[0, part, first : first + 8, lanes] = pieces[
                            xlo, core, place, row : row + 8
                        ]


def own_kernel(place, whole, own, left, sems):
    rows = pl.ds(pl.multiple_of(place[0] * SLAB, SLAB), BAND)
    first = pltpu.make_async_copy(whole.at[:, rows, :], own, sems.at[0])
    second = pltpu.make_async_copy(whole.at[:, rows, pl.ds(0, SIDE)], left, sems.at[1])
    first.start()
    second.start()
    first.wait()
    second.wait()


def take_own(mode, object_tiles, after):
    vmem = pl.BlockSpec(memory_space=pltpu.VMEM)
    anywhere = pl.BlockSpec(memory_space=pl.ANY)

    def body(place, whole, _, own, left, sems):
        own_kernel(place, whole, own, left, sems)

    return pl.pallas_call(
        body,
        out_shape=[
            jax.ShapeDtypeStruct((2, BAND, WIDTH), F32),
            jax.ShapeDtypeStruct((2, BAND, SIDE), F32),
        ],
        in_specs=[pl.BlockSpec(memory_space=pltpu.SMEM), anywhere, anywhere],
        out_specs=[vmem, vmem],
        scratch_shapes=[pltpu.SemaphoreType.DMA((2,))],
        compiler_params=pltpu.CompilerParams(vmem_limit_bytes=VMEM_LIMIT),
        name="own_kernel",
    )(mode.astype(jnp.int32).reshape(1), object_tiles, after)


def call(kernel, outs, *args, scalars=True, after=()):
    vmem = pl.BlockSpec(memory_space=pltpu.VMEM)
    in_specs = [vmem] * len(args) + [pl.BlockSpec(memory_space=pl.ANY)] * len(after)

    def body(*refs):
        taken = list(refs[: len(args)])
        if scalars:
            taken[0] = [taken[0][0, index] for index in range(BAND_ID + 1)]
        kernel(*taken, *refs[len(args) + len(after) :])

    return pl.pallas_call(
        body,
        out_shape=[jax.ShapeDtypeStruct(shape, F32) for shape in outs],
        in_specs=in_specs,
        out_specs=[vmem] * len(outs),
        compiler_params=pltpu.CompilerParams(vmem_limit_bytes=VMEM_LIMIT),
        name=kernel.__name__,
    )(*args, *after)


def shift(value, axes, count, steps):
    first, last = max(0, -steps), min(count, count - steps)
    return lax.ppermute(value, axes, [(i, i + steps) for i in range(first, last)])


def other(value, axis):
    return lax.ppermute(value, axis, [(0, 1), (1, 0)])


def beside_slab(value, steps):
    first, last = max(0, -steps), min(MODES, MODES - steps)
    pairs = [(slab_of(i), slab_of(i + steps)) for i in range(first, last)]
    return lax.ppermute(value, MODE_AXES, pairs)


def exchange_rings(value):
    groups = [[(ring + RINGS // 2) % RINGS for ring in range(RINGS)]]
    value = value.reshape(RINGS, 1, MESSAGE * LANES)
    value = lax.all_to_all(value, "z", 0, 0, tiled=True, axis_index_groups=groups)
    return value.reshape(RINGS * MESSAGE, LANES)


def exchange(value, axes):
    return lax.all_to_all(value, axes, 0, 0, tiled=True)


def gather_pieces(piece):
    gathered = lax.all_gather(piece, ("xlo", "core"))
    return gathered.reshape((2, 2) + piece.shape)


def per_device(
    object_tiles, probe_modes, measured, row_offset, col_offset, live_counts, visit_order
):
    tables = jnp.asarray(fourier_tables())
    slots = visit_order[0]
    tile = lax.axis_index(TILE_AXES)
    mode = lax.axis_index(MODE_AXES)
    slab = jnp.where(mode < MODES // 2, mode, 11 - mode)
    (pieces,) = call(split_kernel, [(MODES, 2, SLAB, SIDE)], probe_modes, scalars=False)
    probe = exchange(pieces, MODE_AXES)
    own, left = take_own(slab, object_tiles, pieces)
    beside = shift(left, TILE_AXES, TILES, -1)
    places = [
        mode,
        lax.axis_index("core"),
        lax.axis_index("xlo"),
        lax.axis_index("z"),
        (tile < TILES - 1).astype(jnp.int32),
        slab,
    ]
    chosen = slots[:, None] == jnp.arange(STEPS, dtype=jnp.int32)[None, :]
    per_step = [
        jnp.sum(jnp.where(chosen, row_offset, 0), axis=1),
        jnp.sum(jnp.where(chosen, col_offset, 0), axis=1),
        slots,
        (slots < live_counts[0]).astype(jnp.int32),
    ]
    scalars = jnp.stack(
        per_step + [jnp.broadcast_to(place, (STEPS,)) for place in places], axis=1
    )
    slabs = (MODES, 2, SLAB, SIDE)
    slab_pair = (2, SLAB, SIDE)
    band_shape = (2, BAND, WIDE)
    edge = (2, BAND, SIDE)
    counts_shapes = [(SIDE, LANES), (3, 8, SIDE)]
    counts, flags = call(counts_kernel, counts_shapes, scalars[:1], measured)
    for step in range(STEPS):
        scal = scalars[step : step + 1]
        final = step == STEPS - 1
        if step == 0:
            band, view, shard, spectra = call(
                first_kernel,
                [band_shape, slab_pair, (2 * MODES, LANES), slabs],
                scal,
                own,
                beside,
                probe,
                tables,
                after=(counts,),
            )
        else:
            probe, spectra = call(
                next_kernel,
                [slabs, slabs],
                view,
                pieces,
                tables,
                scalars=False,
                after=(counts,),
            )
        spectra = exchange(spectra, MODE_AXES)
        (spectra,) = call(
            ratio_kernel, [slabs], spectra, counts, flags, tables, scalars=False
        )
        spectra = exchange(spectra, MODE_AXES)
        chi, keep, send = call(
            backward_kernel,
            [slabs] + [(2 * MODES + 1, 16, SIDE)] * 2,
            spectra,
            view,
            flags,
            tables,
            scalars=False,
        )
        received = other(send, "core")
        keep, send = call(
            halve_kernel, [(2 * MODES + 1, 8, SIDE)] * 2, keep, received, flags, scalars=False
        )
        received = other(send, "xlo")
        (object_step,) = call(
            step_kernel, [slab_pair], chi, probe, scalars=False, after=(keep,)
        )
        above = beside_slab(object_step, 1)
        below = beside_slab(object_step, -1)
        if not final:
            next_scal = scalars[step + 1 : step + 2]
            counts, flags = call(
                counts_kernel, counts_shapes, next_scal, measured, after=(keep,)
            )
        (packed,) = call(
            pack_kernel,
            [(RINGS * MESSAGE, LANES)],
            keep,
            received,
            scalars=False,
            after=(object_step,) if final else (object_step, counts),
        )
        sums = exchange_rings(packed)
        shard, shards = call(
            probe_kernel,
            [(2 * MODES, LANES), (RINGS, 2 * MODES, LANES)],
            sums,
            shard,
            scalars=False,
            after=(above, below),
        )
        piece = exchange(shards, "z")
        part_band, to_left, to_right = call(
            place_kernel,
            [band_shape, edge, edge],
            scal,
            above,
            object_step,
            below,
            band,
            after=(shards,),
        )
        from_left = shift(to_right, TILE_AXES, TILES, 1)
        if final:
            (rows_out,) = call(
                out_rows_kernel, [(2, OUT_ROWS, WIDTH)], scal, part_band, from_left
            )
            piece, rows_out = lax.optimization_barrier((piece, rows_out))
        else:
            from_right = shift(to_left, TILE_AXES, TILES, -1)
            band, view = call(
                view_kernel,
                [band_shape, slab_pair],
                next_scal,
                part_band,
                from_left,
                from_right,
            )
            piece, view = lax.optimization_barrier((piece, view))
            pieces = gather_pieces(piece.reshape(2 * MODES * RINGS, LANES))
    tail_rows = 32 + 8 * OUT_ROWS
    (tail,) = call(
        tail_kernel,
        [(MODES, tail_rows, LANES)],
        piece.reshape(2 * MODES * RINGS, LANES),
        rows_out,
        scalars=False,
    )
    tail = exchange(tail, MODE_AXES)
    pieces = gather_pieces(tail[:, :32])
    (object_out,) = call(object_kernel, [(2, HEIGHT, WIDTH)], tail, scalars=False)
    (probe_out,) = call(probe_out_kernel, [(1, 2, SIDE, SIDE)], pieces, scalars=False)
    return object_out, probe_out


def solution(mesh):
    grid = Mesh(mesh.devices.reshape(2, 16, 2, 2, 4), TILE_AXES + MODE_AXES)
    return jax.shard_map(
        per_device,
        mesh=grid,
        in_specs=(
            P(None, None, TILE_AXES),
            P(MODE_AXES, None, None, None),
            P(TILE_AXES, None, None, None),
            P(TILE_AXES, None),
            P(TILE_AXES, None),
            P(TILE_AXES),
            P(TILE_AXES, None),
        ),
        out_specs=(P(None, None, TILE_AXES), P(MODE_AXES, None, None, None)),
        check_vma=False,
    )
```

```python
import math

import jax
import jax.numpy as jnp
import numpy as np
from jax import lax
from jax.experimental import pallas as pl
from jax.experimental.pallas import tpu as pltpu
from jax.sharding import Mesh
from jax.sharding import PartitionSpec as P

SOFT_FLOOR = 0.5
OBJECT_RATE = 1.0
OBJECT_DAMP = 0.5
PROBE_RATE = 1.0
PROBE_DAMP = 1.0

SIDE = 256
HEIGHT = 288
WIDTH = 512
WIDE = WIDTH + SIDE
MODES = 8
SLAB = SIDE // MODES
BAND = 2 * SLAB
STEPS = 3
TILES = 64
RINGS = 16
LANES = 128
COL_SPAN = SIDE + LANES
OUT_ROWS = HEIGHT // MODES
MESSAGE = 2 * MODES + 1
VMEM_LIMIT = 16 * 1024 * 1024

TILE_AXES = ("xlo", "z", "core")
MODE_AXES = ("xhi", "y")

ROW, COL, SLOT, LIVE, MODE, CORE, XLO, RING, HAS_NEXT, BAND_ID = range(10)

F32 = jnp.float32
BF16 = jnp.bfloat16


def slab_of(place):
    return place if place < MODES // 2 else 11 - place


def fourier_tables():
    index = np.arange(SIDE)
    angles = (index[:, None] * index[None, :] % SIDE) * (2.0 * math.pi / SIDE)
    cosine, sine = np.cos(angles) / math.sqrt(SIDE), np.sin(angles) / math.sqrt(SIDE)
    exact = np.stack([cosine, cosine + sine, cosine - sine])
    high = exact.astype(jnp.bfloat16)
    low = (exact - high.astype(np.float64)).astype(jnp.bfloat16)
    return np.stack([high, low], axis=1)


def halves(value):
    high = value.astype(BF16)
    return high, (value - high.astype(F32)).astype(BF16)


def dot(left, right):
    return jnp.dot(left, right, preferred_element_type=F32)


def transform(real, imag, by, direction):
    turned = direction * imag
    shared = by(0, real + turned)
    return shared - by(2, turned), direction * (shared - by(1, real))


def rows_transform(real, imag, tables, direction):
    def by(which, value):
        high, low = halves(value)
        return (
            dot(high, tables[which, 0]) + dot(low, tables[which, 0]) + dot(high, tables[which, 1])
        )

    return transform(real, imag, by, direction)


def columns_transform(real, imag, tables, direction):
    def by(which, value):
        high, low = halves(value)
        return (
            dot(tables[which, 0], high) + dot(tables[which, 0], low) + dot(tables[which, 1], high)
        )

    return transform(real, imag, by, direction)


def swap_blocks(parts):
    lanes = lax.broadcasted_iota(jnp.int32, (parts[0].shape[0], LANES), 1)
    grid = [[part[:, :LANES], part[:, LANES:]] for part in parts]
    grid = [[grid[(m & 3) | (h << 2)][m >> 2] for h in range(2)] for m in range(MODES)]
    for bit in (2, 1):
        shift = bit * SLAB
        low = (lanes & shift) == 0
        new = [None] * MODES
        for m in range(MODES):
            if m & bit:
                continue
            a, b = grid[m], grid[m | bit]
            new[m] = [jnp.where(low, a[h], pltpu.roll(b[h], shift, 1)) for h in range(2)]
            new[m | bit] = [
                jnp.where(low, pltpu.roll(a[h], LANES - shift, 1), b[h]) for h in range(2)
            ]
        grid = new
    return [jnp.concatenate(pair, axis=1) for pair in grid]


def stacked(pieces):
    return jnp.concatenate(list(pieces), axis=0)


def column_window(scal):
    col = scal[COL]
    block = jnp.minimum(col // LANES, WIDTH // LANES - 1)
    return pl.ds(pl.multiple_of(block * LANES, LANES), COL_SPAN), col - block * LANES


def take_patch(scal, band, view):
    cols, rest = column_window(scal)
    for part in range(2):
        block = band[part, :, cols]
        block = pltpu.roll(block, lax.rem(COL_SPAN - rest, COL_SPAN), 1)[:, :SIDE]
        view[part] = pltpu.roll(block, lax.rem(BAND - scal[ROW], BAND), 0)[:SLAB]


def forward(view, probe, tables, spectra):
    view_real = stacked([view[0]] * MODES)
    view_imag = stacked([view[1]] * MODES)
    probe_real = stacked(probe[mode, 0] for mode in range(MODES))
    probe_imag = stacked(probe[mode, 1] for mode in range(MODES))
    both = rows_transform(
        probe_real * view_real - probe_imag * view_imag,
        probe_real * view_imag + probe_imag * view_real,
        tables,
        1.0,
    )
    for part in range(2):
        blocks = [both[part][mode * SLAB : (mode + 1) * SLAB] for mode in range(MODES)]
        for place, block in enumerate(swap_blocks(blocks)):
            spectra[place, part] = block


def split_kernel(probe_in, pieces):
    for place in range(MODES):
        row = slab_of(place) * SLAB
        pieces[place] = probe_in[0, :, row : row + SLAB, :]


def first_kernel(scal, own, beside, probe, tables, band, view, shard, spectra):
    band[:, :, :WIDTH] = own[...]
    band[:, :, WIDTH:] = beside[...]
    take_patch(scal, band, view)
    rows = pl.ds(pl.multiple_of(scal[CORE] * 16 + scal[XLO] * 8, 8), 8)
    wanted = lax.broadcasted_iota(jnp.int32, (8, LANES), 0) == scal[RING] // 2
    second = lax.rem(scal[RING], 2) == 1
    for mode in range(MODES):
        for part in range(2):
            block = jnp.where(second, probe[mode, part, rows, LANES:], probe[mode, part, rows, :LANES])
            index = 2 * mode + part
            shard[index : index + 1] = jnp.sum(
                jnp.where(wanted, block, 0.0), axis=0, keepdims=True
            )
    forward(view, probe, tables, spectra)


def next_kernel(view, pieces, tables, probe, spectra):
    for xlo in range(2):
        for core in range(2):
            row = core * 16 + xlo * 8
            for index in range(2 * MODES):
                for half in range(2):
                    lanes = slice(half * LANES, (half + 1) * LANES)
                    piece = pieces[xlo, core, pl.ds(RINGS * half + index, 8, stride=2 * RINGS), :]
                    probe[index // 2, index % 2, row : row + 8, lanes] = piece
    forward(view, probe, tables, spectra)


def counts_kernel(scal, measured, counts, flags):
    for place, which in enumerate((LIVE, CORE, XLO)):
        flags[place] = jnp.full((8, SIDE), scal[which].astype(F32))
    block = measured[0, scal[SLOT]].astype(F32)
    block = pltpu.roll(block, lax.rem(SIDE - scal[MODE] * SLAB, SIDE), 1)[:, :LANES]
    lanes = lax.broadcasted_iota(jnp.int32, block.shape, 1)
    block = jnp.where(lanes < SLAB, block, 0.0)
    block = block + pltpu.roll(block, SLAB, 1)
    counts[...] = block + pltpu.roll(block, 2 * SLAB, 1)


def ratio_kernel(spectra, counts, flags, tables, out):
    real = stacked(spectra[slab_of(index), 0] for index in range(MODES))
    imag = stacked(spectra[slab_of(index), 1] for index in range(MODES))
    far_real, far_imag = columns_transform(real, imag, tables, 1.0)
    power = far_real * far_real + far_imag * far_imag
    total = power[:, :LANES] + power[:, LANES:]
    total = total + pltpu.roll(total, 2 * SLAB, 1)
    total = total + pltpu.roll(total, SLAB, 1)
    ratio = jnp.sqrt((counts[...] + SOFT_FLOOR) / (total + SOFT_FLOOR)) - 1.0
    ratio = ratio * flags[0, 0:1, :LANES]
    ratio = jnp.concatenate([ratio, ratio], axis=1)
    both = columns_transform(far_real * ratio, far_imag * ratio, tables, -1.0)
    for part in range(2):
        for place in range(MODES):
            row = slab_of(place) * SLAB
            out[place, part] = both[part][row : row + SLAB]


def backward_kernel(spectra, view, flags, tables, chi, keep, send):
    real = stacked(swap_blocks([spectra[place, 0] for place in range(MODES)]))
    imag = stacked(swap_blocks([spectra[place, 1] for place in range(MODES)]))
    chi_real, chi_imag = rows_transform(real, imag, tables, -1.0)
    view_real, view_imag = view[0], view[1]
    sums = []
    for mode in range(MODES):
        real = chi_real[mode * SLAB : (mode + 1) * SLAB]
        imag = chi_imag[mode * SLAB : (mode + 1) * SLAB]
        chi[mode, 0] = real
        chi[mode, 1] = imag
        sums.append(view_real * real + view_imag * imag)
        sums.append(view_real * imag - view_imag * real)
    sums.append((view_real * view_real + view_imag * view_imag) * flags[0, 0:1, :])
    second = jnp.broadcast_to(flags[1, 0:1, :], (16, SIDE)) > 0.5
    for index, value in enumerate(sums):
        keep[index] = jnp.where(second, value[16:], value[:16])
        send[index] = jnp.where(second, value[:16], value[16:])


def halve_kernel(mine, theirs, flags, keep, send):
    second = jnp.broadcast_to(flags[2, 0:1, :], (8, SIDE)) > 0.5
    for index in range(2 * MODES + 1):
        value = mine[index] + theirs[index]
        keep[index] = jnp.where(second, value[8:], value[:8])
        send[index] = jnp.where(second, value[:8], value[8:])


def pack_kernel(mine, theirs, packed):
    for index in range(MESSAGE):
        total = pltpu.roll(mine[index] + theirs[index], RINGS // 4, 0)
        for half in range(2):
            rows = pl.ds(MESSAGE * half + index, 8, stride=2 * MESSAGE)
            packed[rows, :] = total[:, half * LANES : (half + 1) * LANES]


def step_kernel(chi, probe, step):
    real = imag = light = 0.0
    for mode in range(MODES):
        probe_real, probe_imag = probe[mode, 0], probe[mode, 1]
        real = real + (probe_real * chi[mode, 0] + probe_imag * chi[mode, 1])
        imag = imag + (probe_real * chi[mode, 1] - probe_imag * chi[mode, 0])
        light = light + (probe_real * probe_real + probe_imag * probe_imag)
    step[0] = OBJECT_RATE * real / (light + OBJECT_DAMP)
    step[1] = OBJECT_RATE * imag / (light + OBJECT_DAMP)


def place_kernel(scal, above, step, below, band, part_band, to_left, to_right):
    cols, rest = column_window(scal)
    height = 3 * SLAB
    part_band[...] = jnp.zeros_like(part_band)
    for part in range(2):
        block = stacked([above[part], step[part], below[part]])
        block = pltpu.roll(block, lax.rem(2 * SLAB + scal[ROW], height), 0)[:BAND]
        block = jnp.concatenate([block, jnp.zeros((BAND, LANES), F32)], axis=1)
        part_band[part, :, cols] = pltpu.roll(block, rest, 1)
    to_left[...] = part_band[:, :, :SIDE]
    to_right[...] = part_band[:, :, WIDTH:]
    part_band[:, :, :WIDTH] = part_band[:, :, :WIDTH] + band[:, :, :WIDTH]
    part_band[:, :, WIDTH:] = (
        part_band[:, :, WIDTH:] * scal[HAS_NEXT].astype(F32) + band[:, :, WIDTH:]
    )


def view_kernel(scal, part_band, from_left, from_right, band, view):
    band[:, :, :SIDE] = part_band[:, :, :SIDE] + from_left[...]
    band[:, :, SIDE:WIDTH] = part_band[:, :, SIDE:WIDTH]
    band[:, :, WIDTH:] = part_band[:, :, WIDTH:] + from_right[...]
    take_patch(scal, band, view)


def probe_kernel(sums, shard_in, shard, copies):
    total = sums[:MESSAGE]
    for ring in range(1, RINGS):
        total = total + sums[ring * MESSAGE : (ring + 1) * MESSAGE]
    rows = 2 * MODES
    new = shard_in[...] + PROBE_RATE * total[:rows] / (total[rows:] + PROBE_DAMP)
    shard[...] = new
    for ring in range(RINGS):
        copies[ring] = new


def out_rows_kernel(scal, part_band, from_left, rows_out):
    slab = scal[BAND_ID]
    odd = lax.rem(slab, 2) == 1
    rows = pl.ds(pl.multiple_of(slab // 2 * 8, 8), OUT_ROWS + 4)
    for part in range(2):
        edge = part_band[part, rows, :SIDE] + from_left[part, rows, :]
        block = jnp.concatenate([edge, part_band[part, rows, SIDE:WIDTH]], axis=1)
        block = jnp.where(odd, pltpu.roll(block, OUT_ROWS, 0), block)
        rows_out[part] = block[:OUT_ROWS]


def tail_kernel(piece, rows_out, tail):
    for place in range(MODES):
        for half in range(2):
            for part in range(2):
                row = (half * 2 + part) * 8
                rows = pl.ds(RINGS * half + 2 * place + part, 8, stride=2 * RINGS)
                tail[place, row : row + 8] = piece[rows, :]
        for part in range(2):
            for block in range(WIDTH // LANES):
                row = 32 + (part * 4 + block) * OUT_ROWS
                lanes = slice(block * LANES, (block + 1) * LANES)
                tail[place, row : row + OUT_ROWS] = rows_out[part, :, lanes]


def last_kernel(tail, pieces, object_out, probe_out):
    for place in range(MODES):
        first = slab_of(place) * OUT_ROWS
        for part in range(2):
            for block in range(WIDTH // LANES):
                row = 32 + (part * 4 + block) * OUT_ROWS
                lanes = slice(block * LANES, (block + 1) * LANES)
                object_out[part, first : first + OUT_ROWS, lanes] = tail[
                    place, row : row + OUT_ROWS
                ]
    for xlo in range(2):
        for core in range(2):
            for place in range(MODES):
                first = slab_of(place) * SLAB + core * 16 + xlo * 8
                for half in range(2):
                    lanes = slice(half * LANES, (half + 1) * LANES)
                    for part in range(2):
                        row = (half * 2 + part) * 8
                        probe_out[0, part, first : first + 8, lanes] = pieces[
                            xlo, core, place, row : row + 8
                        ]


def own_kernel(place, whole, own, left, sems):
    rows = pl.ds(pl.multiple_of(place[0] * SLAB, SLAB), BAND)
    first = pltpu.make_async_copy(whole.at[:, rows, :], own, sems.at[0])
    second = pltpu.make_async_copy(whole.at[:, rows, pl.ds(0, SIDE)], left, sems.at[1])
    first.start()
    second.start()
    first.wait()
    second.wait()


def take_own(mode, object_tiles, after):
    vmem = pl.BlockSpec(memory_space=pltpu.VMEM)
    anywhere = pl.BlockSpec(memory_space=pl.ANY)

    def body(place, whole, _, own, left, sems):
        own_kernel(place, whole, own, left, sems)

    return pl.pallas_call(
        body,
        out_shape=[
            jax.ShapeDtypeStruct((2, BAND, WIDTH), F32),
            jax.ShapeDtypeStruct((2, BAND, SIDE), F32),
        ],
        in_specs=[pl.BlockSpec(memory_space=pltpu.SMEM), anywhere, anywhere],
        out_specs=[vmem, vmem],
        scratch_shapes=[pltpu.SemaphoreType.DMA((2,))],
        compiler_params=pltpu.CompilerParams(vmem_limit_bytes=VMEM_LIMIT),
        name="own_kernel",
    )(mode.astype(jnp.int32).reshape(1), object_tiles, after)


def call(kernel, outs, *args, scalars=True, after=()):
    vmem = pl.BlockSpec(memory_space=pltpu.VMEM)
    in_specs = [vmem] * len(args) + [pl.BlockSpec(memory_space=pl.ANY)] * len(after)

    def body(*refs):
        taken = list(refs[: len(args)])
        if scalars:
            taken[0] = [taken[0][0, index] for index in range(BAND_ID + 1)]
        kernel(*taken, *refs[len(args) + len(after) :])

    return pl.pallas_call(
        body,
        out_shape=[jax.ShapeDtypeStruct(shape, F32) for shape in outs],
        in_specs=in_specs,
        out_specs=[vmem] * len(outs),
        compiler_params=pltpu.CompilerParams(vmem_limit_bytes=VMEM_LIMIT),
        name=kernel.__name__,
    )(*args, *after)


def shift(value, axes, count, steps):
    first, last = max(0, -steps), min(count, count - steps)
    return lax.ppermute(value, axes, [(i, i + steps) for i in range(first, last)])


def other(value, axis):
    return lax.ppermute(value, axis, [(0, 1), (1, 0)])


def beside_slab(value, steps):
    first, last = max(0, -steps), min(MODES, MODES - steps)
    pairs = [(slab_of(i), slab_of(i + steps)) for i in range(first, last)]
    return lax.ppermute(value, MODE_AXES, pairs)


def exchange_rings(value):
    groups = [[(ring + RINGS // 2) % RINGS for ring in range(RINGS)]]
    value = value.reshape(RINGS, 1, MESSAGE * LANES)
    value = lax.all_to_all(value, "z", 0, 0, tiled=True, axis_index_groups=groups)
    return value.reshape(RINGS * MESSAGE, LANES)


def exchange(value, axes):
    return lax.all_to_all(value, axes, 0, 0, tiled=True)


def gather_pieces(piece):
    gathered = lax.all_gather(piece, ("xlo", "core"))
    return gathered.reshape((2, 2) + piece.shape)


def per_device(
    object_tiles, probe_modes, measured, row_offset, col_offset, live_counts, visit_order
):
    tables = jnp.asarray(fourier_tables())
    slots = visit_order[0]
    tile = lax.axis_index(TILE_AXES)
    mode = lax.axis_index(MODE_AXES)
    slab = jnp.where(mode < MODES // 2, mode, 11 - mode)
    (pieces,) = call(split_kernel, [(MODES, 2, SLAB, SIDE)], probe_modes, scalars=False)
    probe = exchange(pieces, MODE_AXES)
    own, left = take_own(slab, object_tiles, pieces)
    beside = shift(left, TILE_AXES, TILES, -1)
    places = [
        mode,
        lax.axis_index("core"),
        lax.axis_index("xlo"),
        lax.axis_index("z"),
        (tile < TILES - 1).astype(jnp.int32),
        slab,
    ]
    chosen = slots[:, None] == jnp.arange(STEPS, dtype=jnp.int32)[None, :]
    per_step = [
        jnp.sum(jnp.where(chosen, row_offset, 0), axis=1),
        jnp.sum(jnp.where(chosen, col_offset, 0), axis=1),
        slots,
        (slots < live_counts[0]).astype(jnp.int32),
    ]
    scalars = jnp.stack(
        per_step + [jnp.broadcast_to(place, (STEPS,)) for place in places], axis=1
    )
    slabs = (MODES, 2, SLAB, SIDE)
    slab_pair = (2, SLAB, SIDE)
    band_shape = (2, BAND, WIDE)
    edge = (2, BAND, SIDE)
    counts_shapes = [(SIDE, LANES), (3, 8, SIDE)]
    counts, flags = call(counts_kernel, counts_shapes, scalars[:1], measured)
    for step in range(STEPS):
        scal = scalars[step : step + 1]
        final = step == STEPS - 1
        if step == 0:
            band, view, shard, spectra = call(
                first_kernel,
                [band_shape, slab_pair, (2 * MODES, LANES), slabs],
                scal,
                own,
                beside,
                probe,
                tables,
                after=(counts,),
            )
        else:
            probe, spectra = call(
                next_kernel,
                [slabs, slabs],
                view,
                pieces,
                tables,
                scalars=False,
                after=(counts,),
            )
        spectra = exchange(spectra, MODE_AXES)
        (spectra,) = call(
            ratio_kernel, [slabs], spectra, counts, flags, tables, scalars=False
        )
        spectra = exchange(spectra, MODE_AXES)
        chi, keep, send = call(
            backward_kernel,
            [slabs] + [(2 * MODES + 1, 16, SIDE)] * 2,
            spectra,
            view,
            flags,
            tables,
            scalars=False,
        )
        received = other(send, "core")
        keep, send = call(
            halve_kernel, [(2 * MODES + 1, 8, SIDE)] * 2, keep, received, flags, scalars=False
        )
        received = other(send, "xlo")
        (object_step,) = call(
            step_kernel, [slab_pair], chi, probe, scalars=False, after=(keep,)
        )
        above = beside_slab(object_step, 1)
        below = beside_slab(object_step, -1)
        if not final:
            next_scal = scalars[step + 1 : step + 2]
            counts, flags = call(
                counts_kernel, counts_shapes, next_scal, measured, after=(keep,)
            )
        (packed,) = call(
            pack_kernel,
            [(RINGS * MESSAGE, LANES)],
            keep,
            received,
            scalars=False,
            after=(above,) if final else (above, counts),
        )
        sums = exchange_rings(packed)
        shard, shards = call(
            probe_kernel,
            [(2 * MODES, LANES), (RINGS, 2 * MODES, LANES)],
            sums,
            shard,
            scalars=False,
            after=(above, below),
        )
        piece = exchange(shards, "z")
        part_band, to_left, to_right = call(
            place_kernel,
            [band_shape, edge, edge],
            scal,
            above,
            object_step,
            below,
            band,
            after=(shards,),
        )
        from_left = shift(to_right, TILE_AXES, TILES, 1)
        if final:
            (rows_out,) = call(
                out_rows_kernel, [(2, OUT_ROWS, WIDTH)], scal, part_band, from_left
            )
            piece, rows_out = lax.optimization_barrier((piece, rows_out))
        else:
            from_right = shift(to_left, TILE_AXES, TILES, -1)
            band, view = call(
                view_kernel,
                [band_shape, slab_pair],
                next_scal,
                part_band,
                from_left,
                from_right,
            )
            piece, view = lax.optimization_barrier((piece, view))
            pieces = gather_pieces(piece.reshape(2 * MODES * RINGS, LANES))
    tail_rows = 32 + 8 * OUT_ROWS
    (tail,) = call(
        tail_kernel,
        [(MODES, tail_rows, LANES)],
        piece.reshape(2 * MODES * RINGS, LANES),
        rows_out,
        scalars=False,
    )
    tail = exchange(tail, MODE_AXES)
    pieces = gather_pieces(tail[:, :32])
    return call(
        last_kernel,
        [(2, HEIGHT, WIDTH), (1, 2, SIDE, SIDE)],
        tail,
        pieces,
        scalars=False,
    )


def solution(mesh):
    grid = Mesh(mesh.devices.reshape(2, 16, 2, 2, 4), TILE_AXES + MODE_AXES)
    return jax.shard_map(
        per_device,
        mesh=grid,
        in_specs=(
            P(None, None, TILE_AXES),
            P(MODE_AXES, None, None, None),
            P(TILE_AXES, None, None, None),
            P(TILE_AXES, None),
            P(TILE_AXES, None),
            P(TILE_AXES),
            P(TILE_AXES, None),
        ),
        out_specs=(P(None, None, TILE_AXES), P(MODE_AXES, None, None, None)),
        check_vma=False,
    )
```

```python
import math

import jax
import jax.numpy as jnp
import numpy as np
from jax import lax
from jax.experimental import pallas as pl
from jax.experimental.pallas import tpu as pltpu
from jax.sharding import Mesh
from jax.sharding import PartitionSpec as P

SOFT_FLOOR = 0.5
OBJECT_RATE = 1.0
OBJECT_DAMP = 0.5
PROBE_RATE = 1.0
PROBE_DAMP = 1.0

SIDE = 256
HEIGHT = 288
WIDTH = 512
WIDE = WIDTH + SIDE
MODES = 8
SLAB = SIDE // MODES
BAND = 2 * SLAB
STEPS = 3
TILES = 64
RINGS = 16
LANES = 128
COL_SPAN = SIDE + LANES
OUT_ROWS = HEIGHT // MODES
MESSAGE = 2 * MODES + 1
VMEM_LIMIT = 16 * 1024 * 1024

TILE_AXES = ("xlo", "z", "core")
MODE_AXES = ("xhi", "y")

ROW, COL, SLOT, LIVE, MODE, CORE, XLO, RING, HAS_NEXT, BAND_ID = range(10)

F32 = jnp.float32
BF16 = jnp.bfloat16


def slab_of(place):
    return place if place < MODES // 2 else 11 - place


def fourier_tables():
    index = np.arange(SIDE)
    angles = (index[:, None] * index[None, :] % SIDE) * (2.0 * math.pi / SIDE)
    cosine, sine = np.cos(angles) / math.sqrt(SIDE), np.sin(angles) / math.sqrt(SIDE)
    exact = np.stack([cosine, cosine + sine, cosine - sine])
    high = exact.astype(jnp.bfloat16)
    low = (exact - high.astype(np.float64)).astype(jnp.bfloat16)
    return np.stack([high, low], axis=1)


def halves(value):
    high = value.astype(BF16)
    return high, (value - high.astype(F32)).astype(BF16)


def dot(left, right):
    return jnp.dot(left, right, preferred_element_type=F32)


def transform(real, imag, by, direction):
    turned = direction * imag
    shared = by(0, real + turned)
    return shared - by(2, turned), direction * (shared - by(1, real))


def rows_transform(real, imag, tables, direction):
    def by(which, value):
        high, low = halves(value)
        return (
            dot(high, tables[which, 0]) + dot(low, tables[which, 0]) + dot(high, tables[which, 1])
        )

    return transform(real, imag, by, direction)


def columns_transform(real, imag, tables, direction):
    def by(which, value):
        high, low = halves(value)
        return (
            dot(tables[which, 0], high) + dot(tables[which, 0], low) + dot(tables[which, 1], high)
        )

    return transform(real, imag, by, direction)


def swap_blocks(parts):
    lanes = lax.broadcasted_iota(jnp.int32, (parts[0].shape[0], LANES), 1)
    grid = [[part[:, :LANES], part[:, LANES:]] for part in parts]
    grid = [[grid[(m & 3) | (h << 2)][m >> 2] for h in range(2)] for m in range(MODES)]
    for bit in (2, 1):
        shift = bit * SLAB
        low = (lanes & shift) == 0
        new = [None] * MODES
        for m in range(MODES):
            if m & bit:
                continue
            a, b = grid[m], grid[m | bit]
            new[m] = [jnp.where(low, a[h], pltpu.roll(b[h], shift, 1)) for h in range(2)]
            new[m | bit] = [
                jnp.where(low, pltpu.roll(a[h], LANES - shift, 1), b[h]) for h in range(2)
            ]
        grid = new
    return [jnp.concatenate(pair, axis=1) for pair in grid]


def stacked(pieces):
    return jnp.concatenate(list(pieces), axis=0)


def column_window(scal):
    col = scal[COL]
    block = jnp.minimum(col // LANES, WIDTH // LANES - 1)
    return pl.ds(pl.multiple_of(block * LANES, LANES), COL_SPAN), col - block * LANES


def take_patch(scal, band, view):
    cols, rest = column_window(scal)
    for part in range(2):
        block = band[part, :, cols]
        block = pltpu.roll(block, lax.rem(COL_SPAN - rest, COL_SPAN), 1)[:, :SIDE]
        view[part] = pltpu.roll(block, lax.rem(BAND - scal[ROW], BAND), 0)[:SLAB]


def forward(view, probe, tables, spectra):
    view_real = stacked([view[0]] * MODES)
    view_imag = stacked([view[1]] * MODES)
    probe_real = stacked(probe[mode, 0] for mode in range(MODES))
    probe_imag = stacked(probe[mode, 1] for mode in range(MODES))
    both = rows_transform(
        probe_real * view_real - probe_imag * view_imag,
        probe_real * view_imag + probe_imag * view_real,
        tables,
        1.0,
    )
    for part in range(2):
        blocks = [both[part][mode * SLAB : (mode + 1) * SLAB] for mode in range(MODES)]
        for place, block in enumerate(swap_blocks(blocks)):
            spectra[place, part] = block


def split_kernel(probe_in, pieces):
    for place in range(MODES):
        row = slab_of(place) * SLAB
        pieces[place] = probe_in[0, :, row : row + SLAB, :]


def first_kernel(scal, own, beside, probe, tables, band, view, shard, spectra):
    band[:, :, :WIDTH] = own[...]
    band[:, :, WIDTH:] = beside[...]
    take_patch(scal, band, view)
    rows = pl.ds(pl.multiple_of(scal[CORE] * 16 + scal[XLO] * 8, 8), 8)
    wanted = lax.broadcasted_iota(jnp.int32, (8, LANES), 0) == scal[RING] // 2
    second = lax.rem(scal[RING], 2) == 1
    for mode in range(MODES):
        for part in range(2):
            block = jnp.where(second, probe[mode, part, rows, LANES:], probe[mode, part, rows, :LANES])
            index = 2 * mode + part
            shard[index : index + 1] = jnp.sum(
                jnp.where(wanted, block, 0.0), axis=0, keepdims=True
            )
    forward(view, probe, tables, spectra)


def next_kernel(view, pieces, tables, probe, spectra):
    for xlo in range(2):
        for core in range(2):
            row = core * 16 + xlo * 8
            for index in range(2 * MODES):
                for half in range(2):
                    lanes = slice(half * LANES, (half + 1) * LANES)
                    piece = pieces[xlo, core, pl.ds(RINGS * half + index, 8, stride=2 * RINGS), :]
                    probe[index // 2, index % 2, row : row + 8, lanes] = piece
    forward(view, probe, tables, spectra)


def counts_kernel(scal, measured, counts, flags):
    for place, which in enumerate((LIVE, CORE, XLO)):
        flags[place] = jnp.full((8, SIDE), scal[which].astype(F32))
    block = measured[0, scal[SLOT]].astype(F32)
    block = pltpu.roll(block, lax.rem(SIDE - scal[MODE] * SLAB, SIDE), 1)[:, :LANES]
    lanes = lax.broadcasted_iota(jnp.int32, block.shape, 1)
    block = jnp.where(lanes < SLAB, block, 0.0)
    block = block + pltpu.roll(block, SLAB, 1)
    counts[...] = block + pltpu.roll(block, 2 * SLAB, 1)


def ratio_kernel(spectra, counts, flags, tables, out):
    real = stacked(spectra[slab_of(index), 0] for index in range(MODES))
    imag = stacked(spectra[slab_of(index), 1] for index in range(MODES))
    far_real, far_imag = columns_transform(real, imag, tables, 1.0)
    power = far_real * far_real + far_imag * far_imag
    total = power[:, :LANES] + power[:, LANES:]
    total = total + pltpu.roll(total, 2 * SLAB, 1)
    total = total + pltpu.roll(total, SLAB, 1)
    ratio = jnp.sqrt((counts[...] + SOFT_FLOOR) / (total + SOFT_FLOOR)) - 1.0
    ratio = ratio * flags[0, 0:1, :LANES]
    ratio = jnp.concatenate([ratio, ratio], axis=1)
    both = columns_transform(far_real * ratio, far_imag * ratio, tables, -1.0)
    for part in range(2):
        for place in range(MODES):
            row = slab_of(place) * SLAB
            out[place, part] = both[part][row : row + SLAB]


def backward_kernel(spectra, view, flags, tables, chi, keep, send):
    real = stacked(swap_blocks([spectra[place, 0] for place in range(MODES)]))
    imag = stacked(swap_blocks([spectra[place, 1] for place in range(MODES)]))
    chi_real, chi_imag = rows_transform(real, imag, tables, -1.0)
    view_real, view_imag = view[0], view[1]
    sums = []
    for mode in range(MODES):
        real = chi_real[mode * SLAB : (mode + 1) * SLAB]
        imag = chi_imag[mode * SLAB : (mode + 1) * SLAB]
        chi[mode, 0] = real
        chi[mode, 1] = imag
        sums.append(view_real * real + view_imag * imag)
        sums.append(view_real * imag - view_imag * real)
    sums.append((view_real * view_real + view_imag * view_imag) * flags[0, 0:1, :])
    second = jnp.broadcast_to(flags[1, 0:1, :], (16, SIDE)) > 0.5
    for index, value in enumerate(sums):
        keep[index] = jnp.where(second, value[16:], value[:16])
        send[index] = jnp.where(second, value[:16], value[16:])


def halve_kernel(mine, theirs, flags, keep, send):
    second = jnp.broadcast_to(flags[2, 0:1, :], (8, SIDE)) > 0.5
    for index in range(2 * MODES + 1):
        value = mine[index] + theirs[index]
        keep[index] = jnp.where(second, value[8:], value[:8])
        send[index] = jnp.where(second, value[:8], value[8:])


def pack_kernel(mine, theirs, packed):
    for index in range(MESSAGE):
        total = pltpu.roll(mine[index] + theirs[index], RINGS // 4, 0)
        for half in range(2):
            rows = pl.ds(MESSAGE * half + index, 8, stride=2 * MESSAGE)
            packed[rows, :] = total[:, half * LANES : (half + 1) * LANES]


def step_kernel(chi, probe, step):
    real = imag = light = 0.0
    for mode in range(MODES):
        probe_real, probe_imag = probe[mode, 0], probe[mode, 1]
        real = real + (probe_real * chi[mode, 0] + probe_imag * chi[mode, 1])
        imag = imag + (probe_real * chi[mode, 1] - probe_imag * chi[mode, 0])
        light = light + (probe_real * probe_real + probe_imag * probe_imag)
    step[0] = OBJECT_RATE * real / (light + OBJECT_DAMP)
    step[1] = OBJECT_RATE * imag / (light + OBJECT_DAMP)


def place_kernel(scal, above, step, below, band, part_band, to_right, to_left=None):
    cols, rest = column_window(scal)
    height = 3 * SLAB
    part_band[...] = jnp.zeros_like(part_band)
    for part in range(2):
        block = stacked([above[part], step[part], below[part]])
        block = pltpu.roll(block, lax.rem(2 * SLAB + scal[ROW], height), 0)[:BAND]
        block = jnp.concatenate([block, jnp.zeros((BAND, LANES), F32)], axis=1)
        part_band[part, :, cols] = pltpu.roll(block, rest, 1)
    if to_left is not None:
        to_left[...] = part_band[:, :, :SIDE]
    to_right[...] = part_band[:, :, WIDTH:]
    part_band[:, :, :WIDTH] = part_band[:, :, :WIDTH] + band[:, :, :WIDTH]
    part_band[:, :, WIDTH:] = (
        part_band[:, :, WIDTH:] * scal[HAS_NEXT].astype(F32) + band[:, :, WIDTH:]
    )


def view_kernel(scal, part_band, from_left, from_right, band, view):
    band[:, :, :SIDE] = part_band[:, :, :SIDE] + from_left[...]
    band[:, :, SIDE:WIDTH] = part_band[:, :, SIDE:WIDTH]
    band[:, :, WIDTH:] = part_band[:, :, WIDTH:] + from_right[...]
    take_patch(scal, band, view)


def probe_kernel(sums, shard_in, shard, copies):
    total = sums[:MESSAGE]
    for ring in range(1, RINGS):
        total = total + sums[ring * MESSAGE : (ring + 1) * MESSAGE]
    rows = 2 * MODES
    new = shard_in[...] + PROBE_RATE * total[:rows] / (total[rows:] + PROBE_DAMP)
    shard[...] = new
    for ring in range(RINGS):
        copies[ring] = new


def out_rows_kernel(scal, part_band, from_left, rows_out):
    slab = scal[BAND_ID]
    odd = lax.rem(slab, 2) == 1
    rows = pl.ds(pl.multiple_of(slab // 2 * 8, 8), OUT_ROWS + 4)
    for part in range(2):
        edge = part_band[part, rows, :SIDE] + from_left[part, rows, :]
        block = jnp.concatenate([edge, part_band[part, rows, SIDE:WIDTH]], axis=1)
        block = jnp.where(odd, pltpu.roll(block, OUT_ROWS, 0), block)
        rows_out[part] = block[:OUT_ROWS]


def tail_kernel(piece, rows_out, tail):
    for place in range(MODES):
        for half in range(2):
            for part in range(2):
                row = (half * 2 + part) * 8
                rows = pl.ds(RINGS * half + 2 * place + part, 8, stride=2 * RINGS)
                tail[place, row : row + 8] = piece[rows, :]
        for part in range(2):
            for block in range(WIDTH // LANES):
                row = 32 + (part * 4 + block) * OUT_ROWS
                lanes = slice(block * LANES, (block + 1) * LANES)
                tail[place, row : row + OUT_ROWS] = rows_out[part, :, lanes]


def last_kernel(tail, pieces, object_out, probe_out):
    for place in range(MODES):
        first = slab_of(place) * OUT_ROWS
        for part in range(2):
            for block in range(WIDTH // LANES):
                row = 32 + (part * 4 + block) * OUT_ROWS
                lanes = slice(block * LANES, (block + 1) * LANES)
                object_out[part, first : first + OUT_ROWS, lanes] = tail[
                    place, row : row + OUT_ROWS
                ]
    for xlo in range(2):
        for core in range(2):
            for place in range(MODES):
                first = slab_of(place) * SLAB + core * 16 + xlo * 8
                for half in range(2):
                    lanes = slice(half * LANES, (half + 1) * LANES)
                    for part in range(2):
                        row = (half * 2 + part) * 8
                        probe_out[0, part, first : first + 8, lanes] = pieces[
                            xlo, core, place, row : row + 8
                        ]


def own_kernel(place, whole, own, left, sems):
    rows = pl.ds(pl.multiple_of(place[0] * SLAB, SLAB), BAND)
    first = pltpu.make_async_copy(whole.at[:, rows, :], own, sems.at[0])
    second = pltpu.make_async_copy(whole.at[:, rows, pl.ds(0, SIDE)], left, sems.at[1])
    first.start()
    second.start()
    first.wait()
    second.wait()


def take_own(mode, object_tiles, after):
    vmem = pl.BlockSpec(memory_space=pltpu.VMEM)
    anywhere = pl.BlockSpec(memory_space=pl.ANY)

    def body(place, whole, _, own, left, sems):
        own_kernel(place, whole, own, left, sems)

    return pl.pallas_call(
        body,
        out_shape=[
            jax.ShapeDtypeStruct((2, BAND, WIDTH), F32),
            jax.ShapeDtypeStruct((2, BAND, SIDE), F32),
        ],
        in_specs=[pl.BlockSpec(memory_space=pltpu.SMEM), anywhere, anywhere],
        out_specs=[vmem, vmem],
        scratch_shapes=[pltpu.SemaphoreType.DMA((2,))],
        compiler_params=pltpu.CompilerParams(vmem_limit_bytes=VMEM_LIMIT),
        name="own_kernel",
    )(mode.astype(jnp.int32).reshape(1), object_tiles, after)


def call(kernel, outs, *args, scalars=True, after=()):
    vmem = pl.BlockSpec(memory_space=pltpu.VMEM)
    in_specs = [vmem] * len(args) + [pl.BlockSpec(memory_space=pl.ANY)] * len(after)

    def body(*refs):
        taken = list(refs[: len(args)])
        if scalars:
            taken[0] = [taken[0][0, index] for index in range(BAND_ID + 1)]
        kernel(*taken, *refs[len(args) + len(after) :])

    return pl.pallas_call(
        body,
        out_shape=[jax.ShapeDtypeStruct(shape, F32) for shape in outs],
        in_specs=in_specs,
        out_specs=[vmem] * len(outs),
        compiler_params=pltpu.CompilerParams(vmem_limit_bytes=VMEM_LIMIT),
        name=kernel.__name__,
    )(*args, *after)


def shift(value, axes, count, steps):
    first, last = max(0, -steps), min(count, count - steps)
    return lax.ppermute(value, axes, [(i, i + steps) for i in range(first, last)])


def other(value, axis):
    return lax.ppermute(value, axis, [(0, 1), (1, 0)])


def beside_slab(value, steps):
    first, last = max(0, -steps), min(MODES, MODES - steps)
    pairs = [(slab_of(i), slab_of(i + steps)) for i in range(first, last)]
    return lax.ppermute(value, MODE_AXES, pairs)


def exchange_rings(value):
    groups = [[(ring + RINGS // 2) % RINGS for ring in range(RINGS)]]
    value = value.reshape(RINGS, 1, MESSAGE * LANES)
    value = lax.all_to_all(value, "z", 0, 0, tiled=True, axis_index_groups=groups)
    return value.reshape(RINGS * MESSAGE, LANES)


def exchange(value, axes):
    return lax.all_to_all(value, axes, 0, 0, tiled=True)


def gather_pieces(piece):
    gathered = lax.all_gather(piece, ("xlo", "core"))
    return gathered.reshape((2, 2) + piece.shape)


def per_device(
    object_tiles, probe_modes, measured, row_offset, col_offset, live_counts, visit_order
):
    tables = jnp.asarray(fourier_tables())
    slots = visit_order[0]
    tile = lax.axis_index(TILE_AXES)
    mode = lax.axis_index(MODE_AXES)
    slab = jnp.where(mode < MODES // 2, mode, 11 - mode)
    (pieces,) = call(split_kernel, [(MODES, 2, SLAB, SIDE)], probe_modes, scalars=False)
    probe = exchange(pieces, MODE_AXES)
    own, left = take_own(slab, object_tiles, pieces)
    beside = shift(left, TILE_AXES, TILES, -1)
    places = [
        mode,
        lax.axis_index("core"),
        lax.axis_index("xlo"),
        lax.axis_index("z"),
        (tile < TILES - 1).astype(jnp.int32),
        slab,
    ]
    chosen = slots[:, None] == jnp.arange(STEPS, dtype=jnp.int32)[None, :]
    per_step = [
        jnp.sum(jnp.where(chosen, row_offset, 0), axis=1),
        jnp.sum(jnp.where(chosen, col_offset, 0), axis=1),
        slots,
        (slots < live_counts[0]).astype(jnp.int32),
    ]
    scalars = jnp.stack(
        per_step + [jnp.broadcast_to(place, (STEPS,)) for place in places], axis=1
    )
    slabs = (MODES, 2, SLAB, SIDE)
    slab_pair = (2, SLAB, SIDE)
    band_shape = (2, BAND, WIDE)
    edge = (2, BAND, SIDE)
    counts_shapes = [(SIDE, LANES), (3, 8, SIDE)]
    counts, flags = call(counts_kernel, counts_shapes, scalars[:1], measured)
    for step in range(STEPS):
        scal = scalars[step : step + 1]
        final = step == STEPS - 1
        if step == 0:
            band, view, shard, spectra = call(
                first_kernel,
                [band_shape, slab_pair, (2 * MODES, LANES), slabs],
                scal,
                own,
                beside,
                probe,
                tables,
                after=(counts,),
            )
        else:
            probe, spectra = call(
                next_kernel,
                [slabs, slabs],
                view,
                pieces,
                tables,
                scalars=False,
                after=(counts,),
            )
        spectra = exchange(spectra, MODE_AXES)
        (spectra,) = call(
            ratio_kernel, [slabs], spectra, counts, flags, tables, scalars=False
        )
        spectra = exchange(spectra, MODE_AXES)
        chi, keep, send = call(
            backward_kernel,
            [slabs] + [(2 * MODES + 1, 16, SIDE)] * 2,
            spectra,
            view,
            flags,
            tables,
            scalars=False,
        )
        received = other(send, "core")
        keep, send = call(
            halve_kernel, [(2 * MODES + 1, 8, SIDE)] * 2, keep, received, flags, scalars=False
        )
        received = other(send, "xlo")
        (object_step,) = call(
            step_kernel, [slab_pair], chi, probe, scalars=False, after=(keep,)
        )
        above = beside_slab(object_step, 1)
        below = beside_slab(object_step, -1)
        if not final:
            next_scal = scalars[step + 1 : step + 2]
            counts, flags = call(
                counts_kernel, counts_shapes, next_scal, measured, after=(keep,)
            )
        (packed,) = call(
            pack_kernel,
            [(RINGS * MESSAGE, LANES)],
            keep,
            received,
            scalars=False,
            after=(object_step,) if final else (object_step, counts),
        )
        sums = exchange_rings(packed)
        shard, shards = call(
            probe_kernel,
            [(2 * MODES, LANES), (RINGS, 2 * MODES, LANES)],
            sums,
            shard,
            scalars=False,
            after=(above, below),
        )
        piece = exchange(shards, "z")
        part_band, to_right, *to_left = call(
            place_kernel,
            [band_shape, edge] if final else [band_shape, edge, edge],
            scal,
            above,
            object_step,
            below,
            band,
            after=(shards,),
        )
        from_left = shift(to_right, TILE_AXES, TILES, 1)
        if final:
            (rows_out,) = call(
                out_rows_kernel, [(2, OUT_ROWS, WIDTH)], scal, part_band, from_left
            )
            piece, rows_out = lax.optimization_barrier((piece, rows_out))
        else:
            from_right = shift(to_left[0], TILE_AXES, TILES, -1)
            band, view = call(
                view_kernel,
                [band_shape, slab_pair],
                next_scal,
                part_band,
                from_left,
                from_right,
            )
            piece, view = lax.optimization_barrier((piece, view))
            pieces = gather_pieces(piece.reshape(2 * MODES * RINGS, LANES))
    tail_rows = 32 + 8 * OUT_ROWS
    (tail,) = call(
        tail_kernel,
        [(MODES, tail_rows, LANES)],
        piece.reshape(2 * MODES * RINGS, LANES),
        rows_out,
        scalars=False,
    )
    tail = exchange(tail, MODE_AXES)
    pieces = gather_pieces(tail[:, :32])
    return call(
        last_kernel,
        [(2, HEIGHT, WIDTH), (1, 2, SIDE, SIDE)],
        tail,
        pieces,
        scalars=False,
    )


def solution(mesh):
    grid = Mesh(mesh.devices.reshape(2, 16, 2, 2, 4), TILE_AXES + MODE_AXES)
    return jax.shard_map(
        per_device,
        mesh=grid,
        in_specs=(
            P(None, None, TILE_AXES),
            P(MODE_AXES, None, None, None),
            P(TILE_AXES, None, None, None),
            P(TILE_AXES, None),
            P(TILE_AXES, None),
            P(TILE_AXES),
            P(TILE_AXES, None),
        ),
        out_specs=(P(None, None, TILE_AXES), P(MODE_AXES, None, None, None)),
        check_vma=False,
    )
```

```python
import math

import jax
import jax.numpy as jnp
import numpy as np
from jax import lax
from jax.experimental import pallas as pl
from jax.experimental.pallas import tpu as pltpu
from jax.sharding import Mesh
from jax.sharding import PartitionSpec as P

SOFT_FLOOR = 0.5
OBJECT_RATE = 1.0
OBJECT_DAMP = 0.5
PROBE_RATE = 1.0
PROBE_DAMP = 1.0

SIDE = 256
HEIGHT = 288
WIDTH = 512
WIDE = WIDTH + SIDE
MODES = 8
SLAB = SIDE // MODES
BAND = 2 * SLAB
STEPS = 3
TILES = 64
RINGS = 16
LANES = 128
COL_SPAN = SIDE + LANES
OUT_ROWS = HEIGHT // MODES
MESSAGE = 2 * MODES + 1
VMEM_LIMIT = 16 * 1024 * 1024

TILE_AXES = ("xlo", "z", "core")
MODE_AXES = ("xhi", "y")

ROW, COL, SLOT, LIVE, MODE, CORE, XLO, RING, HAS_NEXT, BAND_ID = range(10)

F32 = jnp.float32
BF16 = jnp.bfloat16


def slab_of(place):
    return place if place < MODES // 2 else 11 - place


def fourier_tables():
    index = np.arange(SIDE)
    angles = (index[:, None] * index[None, :] % SIDE) * (2.0 * math.pi / SIDE)
    cosine, sine = np.cos(angles) / math.sqrt(SIDE), np.sin(angles) / math.sqrt(SIDE)
    exact = np.stack([cosine, cosine + sine, cosine - sine])
    high = exact.astype(jnp.bfloat16)
    low = (exact - high.astype(np.float64)).astype(jnp.bfloat16)
    return np.stack([high, low], axis=1)


def halves(value):
    high = value.astype(BF16)
    return high, (value - high.astype(F32)).astype(BF16)


def dot(left, right):
    return jnp.dot(left, right, preferred_element_type=F32)


def transform(real, imag, by, direction):
    turned = direction * imag
    shared = by(0, real + turned)
    return shared - by(2, turned), direction * (shared - by(1, real))


def rows_transform(real, imag, tables, direction):
    def by(which, value):
        high, low = halves(value)
        return (
            dot(high, tables[which, 0]) + dot(low, tables[which, 0]) + dot(high, tables[which, 1])
        )

    return transform(real, imag, by, direction)


def columns_transform(real, imag, tables, direction):
    def by(which, value):
        high, low = halves(value)
        return (
            dot(tables[which, 0], high) + dot(tables[which, 0], low) + dot(tables[which, 1], high)
        )

    return transform(real, imag, by, direction)


def swap_blocks(parts):
    lanes = lax.broadcasted_iota(jnp.int32, (parts[0].shape[0], LANES), 1)
    grid = [[part[:, :LANES], part[:, LANES:]] for part in parts]
    grid = [[grid[(m & 3) | (h << 2)][m >> 2] for h in range(2)] for m in range(MODES)]
    for bit in (2, 1):
        shift = bit * SLAB
        low = (lanes & shift) == 0
        new = [None] * MODES
        for m in range(MODES):
            if m & bit:
                continue
            a, b = grid[m], grid[m | bit]
            new[m] = [jnp.where(low, a[h], pltpu.roll(b[h], shift, 1)) for h in range(2)]
            new[m | bit] = [
                jnp.where(low, pltpu.roll(a[h], LANES - shift, 1), b[h]) for h in range(2)
            ]
        grid = new
    return [jnp.concatenate(pair, axis=1) for pair in grid]


def stacked(pieces):
    return jnp.concatenate(list(pieces), axis=0)


def column_window(scal):
    col = scal[COL]
    block = jnp.minimum(col // LANES, WIDTH // LANES - 1)
    return pl.ds(pl.multiple_of(block * LANES, LANES), COL_SPAN), col - block * LANES


def take_patch(scal, band, view):
    cols, rest = column_window(scal)
    for part in range(2):
        block = band[part, :, cols]
        block = pltpu.roll(block, lax.rem(COL_SPAN - rest, COL_SPAN), 1)[:, :SIDE]
        view[part] = pltpu.roll(block, lax.rem(BAND - scal[ROW], BAND), 0)[:SLAB]


def forward(view, probe, tables, spectra):
    view_real = stacked([view[0]] * MODES)
    view_imag = stacked([view[1]] * MODES)
    probe_real = stacked(probe[mode, 0] for mode in range(MODES))
    probe_imag = stacked(probe[mode, 1] for mode in range(MODES))
    both = rows_transform(
        probe_real * view_real - probe_imag * view_imag,
        probe_real * view_imag + probe_imag * view_real,
        tables,
        1.0,
    )
    for part in range(2):
        blocks = [both[part][mode * SLAB : (mode + 1) * SLAB] for mode in range(MODES)]
        for place, block in enumerate(swap_blocks(blocks)):
            spectra[place, part] = block


def split_kernel(probe_in, pieces):
    for place in range(MODES):
        row = slab_of(place) * SLAB
        pieces[place] = probe_in[0, :, row : row + SLAB, :]


def first_kernel(scal, own, beside, probe, tables, band, view, shard, spectra):
    band[:, :, :WIDTH] = own[...]
    band[:, :, WIDTH:] = beside[...]
    take_patch(scal, band, view)
    rows = pl.ds(pl.multiple_of(scal[CORE] * 16 + scal[XLO] * 8, 8), 8)
    wanted = lax.broadcasted_iota(jnp.int32, (8, LANES), 0) == scal[RING] // 2
    second = lax.rem(scal[RING], 2) == 1
    for mode in range(MODES):
        for part in range(2):
            block = jnp.where(second, probe[mode, part, rows, LANES:], probe[mode, part, rows, :LANES])
            index = 2 * mode + part
            shard[index : index + 1] = jnp.sum(
                jnp.where(wanted, block, 0.0), axis=0, keepdims=True
            )
    forward(view, probe, tables, spectra)


def next_kernel(view, pieces, tables, probe, spectra):
    for xlo in range(2):
        for core in range(2):
            row = core * 16 + xlo * 8
            for index in range(2 * MODES):
                for half in range(2):
                    lanes = slice(half * LANES, (half + 1) * LANES)
                    piece = pieces[xlo, core, pl.ds(RINGS * half + index, 8, stride=2 * RINGS), :]
                    probe[index // 2, index % 2, row : row + 8, lanes] = piece
    forward(view, probe, tables, spectra)


def counts_kernel(scal, measured, counts, flags):
    for place, which in enumerate((LIVE, CORE, XLO)):
        flags[place] = jnp.full((8, SIDE), scal[which].astype(F32))
    block = measured[0, scal[SLOT]].astype(F32)
    block = pltpu.roll(block, lax.rem(SIDE - scal[MODE] * SLAB, SIDE), 1)[:, :LANES]
    lanes = lax.broadcasted_iota(jnp.int32, block.shape, 1)
    block = jnp.where(lanes < SLAB, block, 0.0)
    block = block + pltpu.roll(block, SLAB, 1)
    counts[...] = block + pltpu.roll(block, 2 * SLAB, 1)


def ratio_kernel(spectra, counts, flags, tables, out):
    real = stacked(spectra[slab_of(index), 0] for index in range(MODES))
    imag = stacked(spectra[slab_of(index), 1] for index in range(MODES))
    far_real, far_imag = columns_transform(real, imag, tables, 1.0)
    power = far_real * far_real + far_imag * far_imag
    total = power[:, :LANES] + power[:, LANES:]
    total = total + pltpu.roll(total, 2 * SLAB, 1)
    total = total + pltpu.roll(total, SLAB, 1)
    ratio = jnp.sqrt((counts[...] + SOFT_FLOOR) / (total + SOFT_FLOOR)) - 1.0
    ratio = ratio * flags[0, 0:1, :LANES]
    ratio = jnp.concatenate([ratio, ratio], axis=1)
    both = columns_transform(far_real * ratio, far_imag * ratio, tables, -1.0)
    for part in range(2):
        for place in range(MODES):
            row = slab_of(place) * SLAB
            out[place, part] = both[part][row : row + SLAB]


def backward_kernel(spectra, view, flags, tables, chi, keep, send):
    real = stacked(swap_blocks([spectra[place, 0] for place in range(MODES)]))
    imag = stacked(swap_blocks([spectra[place, 1] for place in range(MODES)]))
    chi_real, chi_imag = rows_transform(real, imag, tables, -1.0)
    view_real, view_imag = view[0], view[1]
    sums = []
    for mode in range(MODES):
        real = chi_real[mode * SLAB : (mode + 1) * SLAB]
        imag = chi_imag[mode * SLAB : (mode + 1) * SLAB]
        chi[mode, 0] = real
        chi[mode, 1] = imag
        sums.append(view_real * real + view_imag * imag)
        sums.append(view_real * imag - view_imag * real)
    sums.append((view_real * view_real + view_imag * view_imag) * flags[0, 0:1, :])
    second = jnp.broadcast_to(flags[1, 0:1, :], (16, SIDE)) > 0.5
    for index, value in enumerate(sums):
        keep[index] = jnp.where(second, value[16:], value[:16])
        send[index] = jnp.where(second, value[:16], value[16:])


def halve_kernel(mine, theirs, flags, keep, send):
    second = jnp.broadcast_to(flags[2, 0:1, :], (8, SIDE)) > 0.5
    for index in range(2 * MODES + 1):
        value = mine[index] + theirs[index]
        keep[index] = jnp.where(second, value[8:], value[:8])
        send[index] = jnp.where(second, value[:8], value[8:])


def pack_kernel(mine, theirs, packed):
    for index in range(MESSAGE):
        total = pltpu.roll(mine[index] + theirs[index], RINGS // 4, 0)
        for half in range(2):
            rows = pl.ds(MESSAGE * half + index, 8, stride=2 * MESSAGE)
            packed[rows, :] = total[:, half * LANES : (half + 1) * LANES]


def step_kernel(chi, probe, step):
    real = imag = light = 0.0
    for mode in range(MODES):
        probe_real, probe_imag = probe[mode, 0], probe[mode, 1]
        real = real + (probe_real * chi[mode, 0] + probe_imag * chi[mode, 1])
        imag = imag + (probe_real * chi[mode, 1] - probe_imag * chi[mode, 0])
        light = light + (probe_real * probe_real + probe_imag * probe_imag)
    step[0] = OBJECT_RATE * real / (light + OBJECT_DAMP)
    step[1] = OBJECT_RATE * imag / (light + OBJECT_DAMP)


def place_kernel(scal, above, step, below, band, part_band, to_right, to_left=None):
    cols, rest = column_window(scal)
    height = 3 * SLAB
    part_band[...] = jnp.zeros_like(part_band)
    for part in range(2):
        block = stacked([above[part], step[part], below[part]])
        block = pltpu.roll(block, lax.rem(2 * SLAB + scal[ROW], height), 0)[:BAND]
        block = jnp.concatenate([block, jnp.zeros((BAND, LANES), F32)], axis=1)
        part_band[part, :, cols] = pltpu.roll(block, rest, 1)
    if to_left is not None:
        to_left[...] = part_band[:, :, :SIDE]
    to_right[...] = part_band[:, :, WIDTH:]
    part_band[:, :, :WIDTH] = part_band[:, :, :WIDTH] + band[:, :, :WIDTH]
    part_band[:, :, WIDTH:] = (
        part_band[:, :, WIDTH:] * scal[HAS_NEXT].astype(F32) + band[:, :, WIDTH:]
    )


def view_kernel(scal, part_band, from_left, from_right, band, view):
    band[:, :, :SIDE] = part_band[:, :, :SIDE] + from_left[...]
    band[:, :, SIDE:WIDTH] = part_band[:, :, SIDE:WIDTH]
    band[:, :, WIDTH:] = part_band[:, :, WIDTH:] + from_right[...]
    take_patch(scal, band, view)


def probe_kernel(sums, shard_in, shard, copies):
    total = sums[:MESSAGE]
    for ring in range(1, RINGS):
        total = total + sums[ring * MESSAGE : (ring + 1) * MESSAGE]
    rows = 2 * MODES
    new = shard_in[...] + PROBE_RATE * total[:rows] / (total[rows:] + PROBE_DAMP)
    shard[...] = new
    for ring in range(RINGS):
        copies[ring] = new


def out_rows_kernel(scal, part_band, from_left, rows_out):
    slab = scal[BAND_ID]
    odd = lax.rem(slab, 2) == 1
    rows = pl.ds(pl.multiple_of(slab // 2 * 8, 8), OUT_ROWS + 4)
    for part in range(2):
        edge = part_band[part, rows, :SIDE] + from_left[part, rows, :]
        block = jnp.concatenate([edge, part_band[part, rows, SIDE:WIDTH]], axis=1)
        block = jnp.where(odd, pltpu.roll(block, OUT_ROWS, 0), block)
        rows_out[part] = block[:OUT_ROWS]


def tail_kernel(piece, rows_out, tail):
    for place in range(MODES):
        for half in range(2):
            for part in range(2):
                row = (half * 2 + part) * 8
                rows = pl.ds(RINGS * half + 2 * place + part, 8, stride=2 * RINGS)
                tail[place, row : row + 8] = piece[rows, :]
        for part in range(2):
            for block in range(WIDTH // LANES):
                row = 32 + (part * 4 + block) * OUT_ROWS
                lanes = slice(block * LANES, (block + 1) * LANES)
                tail[place, row : row + OUT_ROWS] = rows_out[part, :, lanes]


def last_kernel(tail, pieces, object_out, probe_out):
    for place in range(MODES):
        first = slab_of(place) * OUT_ROWS
        for part in range(2):
            for block in range(WIDTH // LANES):
                row = 32 + (part * 4 + block) * OUT_ROWS
                lanes = slice(block * LANES, (block + 1) * LANES)
                object_out[part, first : first + OUT_ROWS, lanes] = tail[
                    place, row : row + OUT_ROWS
                ]
    for xlo in range(2):
        for core in range(2):
            for place in range(MODES):
                first = slab_of(place) * SLAB + core * 16 + xlo * 8
                for half in range(2):
                    lanes = slice(half * LANES, (half + 1) * LANES)
                    for part in range(2):
                        row = (half * 2 + part) * 8
                        probe_out[0, part, first : first + 8, lanes] = pieces[
                            xlo, core, place, row : row + 8
                        ]


def own_kernel(place, whole, own, left, sems):
    rows = pl.ds(pl.multiple_of(place[0] * SLAB, SLAB), BAND)
    first = pltpu.make_async_copy(whole.at[:, rows, :], own, sems.at[0])
    second = pltpu.make_async_copy(whole.at[:, rows, pl.ds(0, SIDE)], left, sems.at[1])
    first.start()
    second.start()
    first.wait()
    second.wait()


def take_own(mode, object_tiles, after):
    vmem = pl.BlockSpec(memory_space=pltpu.VMEM)
    anywhere = pl.BlockSpec(memory_space=pl.ANY)

    def body(place, whole, _, own, left, sems):
        own_kernel(place, whole, own, left, sems)

    return pl.pallas_call(
        body,
        out_shape=[
            jax.ShapeDtypeStruct((2, BAND, WIDTH), F32),
            jax.ShapeDtypeStruct((2, BAND, SIDE), F32),
        ],
        in_specs=[pl.BlockSpec(memory_space=pltpu.SMEM), anywhere, anywhere],
        out_specs=[vmem, vmem],
        scratch_shapes=[pltpu.SemaphoreType.DMA((2,))],
        compiler_params=pltpu.CompilerParams(vmem_limit_bytes=VMEM_LIMIT),
        name="own_kernel",
    )(mode.astype(jnp.int32).reshape(1), object_tiles, after)


def call(kernel, outs, *args, scalars=True, after=()):
    vmem = pl.BlockSpec(memory_space=pltpu.VMEM)
    in_specs = [vmem] * len(args) + [pl.BlockSpec(memory_space=pl.ANY)] * len(after)

    def body(*refs):
        taken = list(refs[: len(args)])
        if scalars:
            taken[0] = [taken[0][0, index] for index in range(BAND_ID + 1)]
        kernel(*taken, *refs[len(args) + len(after) :])

    return pl.pallas_call(
        body,
        out_shape=[jax.ShapeDtypeStruct(shape, F32) for shape in outs],
        in_specs=in_specs,
        out_specs=[vmem] * len(outs),
        compiler_params=pltpu.CompilerParams(vmem_limit_bytes=VMEM_LIMIT),
        name=kernel.__name__,
    )(*args, *after)


def shift(value, axes, count, steps):
    first, last = max(0, -steps), min(count, count - steps)
    return lax.ppermute(value, axes, [(i, i + steps) for i in range(first, last)])


def other(value, axis):
    return lax.ppermute(value, axis, [(0, 1), (1, 0)])


def beside_slab(value, steps):
    first, last = max(0, -steps), min(MODES, MODES - steps)
    pairs = [(slab_of(i), slab_of(i + steps)) for i in range(first, last)]
    return lax.ppermute(value, MODE_AXES, pairs)


def exchange_rings(value):
    groups = [[(ring + RINGS // 2) % RINGS for ring in range(RINGS)]]
    value = value.reshape(RINGS, 1, MESSAGE * LANES)
    value = lax.all_to_all(value, "z", 0, 0, tiled=True, axis_index_groups=groups)
    return value.reshape(RINGS * MESSAGE, LANES)


def exchange(value, axes):
    return lax.all_to_all(value, axes, 0, 0, tiled=True)


def gather_pieces(piece):
    gathered = lax.all_gather(piece, ("xlo", "core"))
    return gathered.reshape((2, 2) + piece.shape)


def per_device(
    object_tiles, probe_modes, measured, row_offset, col_offset, live_counts, visit_order
):
    tables = jnp.asarray(fourier_tables())
    slots = visit_order[0]
    tile = lax.axis_index(TILE_AXES)
    mode = lax.axis_index(MODE_AXES)
    slab = jnp.where(mode < MODES // 2, mode, 11 - mode)
    (pieces,) = call(split_kernel, [(MODES, 2, SLAB, SIDE)], probe_modes, scalars=False)
    probe = exchange(pieces, MODE_AXES)
    own, left = take_own(slab, object_tiles, pieces)
    beside = shift(left, TILE_AXES, TILES, -1)
    places = [
        mode,
        lax.axis_index("core"),
        lax.axis_index("xlo"),
        lax.axis_index("z"),
        (tile < TILES - 1).astype(jnp.int32),
        slab,
    ]
    chosen = slots[:, None] == jnp.arange(STEPS, dtype=jnp.int32)[None, :]
    per_step = [
        jnp.sum(jnp.where(chosen, row_offset, 0), axis=1),
        jnp.sum(jnp.where(chosen, col_offset, 0), axis=1),
        slots,
        (slots < live_counts[0]).astype(jnp.int32),
    ]
    scalars = jnp.stack(
        per_step + [jnp.broadcast_to(place, (STEPS,)) for place in places], axis=1
    )
    slabs = (MODES, 2, SLAB, SIDE)
    slab_pair = (2, SLAB, SIDE)
    band_shape = (2, BAND, WIDE)
    edge = (2, BAND, SIDE)
    counts_shapes = [(SIDE, LANES), (3, 8, SIDE)]
    counts, flags = call(counts_kernel, counts_shapes, scalars[:1], measured)
    for step in range(STEPS):
        scal = scalars[step : step + 1]
        final = step == STEPS - 1
        if step == 0:
            band, view, shard, spectra = call(
                first_kernel,
                [band_shape, slab_pair, (2 * MODES, LANES), slabs],
                scal,
                own,
                beside,
                probe,
                tables,
                after=(counts,),
            )
        else:
            probe, spectra = call(
                next_kernel,
                [slabs, slabs],
                view,
                pieces,
                tables,
                scalars=False,
                after=(counts,),
            )
        spectra = exchange(spectra, MODE_AXES)
        (spectra,) = call(
            ratio_kernel, [slabs], spectra, counts, flags, tables, scalars=False
        )
        spectra = exchange(spectra, MODE_AXES)
        chi, keep, send = call(
            backward_kernel,
            [slabs] + [(2 * MODES + 1, 16, SIDE)] * 2,
            spectra,
            view,
            flags,
            tables,
            scalars=False,
        )
        received = other(send, "core")
        keep, send = call(
            halve_kernel, [(2 * MODES + 1, 8, SIDE)] * 2, keep, received, flags, scalars=False
        )
        received = other(send, "xlo")
        (object_step,) = call(
            step_kernel, [slab_pair], chi, probe, scalars=False, after=(keep,)
        )
        above = beside_slab(object_step, 1)
        below = beside_slab(object_step, -1)
        if not final:
            next_scal = scalars[step + 1 : step + 2]
            counts, flags = call(
                counts_kernel, counts_shapes, next_scal, measured, after=(keep,)
            )
        (packed,) = call(
            pack_kernel,
            [(RINGS * MESSAGE, LANES)],
            keep,
            received,
            scalars=False,
            after=(object_step,) if final else (object_step, counts),
        )
        sums = exchange_rings(packed)
        shard, shards = call(
            probe_kernel,
            [(2 * MODES, LANES), (RINGS, 2 * MODES, LANES)],
            sums,
            shard,
            scalars=False,
            after=(below,) if final else (above, below),
        )
        piece = exchange(shards, "z")
        part_band, to_right, *to_left = call(
            place_kernel,
            [band_shape, edge] if final else [band_shape, edge, edge],
            scal,
            above,
            object_step,
            below,
            band,
            after=(shards,),
        )
        from_left = shift(to_right, TILE_AXES, TILES, 1)
        if final:
            (rows_out,) = call(
                out_rows_kernel, [(2, OUT_ROWS, WIDTH)], scal, part_band, from_left
            )
            piece, rows_out = lax.optimization_barrier((piece, rows_out))
        else:
            from_right = shift(to_left[0], TILE_AXES, TILES, -1)
            band, view = call(
                view_kernel,
                [band_shape, slab_pair],
                next_scal,
                part_band,
                from_left,
                from_right,
            )
            piece, view = lax.optimization_barrier((piece, view))
            pieces = gather_pieces(piece.reshape(2 * MODES * RINGS, LANES))
    tail_rows = 32 + 8 * OUT_ROWS
    (tail,) = call(
        tail_kernel,
        [(MODES, tail_rows, LANES)],
        piece.reshape(2 * MODES * RINGS, LANES),
        rows_out,
        scalars=False,
    )
    tail = exchange(tail, MODE_AXES)
    pieces = gather_pieces(tail[:, :32])
    return call(
        last_kernel,
        [(2, HEIGHT, WIDTH), (1, 2, SIDE, SIDE)],
        tail,
        pieces,
        scalars=False,
    )


def solution(mesh):
    grid = Mesh(mesh.devices.reshape(2, 16, 2, 2, 4), TILE_AXES + MODE_AXES)
    return jax.shard_map(
        per_device,
        mesh=grid,
        in_specs=(
            P(None, None, TILE_AXES),
            P(MODE_AXES, None, None, None),
            P(TILE_AXES, None, None, None),
            P(TILE_AXES, None),
            P(TILE_AXES, None),
            P(TILE_AXES),
            P(TILE_AXES, None),
        ),
        out_specs=(P(None, None, TILE_AXES), P(MODE_AXES, None, None, None)),
        check_vma=False,
    )
```

```python
import math

import jax
import jax.numpy as jnp
import numpy as np
from jax import lax
from jax.experimental import pallas as pl
from jax.experimental.pallas import tpu as pltpu
from jax.sharding import Mesh
from jax.sharding import PartitionSpec as P

SOFT_FLOOR = 0.5
OBJECT_RATE = 1.0
OBJECT_DAMP = 0.5
PROBE_RATE = 1.0
PROBE_DAMP = 1.0

SIDE = 256
HEIGHT = 288
WIDTH = 512
WIDE = WIDTH + SIDE
MODES = 8
SLAB = SIDE // MODES
BAND = 2 * SLAB
STEPS = 3
TILES = 64
RINGS = 16
LANES = 128
COL_SPAN = SIDE + LANES
OUT_ROWS = HEIGHT // MODES
MESSAGE = 2 * MODES + 1
VMEM_LIMIT = 16 * 1024 * 1024

TILE_AXES = ("xlo", "z", "core")
MODE_AXES = ("xhi", "y")

ROW, COL, SLOT, LIVE, MODE, CORE, XLO, RING, HAS_NEXT, BAND_ID = range(10)

F32 = jnp.float32
BF16 = jnp.bfloat16


def slab_of(place):
    return place if place < MODES // 2 else 11 - place


def fourier_tables():
    index = np.arange(SIDE)
    angles = (index[:, None] * index[None, :] % SIDE) * (2.0 * math.pi / SIDE)
    cosine, sine = np.cos(angles) / math.sqrt(SIDE), np.sin(angles) / math.sqrt(SIDE)
    exact = np.stack([cosine, cosine + sine, cosine - sine])
    high = exact.astype(jnp.bfloat16)
    low = (exact - high.astype(np.float64)).astype(jnp.bfloat16)
    return np.stack([high, low], axis=1)


def halves(value):
    high = value.astype(BF16)
    return high, (value - high.astype(F32)).astype(BF16)


def dot(left, right):
    return jnp.dot(left, right, preferred_element_type=F32)


def transform(real, imag, by, direction):
    turned = direction * imag
    shared = by(0, real + turned)
    return shared - by(2, turned), direction * (shared - by(1, real))


def rows_transform(real, imag, tables, direction):
    def by(which, value):
        high, low = halves(value)
        return (
            dot(high, tables[which, 0]) + dot(low, tables[which, 0]) + dot(high, tables[which, 1])
        )

    return transform(real, imag, by, direction)


def columns_transform(real, imag, tables, direction):
    def by(which, value):
        high, low = halves(value)
        return (
            dot(tables[which, 0], high) + dot(tables[which, 0], low) + dot(tables[which, 1], high)
        )

    return transform(real, imag, by, direction)


def swap_blocks(parts):
    lanes = lax.broadcasted_iota(jnp.int32, (parts[0].shape[0], LANES), 1)
    grid = [[part[:, :LANES], part[:, LANES:]] for part in parts]
    grid = [[grid[(m & 3) | (h << 2)][m >> 2] for h in range(2)] for m in range(MODES)]
    for bit in (2, 1):
        shift = bit * SLAB
        low = (lanes & shift) == 0
        new = [None] * MODES
        for m in range(MODES):
            if m & bit:
                continue
            a, b = grid[m], grid[m | bit]
            new[m] = [jnp.where(low, a[h], pltpu.roll(b[h], shift, 1)) for h in range(2)]
            new[m | bit] = [
                jnp.where(low, pltpu.roll(a[h], LANES - shift, 1), b[h]) for h in range(2)
            ]
        grid = new
    return [jnp.concatenate(pair, axis=1) for pair in grid]


def stacked(pieces):
    return jnp.concatenate(list(pieces), axis=0)


def column_window(scal):
    col = scal[COL]
    block = jnp.minimum(col // LANES, WIDTH // LANES - 1)
    return pl.ds(pl.multiple_of(block * LANES, LANES), COL_SPAN), col - block * LANES


def take_patch(scal, band, view):
    cols, rest = column_window(scal)
    for part in range(2):
        block = band[part, :, cols]
        block = pltpu.roll(block, lax.rem(COL_SPAN - rest, COL_SPAN), 1)[:, :SIDE]
        view[part] = pltpu.roll(block, lax.rem(BAND - scal[ROW], BAND), 0)[:SLAB]


def forward(view, probe, tables, spectra):
    view_real = stacked([view[0]] * MODES)
    view_imag = stacked([view[1]] * MODES)
    probe_real = stacked(probe[mode, 0] for mode in range(MODES))
    probe_imag = stacked(probe[mode, 1] for mode in range(MODES))
    both = rows_transform(
        probe_real * view_real - probe_imag * view_imag,
        probe_real * view_imag + probe_imag * view_real,
        tables,
        1.0,
    )
    for part in range(2):
        blocks = [both[part][mode * SLAB : (mode + 1) * SLAB] for mode in range(MODES)]
        for place, block in enumerate(swap_blocks(blocks)):
            spectra[place, part] = block


def split_kernel(probe_in, pieces):
    for place in range(MODES):
        row = slab_of(place) * SLAB
        pieces[place] = probe_in[0, :, row : row + SLAB, :]


def first_kernel(scal, own, beside, probe, tables, band, view, shard, spectra):
    band[:, :, :WIDTH] = own[...]
    band[:, :, WIDTH:] = beside[...]
    take_patch(scal, band, view)
    rows = pl.ds(pl.multiple_of(scal[CORE] * 16 + scal[XLO] * 8, 8), 8)
    wanted = lax.broadcasted_iota(jnp.int32, (8, LANES), 0) == scal[RING] // 2
    second = lax.rem(scal[RING], 2) == 1
    for mode in range(MODES):
        for part in range(2):
            block = jnp.where(second, probe[mode, part, rows, LANES:], probe[mode, part, rows, :LANES])
            index = 2 * mode + part
            shard[index : index + 1] = jnp.sum(
                jnp.where(wanted, block, 0.0), axis=0, keepdims=True
            )
    forward(view, probe, tables, spectra)


def next_kernel(view, pieces, tables, probe, spectra):
    for xlo in range(2):
        for core in range(2):
            row = core * 16 + xlo * 8
            for index in range(2 * MODES):
                for half in range(2):
                    lanes = slice(half * LANES, (half + 1) * LANES)
                    piece = pieces[xlo, core, pl.ds(RINGS * half + index, 8, stride=2 * RINGS), :]
                    probe[index // 2, index % 2, row : row + 8, lanes] = piece
    forward(view, probe, tables, spectra)


def counts_kernel(scal, measured, counts, flags):
    for place, which in enumerate((LIVE, CORE, XLO)):
        flags[place] = jnp.full((8, SIDE), scal[which].astype(F32))
    block = measured[0, scal[SLOT]].astype(F32)
    block = pltpu.roll(block, lax.rem(SIDE - scal[MODE] * SLAB, SIDE), 1)[:, :LANES]
    lanes = lax.broadcasted_iota(jnp.int32, block.shape, 1)
    block = jnp.where(lanes < SLAB, block, 0.0)
    block = block + pltpu.roll(block, SLAB, 1)
    counts[...] = block + pltpu.roll(block, 2 * SLAB, 1)


def ratio_kernel(spectra, counts, flags, tables, out):
    real = stacked(spectra[slab_of(index), 0] for index in range(MODES))
    imag = stacked(spectra[slab_of(index), 1] for index in range(MODES))
    far_real, far_imag = columns_transform(real, imag, tables, 1.0)
    power = far_real * far_real + far_imag * far_imag
    total = power[:, :LANES] + power[:, LANES:]
    total = total + pltpu.roll(total, 2 * SLAB, 1)
    total = total + pltpu.roll(total, SLAB, 1)
    ratio = jnp.sqrt((counts[...] + SOFT_FLOOR) / (total + SOFT_FLOOR)) - 1.0
    ratio = ratio * flags[0, 0:1, :LANES]
    ratio = jnp.concatenate([ratio, ratio], axis=1)
    both = columns_transform(far_real * ratio, far_imag * ratio, tables, -1.0)
    for part in range(2):
        for place in range(MODES):
            row = slab_of(place) * SLAB
            out[place, part] = both[part][row : row + SLAB]


def backward_kernel(spectra, view, flags, tables, chi, keep, send):
    real = stacked(swap_blocks([spectra[place, 0] for place in range(MODES)]))
    imag = stacked(swap_blocks([spectra[place, 1] for place in range(MODES)]))
    chi_real, chi_imag = rows_transform(real, imag, tables, -1.0)
    view_real, view_imag = view[0], view[1]
    sums = []
    for mode in range(MODES):
        real = chi_real[mode * SLAB : (mode + 1) * SLAB]
        imag = chi_imag[mode * SLAB : (mode + 1) * SLAB]
        chi[mode, 0] = real
        chi[mode, 1] = imag
        sums.append(view_real * real + view_imag * imag)
        sums.append(view_real * imag - view_imag * real)
    sums.append((view_real * view_real + view_imag * view_imag) * flags[0, 0:1, :])
    second = jnp.broadcast_to(flags[1, 0:1, :], (16, SIDE)) > 0.5
    for index, value in enumerate(sums):
        keep[index] = jnp.where(second, value[16:], value[:16])
        send[index] = jnp.where(second, value[:16], value[16:])


def halve_kernel(mine, theirs, flags, keep, send):
    second = jnp.broadcast_to(flags[2, 0:1, :], (8, SIDE)) > 0.5
    for index in range(2 * MODES + 1):
        value = mine[index] + theirs[index]
        keep[index] = jnp.where(second, value[8:], value[:8])
        send[index] = jnp.where(second, value[:8], value[8:])


def pack_kernel(mine, theirs, packed):
    for index in range(MESSAGE):
        total = pltpu.roll(mine[index] + theirs[index], RINGS // 4, 0)
        for half in range(2):
            rows = pl.ds(MESSAGE * half + index, 8, stride=2 * MESSAGE)
            packed[rows, :] = total[:, half * LANES : (half + 1) * LANES]


def step_kernel(chi, probe, step):
    real = imag = light = 0.0
    for mode in range(MODES):
        probe_real, probe_imag = probe[mode, 0], probe[mode, 1]
        real = real + (probe_real * chi[mode, 0] + probe_imag * chi[mode, 1])
        imag = imag + (probe_real * chi[mode, 1] - probe_imag * chi[mode, 0])
        light = light + (probe_real * probe_real + probe_imag * probe_imag)
    step[0] = OBJECT_RATE * real / (light + OBJECT_DAMP)
    step[1] = OBJECT_RATE * imag / (light + OBJECT_DAMP)


def place_kernel(scal, above, step, below, band, part_band, to_right, to_left=None):
    cols, rest = column_window(scal)
    height = 3 * SLAB
    part_band[...] = jnp.zeros_like(part_band)
    for part in range(2):
        block = stacked([above[part], step[part], below[part]])
        block = pltpu.roll(block, lax.rem(2 * SLAB + scal[ROW], height), 0)[:BAND]
        block = jnp.concatenate([block, jnp.zeros((BAND, LANES), F32)], axis=1)
        part_band[part, :, cols] = pltpu.roll(block, rest, 1)
    if to_left is not None:
        to_left[...] = part_band[:, :, :SIDE]
    to_right[...] = part_band[:, :, WIDTH:]
    part_band[:, :, :WIDTH] = part_band[:, :, :WIDTH] + band[:, :, :WIDTH]
    part_band[:, :, WIDTH:] = (
        part_band[:, :, WIDTH:] * scal[HAS_NEXT].astype(F32) + band[:, :, WIDTH:]
    )


def view_kernel(scal, part_band, from_left, from_right, band, view):
    band[:, :, :SIDE] = part_band[:, :, :SIDE] + from_left[...]
    band[:, :, SIDE:WIDTH] = part_band[:, :, SIDE:WIDTH]
    band[:, :, WIDTH:] = part_band[:, :, WIDTH:] + from_right[...]
    take_patch(scal, band, view)


def probe_kernel(sums, shard_in, shard, copies):
    total = sums[:MESSAGE]
    for ring in range(1, RINGS):
        total = total + sums[ring * MESSAGE : (ring + 1) * MESSAGE]
    rows = 2 * MODES
    new = shard_in[...] + PROBE_RATE * total[:rows] / (total[rows:] + PROBE_DAMP)
    shard[...] = new
    for ring in range(RINGS):
        copies[ring] = new


def out_rows_kernel(scal, part_band, from_left, rows_out):
    slab = scal[BAND_ID]
    odd = lax.rem(slab, 2) == 1
    rows = pl.ds(pl.multiple_of(slab // 2 * 8, 8), OUT_ROWS + 4)
    for part in range(2):
        edge = part_band[part, rows, :SIDE] + from_left[part, rows, :]
        block = jnp.concatenate([edge, part_band[part, rows, SIDE:WIDTH]], axis=1)
        block = jnp.where(odd, pltpu.roll(block, OUT_ROWS, 0), block)
        rows_out[part] = block[:OUT_ROWS]


def tail_kernel(piece, rows_out, tail):
    for place in range(MODES):
        for half in range(2):
            for part in range(2):
                row = (half * 2 + part) * 8
                rows = pl.ds(RINGS * half + 2 * place + part, 8, stride=2 * RINGS)
                tail[place, row : row + 8] = pltpu.roll(piece[rows, :], RINGS // 4, 0)
        for part in range(2):
            for block in range(WIDTH // LANES):
                row = 32 + (part * 4 + block) * OUT_ROWS
                lanes = slice(block * LANES, (block + 1) * LANES)
                tail[place, row : row + OUT_ROWS] = rows_out[part, :, lanes]


def last_kernel(tail, pieces, object_out, probe_out):
    for place in range(MODES):
        first = slab_of(place) * OUT_ROWS
        for part in range(2):
            for block in range(WIDTH // LANES):
                row = 32 + (part * 4 + block) * OUT_ROWS
                lanes = slice(block * LANES, (block + 1) * LANES)
                object_out[part, first : first + OUT_ROWS, lanes] = tail[
                    place, row : row + OUT_ROWS
                ]
    for xlo in range(2):
        for core in range(2):
            for place in range(MODES):
                first = slab_of(place) * SLAB + core * 16 + xlo * 8
                for half in range(2):
                    lanes = slice(half * LANES, (half + 1) * LANES)
                    for part in range(2):
                        row = (half * 2 + part) * 8
                        probe_out[0, part, first : first + 8, lanes] = pieces[
                            xlo, core, place, row : row + 8
                        ]


def own_kernel(place, whole, own, left, sems):
    rows = pl.ds(pl.multiple_of(place[0] * SLAB, SLAB), BAND)
    first = pltpu.make_async_copy(whole.at[:, rows, :], own, sems.at[0])
    second = pltpu.make_async_copy(whole.at[:, rows, pl.ds(0, SIDE)], left, sems.at[1])
    first.start()
    second.start()
    first.wait()
    second.wait()


def take_own(mode, object_tiles, after):
    vmem = pl.BlockSpec(memory_space=pltpu.VMEM)
    anywhere = pl.BlockSpec(memory_space=pl.ANY)

    def body(place, whole, _, own, left, sems):
        own_kernel(place, whole, own, left, sems)

    return pl.pallas_call(
        body,
        out_shape=[
            jax.ShapeDtypeStruct((2, BAND, WIDTH), F32),
            jax.ShapeDtypeStruct((2, BAND, SIDE), F32),
        ],
        in_specs=[pl.BlockSpec(memory_space=pltpu.SMEM), anywhere, anywhere],
        out_specs=[vmem, vmem],
        scratch_shapes=[pltpu.SemaphoreType.DMA((2,))],
        compiler_params=pltpu.CompilerParams(vmem_limit_bytes=VMEM_LIMIT),
        name="own_kernel",
    )(mode.astype(jnp.int32).reshape(1), object_tiles, after)


def call(kernel, outs, *args, scalars=True, after=()):
    vmem = pl.BlockSpec(memory_space=pltpu.VMEM)
    in_specs = [vmem] * len(args) + [pl.BlockSpec(memory_space=pl.ANY)] * len(after)

    def body(*refs):
        taken = list(refs[: len(args)])
        if scalars:
            taken[0] = [taken[0][0, index] for index in range(BAND_ID + 1)]
        kernel(*taken, *refs[len(args) + len(after) :])

    return pl.pallas_call(
        body,
        out_shape=[jax.ShapeDtypeStruct(shape, F32) for shape in outs],
        in_specs=in_specs,
        out_specs=[vmem] * len(outs),
        compiler_params=pltpu.CompilerParams(vmem_limit_bytes=VMEM_LIMIT),
        name=kernel.__name__,
    )(*args, *after)


def shift(value, axes, count, steps):
    first, last = max(0, -steps), min(count, count - steps)
    return lax.ppermute(value, axes, [(i, i + steps) for i in range(first, last)])


def other(value, axis):
    return lax.ppermute(value, axis, [(0, 1), (1, 0)])


def beside_slab(value, steps):
    first, last = max(0, -steps), min(MODES, MODES - steps)
    pairs = [(slab_of(i), slab_of(i + steps)) for i in range(first, last)]
    return lax.ppermute(value, MODE_AXES, pairs)


def exchange_far_first(value):
    groups = [[(ring + RINGS // 2) % RINGS for ring in range(RINGS)]]
    return lax.all_to_all(value, "z", 0, 0, tiled=True, axis_index_groups=groups)


def exchange_rings(value):
    value = exchange_far_first(value.reshape(RINGS, 1, MESSAGE * LANES))
    return value.reshape(RINGS * MESSAGE, LANES)


def exchange(value, axes):
    return lax.all_to_all(value, axes, 0, 0, tiled=True)


def gather_pieces(piece):
    gathered = lax.all_gather(piece, ("xlo", "core"))
    return gathered.reshape((2, 2) + piece.shape)


def per_device(
    object_tiles, probe_modes, measured, row_offset, col_offset, live_counts, visit_order
):
    tables = jnp.asarray(fourier_tables())
    slots = visit_order[0]
    tile = lax.axis_index(TILE_AXES)
    mode = lax.axis_index(MODE_AXES)
    slab = jnp.where(mode < MODES // 2, mode, 11 - mode)
    (pieces,) = call(split_kernel, [(MODES, 2, SLAB, SIDE)], probe_modes, scalars=False)
    probe = exchange(pieces, MODE_AXES)
    own, left = take_own(slab, object_tiles, pieces)
    beside = shift(left, TILE_AXES, TILES, -1)
    places = [
        mode,
        lax.axis_index("core"),
        lax.axis_index("xlo"),
        lax.axis_index("z"),
        (tile < TILES - 1).astype(jnp.int32),
        slab,
    ]
    chosen = slots[:, None] == jnp.arange(STEPS, dtype=jnp.int32)[None, :]
    per_step = [
        jnp.sum(jnp.where(chosen, row_offset, 0), axis=1),
        jnp.sum(jnp.where(chosen, col_offset, 0), axis=1),
        slots,
        (slots < live_counts[0]).astype(jnp.int32),
    ]
    scalars = jnp.stack(
        per_step + [jnp.broadcast_to(place, (STEPS,)) for place in places], axis=1
    )
    slabs = (MODES, 2, SLAB, SIDE)
    slab_pair = (2, SLAB, SIDE)
    band_shape = (2, BAND, WIDE)
    edge = (2, BAND, SIDE)
    counts_shapes = [(SIDE, LANES), (3, 8, SIDE)]
    counts, flags = call(counts_kernel, counts_shapes, scalars[:1], measured)
    for step in range(STEPS):
        scal = scalars[step : step + 1]
        final = step == STEPS - 1
        if step == 0:
            band, view, shard, spectra = call(
                first_kernel,
                [band_shape, slab_pair, (2 * MODES, LANES), slabs],
                scal,
                own,
                beside,
                probe,
                tables,
                after=(counts,),
            )
        else:
            probe, spectra = call(
                next_kernel,
                [slabs, slabs],
                view,
                pieces,
                tables,
                scalars=False,
                after=(counts,),
            )
        spectra = exchange(spectra, MODE_AXES)
        (spectra,) = call(
            ratio_kernel, [slabs], spectra, counts, flags, tables, scalars=False
        )
        spectra = exchange(spectra, MODE_AXES)
        chi, keep, send = call(
            backward_kernel,
            [slabs] + [(2 * MODES + 1, 16, SIDE)] * 2,
            spectra,
            view,
            flags,
            tables,
            scalars=False,
        )
        received = other(send, "core")
        keep, send = call(
            halve_kernel, [(2 * MODES + 1, 8, SIDE)] * 2, keep, received, flags, scalars=False
        )
        received = other(send, "xlo")
        (object_step,) = call(
            step_kernel, [slab_pair], chi, probe, scalars=False, after=(keep,)
        )
        above = beside_slab(object_step, 1)
        below = beside_slab(object_step, -1)
        if not final:
            next_scal = scalars[step + 1 : step + 2]
            counts, flags = call(
                counts_kernel, counts_shapes, next_scal, measured, after=(keep,)
            )
        (packed,) = call(
            pack_kernel,
            [(RINGS * MESSAGE, LANES)],
            keep,
            received,
            scalars=False,
            after=(object_step,) if final else (object_step, counts),
        )
        sums = exchange_rings(packed)
        shard, shards = call(
            probe_kernel,
            [(2 * MODES, LANES), (RINGS, 2 * MODES, LANES)],
            sums,
            shard,
            scalars=False,
            after=(above, below),
        )
        piece = exchange_far_first(shards) if final else exchange(shards, "z")
        part_band, to_right, *to_left = call(
            place_kernel,
            [band_shape, edge] if final else [band_shape, edge, edge],
            scal,
            above,
            object_step,
            below,
            band,
            after=(shards,),
        )
        from_left = shift(to_right, TILE_AXES, TILES, 1)
        if final:
            (rows_out,) = call(
                out_rows_kernel, [(2, OUT_ROWS, WIDTH)], scal, part_band, from_left
            )
            piece, rows_out = lax.optimization_barrier((piece, rows_out))
        else:
            from_right = shift(to_left[0], TILE_AXES, TILES, -1)
            band, view = call(
                view_kernel,
                [band_shape, slab_pair],
                next_scal,
                part_band,
                from_left,
                from_right,
            )
            piece, view = lax.optimization_barrier((piece, view))
            pieces = gather_pieces(piece.reshape(2 * MODES * RINGS, LANES))
    tail_rows = 32 + 8 * OUT_ROWS
    (tail,) = call(
        tail_kernel,
        [(MODES, tail_rows, LANES)],
        piece.reshape(2 * MODES * RINGS, LANES),
        rows_out,
        scalars=False,
    )
    tail = exchange(tail, MODE_AXES)
    pieces = gather_pieces(tail[:, :32])
    return call(
        last_kernel,
        [(2, HEIGHT, WIDTH), (1, 2, SIDE, SIDE)],
        tail,
        pieces,
        scalars=False,
    )


def solution(mesh):
    grid = Mesh(mesh.devices.reshape(2, 16, 2, 2, 4), TILE_AXES + MODE_AXES)
    return jax.shard_map(
        per_device,
        mesh=grid,
        in_specs=(
            P(None, None, TILE_AXES),
            P(MODE_AXES, None, None, None),
            P(TILE_AXES, None, None, None),
            P(TILE_AXES, None),
            P(TILE_AXES, None),
            P(TILE_AXES),
            P(TILE_AXES, None),
        ),
        out_specs=(P(None, None, TILE_AXES), P(MODE_AXES, None, None, None)),
        check_vma=False,
    )
```
